32 devices in a mesh: fsdp: 4 (over z), win: 8 (over y, x, core).
Axes of the slice: x: 2, y: 2, z: 4, core: 2. Of those that a mesh axis runs over, the one named last changes fastest.
Arguments:
- tokens: bfloat16 [512, 100, 512], P(('fsdp', 'win')), may hold values from -6 to 6
- live: int32 [32], P(('fsdp', 'win')), may hold values from 8 to 16, as said below
- vectors: float32 [8, 512], P(None, ('fsdp', 'win'))
- fc1_bias: float32 [2048], P(('fsdp', 'win')), may hold values from -1.8 to 1.8
- w_qkv: bfloat16 [512, 1536], P('win', 'fsdp'), may hold values from -0.25 to 0.25
- w_proj: bfloat16 [512, 512], P('win', 'fsdp'), may hold values from -0.5 to 0.5
- w_fc1: bfloat16 [512, 2048], P('win', 'fsdp'), may hold values from -0.25 to 0.25
- w_fc2: bfloat16 [2048, 512], P('win', 'fsdp'), may hold values from -0.125 to 0.125
- rel_table: float32 [361, 16], replicated, may hold values from -5 to 5
- cotangent: bfloat16 [512, 100, 512], P(('fsdp', 'win')), may hold values from -6 to 6
Outputs:
- block_out: bfloat16 [512, 100, 512], P(('fsdp', 'win'))
- grad_tokens: bfloat16 [512, 100, 512], P(('fsdp', 'win'))
- grad_vectors: float32 [8, 512], P(None, ('fsdp', 'win'))
- grad_fc1_bias: float32 [2048], P(('fsdp', 'win'))
- grad_qkv: float32 [512, 1536], P('win', 'fsdp')
- grad_proj: float32 [512, 512], P('win', 'fsdp')
- grad_fc1: float32 [512, 2048], P('win', 'fsdp')
- grad_fc2: float32 [2048, 512], P('win', 'fsdp')
- grad_table: float32 [361, 16], replicated
The draws below stay inside these ranges and needn't reach their ends.
Inputs may be any that keep to these rules, and one draw needn't show every extreme that they name: Every device has at least half of its 16 slots live, and some device has all of them live.
All inputs are finite; a program needn't handle non-finite values.
Results may differ from the reference program's by a relative error of at most 0.017.
Values may be sent and summed in bfloat16 or wider, within the bound.
No kernel may reach another device: no remote copies, remote signals or barrier semaphores. Data moves between devices by JAX's collectives and lax.ppermute only.
A program may use at most 192 MiB of HBM per device.

```python
import jax
import jax.numpy as jnp
from jax import lax

D = 512
HEADS = 16
HD = 32
FF = 2048
WS = 10
CAP = 16
WT = 100
TABLE = 361
SLOTS_ALL = 32
WINDOWS = 512


def draw_live(key, part):
    key = jax.random.fold_in(key, 7)
    first_key, second_key = jax.random.split(key)
    counts = jax.random.randint(first_key, (SLOTS_ALL,), max(1, CAP // 2), CAP + 1)
    spot = jax.random.randint(second_key, (), 0, SLOTS_ALL)
    return counts.at[spot].set(CAP).astype(jnp.int32)


def draw_vectors(key, part):
    key = jax.random.fold_in(key, 11)
    first_key, second_key = jax.random.split(key)
    biases = jax.random.normal(first_key, (8, D), jnp.float32) * 0.3
    gains = jax.random.uniform(second_key, (8, D), jnp.float32, 0.5, 1.5)
    which = jnp.arange(8)[:, None]
    gain_rows = (which == 0) | (which == 5)
    return jnp.where(gain_rows, gains, biases).astype(jnp.float32)


def block_levels(key, dims, cuts, smallest, largest):
    loudness, own = 1.0, jax.random.fold_in(key, 6)
    for position, parts in cuts:
        steps = jnp.exp(jax.random.uniform(jax.random.fold_in(own, position), (parts,), jnp.float32, smallest / len(cuts), largest / len(cuts)))
        loudness = loudness * jnp.repeat(steps, dims[position] // parts).reshape([-1 if axis == position else 1 for axis in range(len(dims))])
    return loudness


def bell_draw(rng, shape, width, limit, shards=(), held_as=jnp.bfloat16):
    entries = jax.random.normal(rng, shape, jnp.float32) * width
    if len(shards) > 0:
        entries = block_levels(rng, shape, shards, -0.22, 0.18) * entries
    return jnp.clip(entries, min=-limit, max=limit).astype(held_as)


def setup_inputs(seed: int = 0) -> dict:
    arg_keys = jax.random.split(jax.random.key(seed), 11)
    return {
        "tokens": bell_draw(arg_keys[0], (WINDOWS, WT, D), 1.0, 6.0, ((0, 32),)),
        "live": draw_live(jax.random.fold_in(arg_keys[10], 71), 0),
        "vectors": draw_vectors(jax.random.fold_in(arg_keys[10], 71), 0),
        "fc1_bias": bell_draw(arg_keys[3], (FF,), 0.3, 1.8, ((0, 32),), jnp.float32),
        "w_qkv": bell_draw(arg_keys[4], (D, 3 * D), D ** -0.5, 0.25, ((0, 8), (1, 4))),
        "w_proj": bell_draw(arg_keys[5], (D, D), (D // 4) ** -0.5, 0.5, ((0, 8), (1, 4))),
        "w_fc1": bell_draw(arg_keys[6], (D, FF), D ** -0.5, 0.25, ((0, 8), (1, 4))),
        "w_fc2": bell_draw(arg_keys[7], (FF, D), FF ** -0.5, 0.125, ((0, 8), (1, 4))),
        "rel_table": bell_draw(arg_keys[8], (TABLE, HEADS), 1.0, 5.0, (), jnp.float32),
        "cotangent": bell_draw(arg_keys[9], (WINDOWS, WT, D), 1.0, 6.0, ((0, 32),)),
    }


@jax.custom_vjp
def low(v):
    return lax.optimization_barrier(v.astype(jnp.bfloat16)).astype(jnp.float32)

@jax.custom_vjp
def low_back(v):
    return v

def low_keep(v):
    return (low(v), None)

def low_pass(kept, grad):
    return (grad,)

def back_keep(v):
    return (v, None)

def back_low(kept, grad):
    return (low(grad),)
low.defvjp(low_keep, low_pass)
low_back.defvjp(back_keep, back_low)
NORM_EPS = 1e-05
HIGH = lax.Precision.HIGHEST

def layer_norm(values, gain, shift):
    centre = values - lax.optimization_barrier(jnp.mean(values, -1, keepdims=True))
    spread = lax.optimization_barrier(jnp.mean(centre * centre, -1, keepdims=True))
    return centre * lax.rsqrt(spread + NORM_EPS) * gain + shift

def rel_index():
    patch = jnp.arange(WT, dtype=jnp.int32)
    row_pos = patch // WS
    col_pos = patch % WS
    return ((row_pos[:, None] - row_pos[None, :] + WS - 1) * (2 * WS - 1) + col_pos[:, None] - col_pos[None, :] + WS - 1).astype(jnp.int32)

def group_forward(params, window_group, mask_group):
    w_qkv, w_proj, w_fc1, w_fc2, vectors, fc1_bias, rel_table = params
    flat = window_group.reshape(-1, D)
    norm_one = low(layer_norm(flat, vectors[0], vectors[1]))
    mixed = jnp.dot(norm_one, w_qkv, precision=HIGH)
    query = low(low_back((mixed[:, :D] + vectors[2]) * HD ** (-0.5))).reshape(CAP, WT, HEADS, HD)
    keys = low(low_back(mixed[:, D:2 * D])).reshape(CAP, WT, HEADS, HD)
    values = low(low_back(mixed[:, 2 * D:] + vectors[3])).reshape(CAP, WT, HEADS, HD)
    pos_bias = jnp.transpose(rel_table[rel_index()], (2, 0, 1))
    scores = low_back(jnp.einsum('cqhd,ckhd->chqk', query, keys, precision=HIGH) + pos_bias[None])
    probs = jax.nn.softmax(scores, axis=-1)
    attended = jnp.einsum('chqk,ckhd->cqhd', low(probs), values, precision=HIGH).reshape(-1, D)
    attended = low(low_back(attended))
    branch_att = low_back(jnp.dot(attended, w_proj, precision=HIGH) + vectors[4])
    after_att = flat + branch_att
    norm_two = low(layer_norm(after_att, vectors[5], vectors[6]))
    upper = low_back(jnp.dot(norm_two, w_fc1, precision=HIGH) + fc1_bias)
    activated = low(jax.nn.gelu(upper))
    branch_mlp = low_back(jnp.dot(activated, w_fc2, precision=HIGH) + vectors[7])
    result = (after_att + branch_mlp) * jnp.repeat(mask_group, WT)[:, None]
    return result.reshape(CAP, WT, D)

def reference(tokens, live, vectors, fc1_bias, w_qkv, w_proj, w_fc1, w_fc2, rel_table, cotangent):
    masks = (jnp.arange(CAP, dtype=jnp.int32)[None, :] < live[:, None]).astype(jnp.float32)
    inputs = tokens.astype(jnp.float32).reshape(SLOTS_ALL, CAP, WT, D)

    def whole(inputs, w_qkv, w_proj, w_fc1, w_fc2, vectors, fc1_bias, rel_table):
        params = (w_qkv, w_proj, w_fc1, w_fc2, vectors, fc1_bias, rel_table)
        step_fn = jax.checkpoint(group_forward)
        return lax.map(lambda pair: step_fn(params, pair[0], pair[1]), (inputs, masks))
    outputs, pull = jax.vjp(whole, inputs, w_qkv.astype(jnp.float32), w_proj.astype(jnp.float32), w_fc1.astype(jnp.float32), w_fc2.astype(jnp.float32), vectors.astype(jnp.float32), fc1_bias.astype(jnp.float32), rel_table.astype(jnp.float32))
    grads = pull(cotangent.astype(jnp.float32).reshape(SLOTS_ALL, CAP, WT, D))
    grad_in, grad_qkv, grad_proj, grad_fc1, grad_fc2, grad_vectors, grad_bias, grad_table = grads
    return (outputs.reshape(WINDOWS, WT, D).astype(jnp.bfloat16), grad_in.reshape(WINDOWS, WT, D).astype(jnp.bfloat16), grad_vectors, grad_bias, grad_qkv, grad_proj, grad_fc1, grad_fc2, grad_table)
```

```python
import functools

import jax
import jax.numpy as jnp
import numpy as np
from jax import lax
from jax.experimental import pallas as pl
from jax.experimental.pallas import tpu as pltpu
from jax.sharding import PartitionSpec as P

f32 = jnp.float32
bf16 = jnp.bfloat16
HEADS = 16
HD = 32
WS = 10
WT = WS * WS
D = HEADS * HD
FF = 4 * D
SIDE = 2 * WS - 1
TABLE = SIDE * SIDE
TP = 112
TL = 128
TT = 384
GH = 4
NG = HEADS // GH
EPS = 1e-5
SCALE = HD**-0.5
EXTRA = 32
NN = (((1,), (0,)), ((), ()))
NT = (((1,), (1,)), ((), ()))
TN = (((0,), (0,)), ((), ()))


def dot(a, b, dims=NN):
    return lax.dot_general(a, b, dims, preferred_element_type=f32)


def params(n=1):
    return pltpu.CompilerParams(dimension_semantics=("arbitrary",) * n, vmem_limit_bytes=60 * 2**20)


def cost(us):
    return pl.CostEstimate(flops=int(us * 1.1e9), bytes_accessed=int(us * 1e6), transcendentals=0)


def whole(shape):
    n = len(shape)
    return pl.BlockSpec(shape, lambda *a: (0,) * n, pipeline_mode=pl.Buffered(1))


def smem():
    return pl.BlockSpec(memory_space=pltpu.SMEM)


def anyspace():
    return pl.BlockSpec(memory_space=pl.ANY)


def three(x):
    hi = x.astype(bf16)
    rest = x - hi.astype(f32)
    mid = rest.astype(bf16)
    return hi, mid, (rest - mid.astype(f32)).astype(bf16)


def offset_place():
    cj = np.arange(WS)[:, None, None]
    r = np.arange(TT)[None, :, None]
    l = np.arange(256)[None, None, :]
    hit = (l < SIDE * WS) & (r == (l // WS) * SIDE + (l % WS) - cj + WS - 1)
    return jnp.asarray(hit, bf16)


class Geometry:
    def __init__(self, nw, nz):
        self.nw, self.nz = nw, nz
        self.r = D // nw
        self.cq, self.cp, self.c1 = 3 * D // nz // TL, D // nz // TL, FF // nz // TL
        self.r2 = FF // nw
        self.rows_a = self.cq * self.r
        self.rows_b = self.cp * self.r + self.c1 * self.r + self.cp * self.r2


def slabs(x):
    return jnp.concatenate([x[:, i : i + TL] for i in range(0, x.shape[1], TL)], 0)


def pack_body(wq, wp, w1, w2, vec, b1, a_o, b_o):
    ra = 0
    for i in range(0, wq.shape[1], TL):
        a_o[ra : ra + wq.shape[0], :] = wq[:, i : i + TL]
        ra += wq.shape[0]
    buf = jnp.zeros((EXTRA, TL), f32)
    own = vec.shape[1]
    pieces = [p.astype(f32) for p in three(vec[...])] + [p.astype(f32) for p in three(b1[...])]
    rows = [jnp.concatenate([p, jnp.zeros((8, TL - own), f32)], 1) for p in pieces[:3]]
    tail = [jnp.concatenate([p, jnp.zeros((1, TL - b1.shape[1]), f32)], 1) for p in pieces[3:]]
    tail = jnp.concatenate(tail + [jnp.zeros((5, TL), f32)], 0)
    a_o[ra : ra + EXTRA, :] = jnp.concatenate(rows + [tail], 0).astype(bf16)
    rb = 0
    for w in (wp, w1, w2):
        for i in range(0, w.shape[1], TL):
            b_o[rb : rb + w.shape[0], :] = w[:, i : i + TL]
            rb += w.shape[0]


def pack(geo, wq, wp, w1, w2, vec, b1):
    S = jax.ShapeDtypeStruct
    return pl.pallas_call(
        pack_body,
        out_shape=[S((geo.rows_a + EXTRA, TL), bf16), S((geo.rows_b, TL), bf16)],
        compiler_params=pltpu.CompilerParams(vmem_limit_bytes=16 * 2**20),
        cost_estimate=cost(1),
        name="pack",
    )(wq, wp, w1, w2, vec, b1)


def copies_a(geo, bufs, me, wq, sem):
    out = []
    for d in range(geo.nw):
        row = pl.multiple_of((me[0] ^ d) * geo.r, geo.r)
        for e in range(geo.nz):
            col = (me[1] ^ e) * geo.cq
            for i in range(geo.cq):
                out.append(
                    pltpu.make_async_copy(
                        bufs[d].at[e, pl.ds(i * geo.r, geo.r), :],
                        wq.at[col + i, pl.ds(row, geo.r), :],
                        sem,
                    )
                )
    return out


def copies_b(geo, bufs, me, wp, w1, w2, sem):
    out = []
    for d in range(geo.nw):
        row = pl.multiple_of((me[0] ^ d) * geo.r, geo.r)
        row2 = pl.multiple_of((me[0] ^ d) * geo.r2, geo.r2)
        for e in range(geo.nz):
            z = me[1] ^ e
            at = 0
            for w, n, r, to in ((wp, geo.cp, geo.r, row), (w1, geo.c1, geo.r, row), (w2, geo.cp, geo.r2, row2)):
                for i in range(n):
                    out.append(
                        pltpu.make_async_copy(
                            bufs[d].at[e, pl.ds(at, r), :], w.at[z * n + i, pl.ds(to, r), :], sem
                        )
                    )
                    at += r
    return out


def wide(ref, lo, n):
    return jnp.concatenate([ref[lo + i] for i in range(n)], 1)


def strided(ref, first, count, step):
    return jnp.concatenate([ref[half, pl.ds(first, count, stride=step), :] for half in range(2)], 1)


def bias_body(table, place, pb_o, zs):
    parts = jnp.concatenate([p for p in three(table[...])], 0)
    for cj in range(WS):
        z = dot(parts, place[cj])
        z = z[:HEADS] + z[HEADS : 2 * HEADS] + z[2 * HEADS :]
        for half in range(2):
            zs[half, cj * HEADS : (cj + 1) * HEADS, :] = z[:, half * TL : (half + 1) * TL]
    for j in range(NG):
        pb_o[j, WT:TP, :] = jnp.full((TP - WT, GH * TL), -1e30, f32)
        for h in range(GH):
            zh = strided(zs, j * GH + h, WS, HEADS)
            for rj in range(WS):
                off = (WS - 1 - rj) * WS
                part = zh if off == 0 else pltpu.roll(zh, 256 - off, 1)
                pb_o[j, rj * WS : (rj + 1) * WS, h * TL : (h + 1) * TL] = part[:, :TL]


def bias(table, place):
    return pl.pallas_call(
        bias_body,
        out_shape=jax.ShapeDtypeStruct((NG, TP, GH * TL), f32),
        scratch_shapes=[pltpu.VMEM((2, WS * HEADS, TL), f32)],
        compiler_params=pltpu.CompilerParams(vmem_limit_bytes=24 * 2**20),
        cost_estimate=cost(4),
        name="position_bias",
    )(table, place)


def table_sum(gt, place, rs):
    for j in range(NG):
        for h in range(GH):
            total = None
            for rj in range(WS):
                part = gt[j, rj * WS : (rj + 1) * WS, h * TL : (h + 1) * TL]
                part = jnp.concatenate([part, jnp.zeros((WS, TL), f32)], 1)
                off = (WS - 1 - rj) * WS
                part = part if off == 0 else pltpu.roll(part, off, 1)
                total = part if total is None else total + part
            base = (j * GH + h) * 16
            for half in range(2):
                rs[half, base : base + WS, :] = total[:, half * TL : (half + 1) * TL]
    out = jnp.zeros((HEADS, TT), f32)
    for cj in range(WS):
        parts = jnp.concatenate([p for p in three(strided(rs, cj, HEADS, 16))], 0)
        z = dot(parts, place[cj], NT)
        out = out + (z[:HEADS] + z[HEADS : 2 * HEADS] + z[2 * HEADS :])
    return out


def norm(x):
    mean = jnp.sum(x, -1, keepdims=True) * (1.0 / D)
    c = x - mean
    var = jnp.sum(c * c, -1, keepdims=True) * (1.0 / D)
    r = lax.rsqrt(var + EPS)
    return c * r, r


def norm_back(dn, xhat, r, gain):
    t = dn * gain
    m1 = jnp.sum(t, -1, keepdims=True) * (1.0 / D)
    m2 = jnp.sum(t * xhat, -1, keepdims=True) * (1.0 / D)
    return (t - m1 - xhat * m2) * r


def fill_blocks(bd, part):
    lane = lax.broadcasted_iota(jnp.int32, (1, TL), 1) // HD
    for h in range(GH):
        bd[h * TL : h * TL + TP, :] = jnp.where(lane == h, part, jnp.zeros_like(part))


def diag_t(full):
    return jnp.concatenate([full[h * HD : (h + 1) * HD, h * TL : (h + 1) * TL] for h in range(GH)], 0)


def gather_vectors(bufs, geo, me, vec_o, b1_o, tmp):
    own = D // (geo.nw * geo.nz)
    own1 = FF // (geo.nw * geo.nz)
    i32 = jnp.int32
    pick = (lax.broadcasted_iota(i32, (TL, D), 0) == lax.broadcasted_iota(i32, (TL, D), 1) % own).astype(bf16)
    pick1 = (lax.broadcasted_iota(i32, (TL, FF), 0) == lax.broadcasted_iota(i32, (TL, FF), 1) % own1).astype(bf16)
    slot = lax.broadcasted_iota(i32, (1, D), 1) // own
    slot1 = lax.broadcasted_iota(i32, (1, FF), 1) // own1
    vec = jnp.zeros((8, D), f32)
    b1 = jnp.zeros((8, FF), f32)
    for d in range(geo.nw):
        for e in range(geo.nz):
            dev = (me[1] ^ e) * geo.nw + (me[0] ^ d)
            x = tmp[d, e]
            y = dot(x[:24], pick)
            vec = vec + jnp.where(slot == dev, y[:8] + y[8:16] + y[16:24], 0.0)
            y1 = dot(x[24:], pick1)
            b1 = b1 + jnp.where(slot1 == dev, y1, 0.0)
    vec_o[...] = vec
    b1_o[...] = b1[0:1] + b1[1:2] + b1[2:3]


def attn_fwd_body(geo, G, vectors_in, *refs):
    nb = geo.nw
    me, tok, pb = refs[:3]
    bufs = refs[3 : 3 + nb]
    refs = refs[3 + nb :]
    if vectors_in:
        vec, refs = refs[0], refs[1:]
    n1_o, q_o, k_o, v_o, p_o, a_o = refs[:6]
    refs = refs[6:]
    if not vectors_in:
        vec, b1_o = refs[:2]
        refs = refs[2:]
    xs, bd, wq, tmp, sem, sem2 = refs

    @pl.when(pl.program_id(0) == 0)
    def _():
        moves = copies_a(geo, bufs, me, wq, sem)
        for m in moves:
            m.start()
        if not vectors_in:
            small = [
                pltpu.make_async_copy(bufs[d].at[:, pl.ds(geo.rows_a, EXTRA), :], tmp.at[d], sem2)
                for d in range(geo.nw)
            ]
            for m in small:
                m.start()
        xs[...] = jnp.zeros_like(xs)
        bd[...] = jnp.zeros_like(bd)
        if not vectors_in:
            for m in small:
                m.wait()
            gather_vectors(bufs, geo, me, vec, b1_o, tmp)
        for m in moves:
            m.wait()

    for g in range(G):
        xs[g * TP : g * TP + WT, :] = tok[g].astype(f32)
    xhat, _ = norm(xs[...])
    n1 = (xhat * vec[0:1, :] + vec[1:2, :]).astype(bf16)
    n1_o[...] = n1
    q_o[...] = ((dot(n1, wide(wq, 0, NG)) + vec[2:3, :]) * SCALE).astype(bf16)
    k_o[...] = dot(n1, wide(wq, NG, NG)).astype(bf16)
    v_o[...] = (dot(n1, wide(wq, 2 * NG, NG)) + vec[3:4, :]).astype(bf16)

    def window(g, carry):
        rows = pl.ds(pl.multiple_of(g * TP, 16), TP)
        for j in range(NG):
            cols = slice(j * TL, (j + 1) * TL)
            qg = q_o[rows, cols]
            kg = k_o[rows, cols]
            vg = v_o[rows, cols]
            b = bd.at[j]
            fill_blocks(b, qg)
            s = dot(kg, b[...], NT) + pb[j]
            m = jnp.max(s, 0, keepdims=True)
            e = jnp.exp(s - m)
            l = jnp.sum(e, 0, keepdims=True)
            p = (e * (1.0 / l)).astype(bf16)
            p_o[g, j] = p
            at = diag_t(dot(vg, p, TN))
            a_o[rows, cols] = at.T[:TP].astype(bf16)
        return carry

    lax.fori_loop(0, G, window, 0)


def attn_fwd(geo, me, tok, pb, bufs, vec=None, G=4):
    B = tok.shape[0]
    R = B * TP
    S = jax.ShapeDtypeStruct
    act = S((R, D), bf16)
    blk = pl.BlockSpec((G * TP, D), lambda i: (i, 0))
    given = [] if vec is None else [vec]
    out_specs = [blk, blk, blk, blk, pl.BlockSpec((G, NG, TP, GH * TL), lambda i: (i, 0, 0, 0)), blk]
    out_shape = [act, act, act, act, S((B, NG, TP, GH * TL), bf16), act]
    if vec is None:
        out_specs += [whole((8, D)), whole((1, FF))]
        out_shape += [S((8, D), f32), S((1, FF), f32)]
    return pl.pallas_call(
        functools.partial(attn_fwd_body, geo, G, vec is not None),
        grid=(B // G,),
        in_specs=[smem(), pl.BlockSpec((G, WT, D), lambda i: (i, 0, 0)), whole(pb.shape)]
        + [anyspace()] * len(bufs)
        + [whole(g.shape) for g in given],
        out_specs=out_specs,
        out_shape=out_shape,
        scratch_shapes=[
            pltpu.VMEM((G * TP, D), f32),
            pltpu.VMEM((NG, GH * TL, TL), bf16),
            pltpu.VMEM((3 * NG, D, TL), bf16),
            pltpu.VMEM((geo.nw, geo.nz, EXTRA, TL), bf16),
            pltpu.SemaphoreType.DMA,
            pltpu.SemaphoreType.DMA,
        ],
        compiler_params=params(),
        cost_estimate=cost(30),
        name="attn_fwd",
    )(me, tok, pb, *bufs, *given)


GC = 0.7978845608028654
GA = 0.044715


def gelu_both(u):
    u2 = u * u
    t = jnp.tanh(u * (GC + (GC * GA) * u2))
    h = 0.5 + 0.5 * t
    act = u * h
    slope = h + (act * (2.0 - 2.0 * h)) * (GC + (3.0 * GC * GA) * u2)
    return act, slope


def scatter_out(geo, me, blocks, outs):
    cores = len(outs)
    for c in range(cores):
        for xy in range(geo.nw // cores):
            w = me[0] ^ (xy * cores + c)
            for e in range(geo.nz):
                z = me[1] ^ e
                at = 0
                for ref, pick in blocks:
                    for part in pick(ref, w, z):
                        outs[c][xy, e, at : at + part.shape[0], :] = part.astype(bf16)
                        at += part.shape[0]


def mlp_body(geo, G, FC, *refs):
    nb = geo.nw
    me, live, tok, cot, attn = refs[:5]
    bufs = refs[5 : 5 + nb]
    vec, b1 = refs[5 + nb : 7 + nb]
    refs = refs[7 + nb :]
    out_o, dx1_o, da_o, gv_o, gb1_o = refs[:5]
    cores = 2 if nb > 1 else 1
    outs = refs[5 : 5 + cores]
    xs, dys, gp, g1, g2, gv, gb1, acc, dn2, wp, w1, w2, sem = refs[5 + cores :]
    i = pl.program_id(0)
    n = pl.num_programs(0)

    @pl.when(i == 0)
    def _():
        moves = copies_b(geo, bufs, me, wp, w1, w2, sem)
        for m in moves:
            m.start()
        for ref in (xs, dys, gp, g1, g2, gv, gb1):
            ref[...] = jnp.zeros_like(ref)
        for m in moves:
            m.wait()

    for g in range(G):
        xs[g * TP : g * TP + WT, :] = tok[g].astype(f32)
        mask = (i * G + g < live[0]).astype(f32)
        dys[g * TP : g * TP + WT, :] = cot[g].astype(f32) * mask
    at = attn[...]
    wpv = wide(wp, 0, NG)
    x1 = xs[...] + dot(at, wpv) + vec[4:5, :]
    acc[...] = x1 + vec[7:8, :]
    xhat, r = norm(x1)
    n2 = (xhat * vec[5:6, :] + vec[6:7, :]).astype(bf16)
    n2t = n2.T
    dyf = dys[...]
    dy = dyf.astype(bf16)
    dyt = dy.T
    ns = FC // TL
    for c in range(FF // FC):
        cols = slice(c * FC, (c + 1) * FC)
        w1c = wide(w1, c * ns, ns)
        w2c = jnp.concatenate([w2[z, cols, :] for z in range(NG)], 1)
        u = dot(n2, w1c) + b1[:, cols]
        a, ga = gelu_both(u)
        a = a.astype(bf16)
        acc[...] += dot(a, w2c)
        du = (dot(dy, w2c, NT) * ga).astype(bf16)
        t2 = dot(dyt, a)
        t1 = dot(n2t, du)
        for k in range(ns):
            g2[c * ns + k] += t2[:, k * TL : (k + 1) * TL]
            g1[c * ns + k] += t1[:, k * TL : (k + 1) * TL]
        gb1[:, cols] += jnp.sum(du.astype(f32), 0, keepdims=True)
        d = dot(du, w1c, NT)
        if c == 0:
            dn2[...] = d
        else:
            dn2[...] += d
    for g in range(G):
        mask = (i * G + g < live[0]).astype(f32)
        out_o[g] = (acc[g * TP : g * TP + WT, :] * mask).astype(bf16)
    dn = dn2[...]
    gv[7:8, :] += jnp.sum(dyf, 0, keepdims=True)
    gv[5:6, :] += jnp.sum(dn * xhat, 0, keepdims=True)
    gv[6:7, :] += jnp.sum(dn, 0, keepdims=True)
    dx1 = dyf + norm_back(dn, xhat, r, vec[5:6, :])
    dx1_o[...] = dx1
    dl = dx1.astype(bf16)
    gv[4:5, :] += jnp.sum(dl.astype(f32), 0, keepdims=True)
    tp = dot(at.T, dl)
    for k in range(NG):
        gp[k] += tp[:, k * TL : (k + 1) * TL]
    da_o[...] = dot(dl, wpv, NT).astype(bf16)

    @pl.when(i == n - 1)
    def _():
        gv_o[...] = gv[...]
        gb1_o[...] = gb1[...]

        def rows(ref, n):
            def pick(ref, w, z):
                at = pl.multiple_of(w * geo.r, geo.r)
                return [ref[z * n + k, pl.ds(at, geo.r), :] for k in range(n)]

            return ref, pick

        def turned(ref, w, z):
            n, r = geo.r2 // TL, D // geo.nz
            at = pl.multiple_of(z * r, r)
            return [ref[w * n + k, pl.ds(at, r), :] for k in range(n)]

        scatter_out(geo, me, [rows(gp, geo.cp), rows(g1, geo.c1), (g2, turned)], outs)


def mlp(geo, me, live, tok, cot, attn, bufs, vec, b1, G=4, FC=512):
    B = tok.shape[0]
    R = B * TP
    M = G * TP
    blk = pl.BlockSpec((M, D), lambda i: (i, 0))
    win = pl.BlockSpec((G, WT, D), lambda i: (i, 0, 0))
    S = jax.ShapeDtypeStruct
    cores = 2 if geo.nw > 1 else 1
    gshape = (geo.nw // cores, geo.nz, geo.rows_b, TL)
    V = pltpu.VMEM
    return pl.pallas_call(
        functools.partial(mlp_body, geo, G, FC),
        grid=(B // G,),
        in_specs=[smem(), smem(), win, win, blk] + [anyspace()] * len(bufs) + [whole(vec.shape), whole(b1.shape)],
        out_specs=[win, blk, blk, whole((8, D)), whole((1, FF))] + [whole(gshape)] * cores,
        out_shape=[S(tok.shape, bf16), S((R, D), f32), S((R, D), bf16), S((8, D), f32), S((1, FF), f32)]
        + [S(gshape, bf16)] * cores,
        scratch_shapes=[
            V((M, D), f32),
            V((M, D), f32),
            V((NG, D, TL), f32),
            V((FF // TL, D, TL), f32),
            V((FF // TL, D, TL), f32),
            V((8, D), f32),
            V((1, FF), f32),
            V((M, D), f32),
            V((M, D), f32),
            V((NG, D, TL), bf16),
            V((FF // TL, D, TL), bf16),
            V((NG, FF, TL), bf16),
            pltpu.SemaphoreType.DMA,
        ],
        compiler_params=params(),
        cost_estimate=cost(44),
        name="mlp",
    )(me, live, tok, cot, attn, *bufs, vec, b1)


def attn_bwd_body(geo, G, *refs):
    me, q, k, v, p, da, n1, dc_o, gb_o, gt_o = refs[:10]
    cores = 2 if geo.nw > 1 else 1
    outs = refs[10 : 10 + cores]
    bdq, bda, gq, gb, gt = refs[10 + cores :]
    i = pl.program_id(0)
    n = pl.num_programs(0)

    @pl.when(i == 0)
    def _():
        for ref in (bdq, bda, gq, gb, gt):
            ref[...] = jnp.zeros_like(ref)

    def window(g, carry):
        rows = pl.ds(pl.multiple_of(g * TP, 16), TP)
        for j in range(NG):
            cols = slice(j * TL, (j + 1) * TL)
            qg, kg, vg, dg = q[rows, cols], k[rows, cols], v[rows, cols], da[rows, cols]
            bq, ba = bdq.at[j], bda.at[j]
            fill_blocks(bq, qg)
            fill_blocks(ba, dg)
            pt = p[g, j]
            pf = pt.astype(f32)
            dp = dot(vg, ba[...], NT)
            t = pf * dp
            ds = (t - pf * jnp.sum(t, 0, keepdims=True)).astype(bf16)
            gt[j] += ds.astype(f32)
            dv = dot(pt, ba[...])
            dk = dot(ds, bq[...])
            dq = diag_t(dot(kg, ds, TN)).T[:TP] * SCALE
            dc_o[rows, j * TL : (j + 1) * TL] = dq.astype(bf16)
            dc_o[rows, D + j * TL : D + (j + 1) * TL] = dk.astype(bf16)
            dc_o[rows, 2 * D + j * TL : 2 * D + (j + 1) * TL] = dv.astype(bf16)
        return carry

    lax.fori_loop(0, G, window, 0)
    n1t = n1[...].T
    for c in range(3):
        cols = slice(c * D, (c + 1) * D)
        dc = dc_o[:, cols]
        t = dot(n1t, dc)
        for s in range(NG):
            gq[c * NG + s] += t[:, s * TL : (s + 1) * TL]
        gb[:, cols] += jnp.sum(dc.astype(f32), 0, keepdims=True)

    @pl.when(i == n - 1)
    def _():
        gb_o[...] = gb[...]
        gt_o[...] = gt[...]

        def rows(ref, w, z):
            at = pl.multiple_of(w * geo.r, geo.r)
            return [ref[z * geo.cq + s, pl.ds(at, geo.r), :] for s in range(geo.cq)]

        scatter_out(geo, me, [(gq, rows)], outs)


def attn_bwd(geo, me, q, k, v, p, da, n1, G=4):
    R = q.shape[0]
    B = R // TP
    blk = pl.BlockSpec((G * TP, D), lambda i: (i, 0))
    S = jax.ShapeDtypeStruct
    V = pltpu.VMEM
    cores = 2 if geo.nw > 1 else 1
    gshape = (geo.nw // cores, geo.nz, geo.rows_a, TL)
    return pl.pallas_call(
        functools.partial(attn_bwd_body, geo, G),
        grid=(B // G,),
        in_specs=[smem(), blk, blk, blk, pl.BlockSpec((G, NG, TP, GH * TL), lambda i: (i, 0, 0, 0)), blk, blk],
        out_specs=[pl.BlockSpec((G * TP, 3 * D), lambda i: (i, 0)), whole((1, 3 * D)), whole((NG, TP, GH * TL))]
        + [whole(gshape)] * cores,
        out_shape=[S((R, 3 * D), bf16), S((1, 3 * D), f32), S((NG, TP, GH * TL), f32)] + [S(gshape, bf16)] * cores,
        scratch_shapes=[
            V((NG, GH * TL, TL), bf16),
            V((NG, GH * TL, TL), bf16),
            V((3 * NG, D, TL), f32),
            V((1, 3 * D), f32),
            V((NG, TP, GH * TL), f32),
        ],
        compiler_params=params(),
        cost_estimate=cost(30),
        name="attn_bwd",
    )(me, q, k, v, p, da, n1)


def input_bwd_body(geo, G, *refs):
    nb = geo.nw
    me, tok, dc, dx1, vec, gv2, gb, gb1, gt, place = refs[:10]
    bufs = refs[10 : 10 + nb]
    gt_o, small_o, xs, gv, rs, wq, sem = refs[10 + nb :]
    i = pl.program_id(0)
    n = pl.num_programs(0)

    @pl.when(i == 0)
    def _():
        moves = copies_a(geo, bufs, me, wq, sem)
        for m in moves:
            m.start()
        xs[...] = jnp.zeros_like(xs)
        gv[...] = jnp.zeros_like(gv)
        small_o[8:24, :TT] = table_sum(gt, place, rs)
        for k in range(FF // TL):
            small_o[8 + k : 9 + k, TT:] = gb1[:, k * TL : (k + 1) * TL]
        for m in moves:
            m.wait()

    for g in range(G):
        xs[g * TP : g * TP + WT, :] = tok[g].astype(f32)
    dn = dot(dc[...], wide(wq, 0, 3 * NG), NT)
    xhat, r = norm(xs[...])
    gv[0:1, :] += jnp.sum(dn * xhat, 0, keepdims=True)
    gv[1:2, :] += jnp.sum(dn, 0, keepdims=True)
    dx = dx1[...] + norm_back(dn, xhat, r, vec[0:1, :])
    for g in range(G):
        gt_o[g] = dx[g * TP : g * TP + WT].astype(bf16)

    @pl.when(i == n - 1)
    def _():
        small_o[0:2, :] = gv[0:2, :]
        small_o[2:3, :] = gb[:, :D]
        small_o[3:4, :] = gb[:, 2 * D :]
        small_o[4:8, :] = gv2[4:8, :]


def input_bwd(geo, me, tok, dc, dx1, vec, gv2, gb, gb1, gt, place, bufs, G=4):
    B = tok.shape[0]
    blk = pl.BlockSpec((G * TP, D), lambda i: (i, 0))
    win = pl.BlockSpec((G, WT, D), lambda i: (i, 0, 0))
    S = jax.ShapeDtypeStruct
    V = pltpu.VMEM
    return pl.pallas_call(
        functools.partial(input_bwd_body, geo, G),
        grid=(B // G,),
        in_specs=[smem(), win, pl.BlockSpec((G * TP, 3 * D), lambda i: (i, 0)), blk]
        + [whole(x.shape) for x in (vec, gv2, gb, gb1, gt, place)]
        + [anyspace()] * len(bufs),
        out_specs=[win, whole((24, D))],
        out_shape=[S(tok.shape, bf16), S((24, D), f32)],
        scratch_shapes=[
            V((G * TP, D), f32),
            V((8, D), f32),
            V((2, HEADS * 16, TL), f32),
            V((3 * NG, D, TL), bf16),
            pltpu.SemaphoreType.DMA,
        ],
        compiler_params=params(),
        cost_estimate=cost(11),
        name="input_bwd",
    )(me, tok, dc, dx1, vec, gv2, gb, gb1, gt, place, *bufs)


def swap(x, axis, size, d):
    return lax.ppermute(x, axis, [(i, i ^ d) for i in range(size)])


def gather_pieces(buf, nw, nz):
    mine = jnp.stack([buf] + [swap(buf, "fsdp", nz, e) for e in range(1, nz)])
    planes = [mine] + [swap(mine, "win", nw, 2 * d) for d in range(1, nw // 2)]
    out = []
    for x in planes:
        out += [x, swap(x, "win", nw, 1)]
    return out


def scatter_sum(keep, send, nw, nz):
    got = swap(send, "win", nw, 1)
    sums = [(keep[d].astype(f32) + got[d].astype(f32)).astype(bf16) for d in range(nw // 2)]
    total = sums[0].astype(f32)
    for d in range(1, nw // 2):
        total = total + swap(sums[d], "win", nw, 2 * d).astype(f32)
    low = total.astype(bf16)
    own = total[0]
    for e in range(1, nz):
        own = own + swap(low[e], "fsdp", nz, e).astype(f32)
    return own


def sum_all(x, nw, nz):
    x = x + swap(x, "win", nw, 1)
    x = x + functools.reduce(jnp.add, [swap(x, "win", nw, 2 * d) for d in range(1, nw // 2)])
    return x + functools.reduce(jnp.add, [swap(x, "fsdp", nz, e) for e in range(1, nz)])


def unslab(x, n):
    r = x.shape[0] // n
    return jnp.concatenate([x[i * r : (i + 1) * r] for i in range(n)], 1)


def split_b(geo, x):
    a, b = geo.cp * geo.r, (geo.cp + geo.c1) * geo.r
    two = x[b:].reshape(geo.r2 // TL, D // geo.nz, TL).transpose(0, 2, 1).reshape(geo.r2, D // geo.nz)
    return unslab(x[:a], geo.cp), unslab(x[a:b], geo.c1), two


def body(nw, nz, tokens, live, vectors, fc1_bias, w_qkv, w_proj, w_fc1, w_fc2, rel_table, cotangent):
    both = ("fsdp", "win")
    fast = D // nz % TL == 0 and FF // nw % TL == 0 and D // nw % 16 == 0 and nw > 1 and nz > 1
    fast = fast and nw & (nw - 1) == 0 and nz & (nz - 1) == 0
    place = offset_place()
    table = jnp.pad(rel_table.T, ((0, 0), (0, TT - TABLE)))
    if fast:
        geo = Geometry(nw, nz)
        me = jnp.stack([lax.axis_index("win"), lax.axis_index("fsdp")]).astype(jnp.int32)
        buf_a, buf_b = pack(geo, w_qkv, w_proj, w_fc1, w_fc2, vectors, fc1_bias.reshape(1, -1))
        bufs_a = gather_pieces(buf_a, nw, nz)
        bufs_b = gather_pieces(buf_b, nw, nz)
        pb = bias(table, place)
        n1, q, k, v, p, att, vec, b1 = attn_fwd(geo, me, tokens, pb, bufs_a)
    else:
        geo = Geometry(1, 1)
        me = jnp.zeros((2,), jnp.int32)

        def full(w):
            return lax.all_gather(lax.all_gather(w, "fsdp", axis=1, tiled=True), "win", axis=0, tiled=True)

        bufs_a = [slabs(full(w_qkv))[None]]
        bufs_b = [jnp.concatenate([slabs(full(w)) for w in (w_proj, w_fc1, w_fc2)], 0)[None]]
        vec = lax.all_gather(vectors, both, axis=1, tiled=True)
        b1 = lax.all_gather(fc1_bias, both, axis=0, tiled=True).reshape(1, -1)
        pb = bias(table, place)
        n1, q, k, v, p, att = attn_fwd(geo, me, tokens, pb, bufs_a, vec)
    out, dx1, da, gv2, gb1, *gw = mlp(geo, me, live, tokens, cotangent, att, bufs_b, vec, b1)
    dc, gb, gt, *gq = attn_bwd(geo, me, q, k, v, p, da, n1)
    grad_tokens, small = input_bwd(geo, me, tokens, dc, dx1, vec, gv2, gb, gb1, gt, place, bufs_a)
    if fast:
        own_b = scatter_sum(*gw, nw, nz)
        own_a = scatter_sum(*gq, nw, nz)
        small = sum_all(small, nw, nz)
        grad_qkv = unslab(own_a, geo.cq)
        grad_proj, grad_one, grad_two = split_b(geo, own_b)
    else:

        def down(g):
            g = lax.psum_scatter(g.astype(bf16), "win", scatter_dimension=0, tiled=True)
            return lax.psum_scatter(g, "fsdp", scatter_dimension=1, tiled=True).astype(f32)

        grad_qkv = down(unslab(gq[0][0, 0], geo.cq))
        grad_proj, grad_one, grad_two = [down(g) for g in split_b(geo, gw[0][0, 0])]
        small = lax.psum(small, both)
    dev = lax.axis_index(both)
    own, own1 = D // (nw * nz), FF // (nw * nz)
    grad_vectors = lax.dynamic_slice_in_dim(small[:8], dev * own, own, 1)
    grad_bias = lax.dynamic_slice_in_dim(small[8:, TT:].reshape(FF), dev * own1, own1, 0)
    grad_table = small[8:, :TABLE].T
    return out, grad_tokens, grad_vectors, grad_bias, grad_qkv, grad_proj, grad_one, grad_two, grad_table


def solution(mesh):
    split = P(("fsdp", "win"), None, None)
    vecs = P(None, ("fsdp", "win"))
    flat = P(("fsdp", "win"))
    cut = P("win", "fsdp")
    return jax.shard_map(
        functools.partial(body, mesh.shape["win"], mesh.shape["fsdp"]),
        mesh=mesh,
        in_specs=(split, flat, vecs, flat, cut, cut, cut, cut, P(), split),
        out_specs=(split, split, vecs, flat, cut, cut, cut, cut, P()),
        check_vma=False,
    )
```

```python
import functools

import jax
import jax.numpy as jnp
import numpy as np
from jax import lax
from jax.experimental import pallas as pl
from jax.experimental.pallas import tpu as pltpu
from jax.sharding import PartitionSpec as P

f32 = jnp.float32
bf16 = jnp.bfloat16
HEADS = 16
HD = 32
WS = 10
WT = WS * WS
D = HEADS * HD
FF = 4 * D
SIDE = 2 * WS - 1
TABLE = SIDE * SIDE
TP = 112
TL = 128
TT = 384
GH = 4
NG = HEADS // GH
EPS = 1e-5
SCALE = HD**-0.5
EXTRA = 32
NN = (((1,), (0,)), ((), ()))
NT = (((1,), (1,)), ((), ()))
TN = (((0,), (0,)), ((), ()))


def dot(a, b, dims=NN):
    return lax.dot_general(a, b, dims, preferred_element_type=f32)


def params(n=1):
    return pltpu.CompilerParams(dimension_semantics=("arbitrary",) * n, vmem_limit_bytes=60 * 2**20)


def cost(us):
    return pl.CostEstimate(flops=int(us * 1.1e9), bytes_accessed=int(us * 1e6), transcendentals=0)


def whole(shape):
    n = len(shape)
    return pl.BlockSpec(shape, lambda *a: (0,) * n, pipeline_mode=pl.Buffered(1))


def smem():
    return pl.BlockSpec(memory_space=pltpu.SMEM)


def anyspace():
    return pl.BlockSpec(memory_space=pl.ANY)


def three(x):
    hi = x.astype(bf16)
    rest = x - hi.astype(f32)
    mid = rest.astype(bf16)
    return hi, mid, (rest - mid.astype(f32)).astype(bf16)


def offset_place():
    cj = np.arange(WS)[:, None, None]
    r = np.arange(TT)[None, :, None]
    l = np.arange(256)[None, None, :]
    hit = (l < SIDE * WS) & (r == (l // WS) * SIDE + (l % WS) - cj + WS - 1)
    return jnp.asarray(hit, bf16)


class Geometry:
    def __init__(self, nw, nz):
        self.nw, self.nz = nw, nz
        self.r = D // nw
        self.cq, self.cp, self.c1 = 3 * D // nz // TL, D // nz // TL, FF // nz // TL
        self.r2 = FF // nw
        self.rows_a = self.cq * self.r
        self.rows_b = self.cp * self.r + self.c1 * self.r + self.cp * self.r2


def slabs(x):
    return jnp.concatenate([x[:, i : i + TL] for i in range(0, x.shape[1], TL)], 0)


def pack_body(count, *refs):
    srcs, out = refs[:count], refs[count]
    rest = refs[count + 1 :]
    stage, flat, sem = rest[: len(srcs)], rest[-2], rest[-1]
    moves = [pltpu.make_async_copy(x, y, sem.at[i]) for i, (x, y) in enumerate(zip(srcs, stage))]
    for m in moves:
        m.start()
    at = 0
    for m, w in zip(moves, stage):
        m.wait()
        if w.dtype == f32:
            part = [p.astype(f32) for p in three(w[...])]
            part = [jnp.concatenate([p, jnp.zeros((p.shape[0], TL - p.shape[1]), f32)], 1) for p in part]
            part = jnp.concatenate(part, 0)
            if part.shape[0] == 24:
                kept = part
                continue
            part = jnp.concatenate([kept, part, jnp.zeros((EXTRA - 27, TL), f32)], 0)
            flat[at : at + EXTRA, :] = part.astype(bf16)
            at += EXTRA
            continue
        for i in range(0, w.shape[1], TL):
            flat[at : at + w.shape[0], :] = w[:, i : i + TL]
            at += w.shape[0]
    last = pltpu.make_async_copy(flat, out, sem.at[count])
    last.start()
    last.wait()


def pack(rows, *arrays):
    V = pltpu.VMEM
    return pl.pallas_call(
        functools.partial(pack_body, len(arrays)),
        in_specs=[anyspace()] * len(arrays),
        out_specs=anyspace(),
        out_shape=jax.ShapeDtypeStruct((rows, TL), bf16),
        scratch_shapes=[V(x.shape, x.dtype) for x in arrays]
        + [V((rows, TL), bf16), pltpu.SemaphoreType.DMA((len(arrays) + 1,))],
        compiler_params=pltpu.CompilerParams(vmem_limit_bytes=60 * 2**20),
        cost_estimate=cost(2),
        name="pack",
    )(*arrays)


def copies_a(geo, bufs, me, wq, sem):
    out = []
    for d in range(geo.nw):
        row = pl.multiple_of((me[0] ^ d) * geo.r, geo.r)
        for e in range(geo.nz):
            col = (me[1] ^ e) * geo.cq
            for i in range(geo.cq):
                out.append(
                    pltpu.make_async_copy(
                        bufs[d].at[e, pl.ds(i * geo.r, geo.r), :],
                        wq.at[col + i, pl.ds(row, geo.r), :],
                        sem,
                    )
                )
    return out


def copies_b(geo, bufs, me, wp, w1, w2, sem):
    out = []
    for d in range(geo.nw):
        row = pl.multiple_of((me[0] ^ d) * geo.r, geo.r)
        row2 = pl.multiple_of((me[0] ^ d) * geo.r2, geo.r2)
        for e in range(geo.nz):
            z = me[1] ^ e
            at = 0
            for w, n, r, to in ((wp, geo.cp, geo.r, row), (w1, geo.c1, geo.r, row), (w2, geo.cp, geo.r2, row2)):
                for i in range(n):
                    out.append(
                        pltpu.make_async_copy(
                            bufs[d].at[e, pl.ds(at, r), :], w.at[z * n + i, pl.ds(to, r), :], sem
                        )
                    )
                    at += r
    return out


def wide(ref, lo, n):
    return jnp.concatenate([ref[lo + i] for i in range(n)], 1)


def strided(ref, first, count, step):
    return jnp.concatenate([ref[half, pl.ds(first, count, stride=step), :] for half in range(2)], 1)


def bias_body(table, place, pb_o, zs):
    parts = jnp.concatenate([p for p in three(table[...])], 0)
    for cj in range(WS):
        z = dot(parts, place[cj])
        z = z[:HEADS] + z[HEADS : 2 * HEADS] + z[2 * HEADS :]
        for half in range(2):
            zs[half, cj * HEADS : (cj + 1) * HEADS, :] = z[:, half * TL : (half + 1) * TL]
    for j in range(NG):
        pb_o[j, WT:TP, :] = jnp.full((TP - WT, GH * TL), -1e30, f32)
        for h in range(GH):
            zh = strided(zs, j * GH + h, WS, HEADS)
            for rj in range(WS):
                off = (WS - 1 - rj) * WS
                part = zh if off == 0 else pltpu.roll(zh, 256 - off, 1)
                pb_o[j, rj * WS : (rj + 1) * WS, h * TL : (h + 1) * TL] = part[:, :TL]


def bias(table, place):
    return pl.pallas_call(
        bias_body,
        out_shape=jax.ShapeDtypeStruct((NG, TP, GH * TL), f32),
        scratch_shapes=[pltpu.VMEM((2, WS * HEADS, TL), f32)],
        compiler_params=pltpu.CompilerParams(vmem_limit_bytes=24 * 2**20),
        cost_estimate=cost(4),
        name="position_bias",
    )(table, place)


def table_sum(gt, place, rs):
    for j in range(NG):
        for h in range(GH):
            total = None
            for rj in range(WS):
                part = gt[j, rj * WS : (rj + 1) * WS, h * TL : (h + 1) * TL]
                part = jnp.concatenate([part, jnp.zeros((WS, TL), f32)], 1)
                off = (WS - 1 - rj) * WS
                part = part if off == 0 else pltpu.roll(part, off, 1)
                total = part if total is None else total + part
            base = (j * GH + h) * 16
            for half in range(2):
                rs[half, base : base + WS, :] = total[:, half * TL : (half + 1) * TL]
    out = jnp.zeros((HEADS, TT), f32)
    for cj in range(WS):
        parts = jnp.concatenate([p for p in three(strided(rs, cj, HEADS, 16))], 0)
        z = dot(parts, place[cj], NT)
        out = out + (z[:HEADS] + z[HEADS : 2 * HEADS] + z[2 * HEADS :])
    return out


def norm(x):
    mean = jnp.sum(x, -1, keepdims=True) * (1.0 / D)
    c = x - mean
    var = jnp.sum(c * c, -1, keepdims=True) * (1.0 / D)
    r = lax.rsqrt(var + EPS)
    return c * r, r


def norm_back(dn, xhat, r, gain):
    t = dn * gain
    m1 = jnp.sum(t, -1, keepdims=True) * (1.0 / D)
    m2 = jnp.sum(t * xhat, -1, keepdims=True) * (1.0 / D)
    return (t - m1 - xhat * m2) * r


def fill_blocks(bd, part):
    lane = lax.broadcasted_iota(jnp.int32, (1, TL), 1) // HD
    for h in range(GH):
        bd[h * TL : h * TL + TP, :] = jnp.where(lane == h, part, jnp.zeros_like(part))


def diag_t(full):
    return jnp.concatenate([full[h * HD : (h + 1) * HD, h * TL : (h + 1) * TL] for h in range(GH)], 0)


def gather_vectors(bufs, geo, me, vec_o, b1_o, tmp):
    own = D // (geo.nw * geo.nz)
    own1 = FF // (geo.nw * geo.nz)
    i32 = jnp.int32
    pick = (lax.broadcasted_iota(i32, (TL, D), 0) == lax.broadcasted_iota(i32, (TL, D), 1) % own).astype(bf16)
    pick1 = (lax.broadcasted_iota(i32, (TL, FF), 0) == lax.broadcasted_iota(i32, (TL, FF), 1) % own1).astype(bf16)
    slot = lax.broadcasted_iota(i32, (1, D), 1) // own
    slot1 = lax.broadcasted_iota(i32, (1, FF), 1) // own1
    vec = jnp.zeros((8, D), f32)
    b1 = jnp.zeros((8, FF), f32)
    for d in range(geo.nw):
        for e in range(geo.nz):
            dev = (me[1] ^ e) * geo.nw + (me[0] ^ d)
            x = tmp[d, e]
            y = dot(x[:24], pick)
            vec = vec + jnp.where(slot == dev, y[:8] + y[8:16] + y[16:24], 0.0)
            y1 = dot(x[24:], pick1)
            b1 = b1 + jnp.where(slot1 == dev, y1, 0.0)
    vec_o[...] = vec
    b1_o[...] = b1[0:1] + b1[1:2] + b1[2:3]


def attn_fwd_body(geo, G, vectors_in, *refs):
    nb = geo.nw
    me, tok, pb = refs[:3]
    bufs = refs[3 : 3 + nb]
    refs = refs[3 + nb :]
    if vectors_in:
        vec, refs = refs[0], refs[1:]
    n1_o, q_o, k_o, v_o, p_o, a_o = refs[:6]
    refs = refs[6:]
    if not vectors_in:
        vec, b1_o = refs[:2]
        refs = refs[2:]
    xs, bd, wq, tmp, sem, sem2 = refs

    @pl.when(pl.program_id(0) == 0)
    def _():
        moves = copies_a(geo, bufs, me, wq, sem)
        for m in moves:
            m.start()
        if not vectors_in:
            small = [
                pltpu.make_async_copy(bufs[d].at[:, pl.ds(geo.rows_a, EXTRA), :], tmp.at[d], sem2)
                for d in range(geo.nw)
            ]
            for m in small:
                m.start()
        xs[...] = jnp.zeros_like(xs)
        bd[...] = jnp.zeros_like(bd)
        if not vectors_in:
            for m in small:
                m.wait()
            gather_vectors(bufs, geo, me, vec, b1_o, tmp)
        for m in moves:
            m.wait()

    for g in range(G):
        xs[g * TP : g * TP + WT, :] = tok[g].astype(f32)
    xhat, _ = norm(xs[...])
    n1 = (xhat * vec[0:1, :] + vec[1:2, :]).astype(bf16)
    n1_o[...] = xhat.astype(bf16)
    q_o[...] = ((dot(n1, wide(wq, 0, NG)) + vec[2:3, :]) * SCALE).astype(bf16)
    k_o[...] = dot(n1, wide(wq, NG, NG)).astype(bf16)
    v_o[...] = (dot(n1, wide(wq, 2 * NG, NG)) + vec[3:4, :]).astype(bf16)

    def window(g, carry):
        rows = pl.ds(pl.multiple_of(g * TP, 16), TP)
        for j in range(NG):
            cols = slice(j * TL, (j + 1) * TL)
            qg = q_o[rows, cols]
            kg = k_o[rows, cols]
            vg = v_o[rows, cols]
            b = bd.at[j]
            fill_blocks(b, qg)
            s = dot(kg, b[...], NT) + pb[j]
            m = jnp.max(s, 0, keepdims=True)
            e = jnp.exp(s - m)
            l = jnp.sum(e, 0, keepdims=True)
            p = (e * (1.0 / l)).astype(bf16)
            p_o[g, j] = p
            at = diag_t(dot(vg, p, TN))
            a_o[rows, cols] = at.T[:TP].astype(bf16)
        return carry

    lax.fori_loop(0, G, window, 0)


def attn_fwd(geo, me, tok, pb, bufs, vec=None, G=4):
    B = tok.shape[0]
    R = B * TP
    S = jax.ShapeDtypeStruct
    act = S((R, D), bf16)
    blk = pl.BlockSpec((G * TP, D), lambda i: (i, 0))
    given = [] if vec is None else [vec]
    out_specs = [blk, blk, blk, blk, pl.BlockSpec((G, NG, TP, GH * TL), lambda i: (i, 0, 0, 0)), blk]
    out_shape = [act, act, act, act, S((B, NG, TP, GH * TL), bf16), act]
    if vec is None:
        out_specs += [whole((8, D)), whole((1, FF))]
        out_shape += [S((8, D), f32), S((1, FF), f32)]
    return pl.pallas_call(
        functools.partial(attn_fwd_body, geo, G, vec is not None),
        grid=(B // G,),
        in_specs=[smem(), pl.BlockSpec((G, WT, D), lambda i: (i, 0, 0)), whole(pb.shape)]
        + [anyspace()] * len(bufs)
        + [whole(g.shape) for g in given],
        out_specs=out_specs,
        out_shape=out_shape,
        scratch_shapes=[
            pltpu.VMEM((G * TP, D), f32),
            pltpu.VMEM((NG, GH * TL, TL), bf16),
            pltpu.VMEM((3 * NG, D, TL), bf16),
            pltpu.VMEM((geo.nw, geo.nz, EXTRA, TL), bf16),
            pltpu.SemaphoreType.DMA,
            pltpu.SemaphoreType.DMA,
        ],
        compiler_params=params(),
        cost_estimate=cost(30),
        name="attn_fwd",
    )(me, tok, pb, *bufs, *given)


GC = 0.7978845608028654
GA = 0.044715


def gelu_both(u):
    u2 = u * u
    t = jnp.tanh(u * (GC + (GC * GA) * u2))
    h = 0.5 + 0.5 * t
    act = u * h
    slope = h + (act * (2.0 - 2.0 * h)) * (GC + (3.0 * GC * GA) * u2)
    return act, slope


def scatter_out(geo, me, blocks, outs):
    cores = len(outs)
    for c in range(cores):
        for xy in range(geo.nw // cores):
            w = me[0] ^ (xy * cores + c)
            for e in range(geo.nz):
                z = me[1] ^ e
                at = 0
                for ref, pick in blocks:
                    for part in pick(ref, w, z):
                        outs[c][xy, e, at : at + part.shape[0], :] = part.astype(bf16)
                        at += part.shape[0]


def mlp_body(geo, G, FC, *refs):
    nb = geo.nw
    me, live, tok, cot, attn = refs[:5]
    bufs = refs[5 : 5 + nb]
    vec, b1 = refs[5 + nb : 7 + nb]
    refs = refs[7 + nb :]
    out_o, dx1_o, da_o, gv_o, gb1_o = refs[:5]
    cores = 2 if nb > 1 else 1
    outs = refs[5 : 5 + cores]
    xs, dys, gp, g1, g2, gv, gb1, acc, dn2, wp, w1, w2, sem = refs[5 + cores :]
    i = pl.program_id(0)
    n = pl.num_programs(0)

    @pl.when(i == 0)
    def _():
        moves = copies_b(geo, bufs, me, wp, w1, w2, sem)
        for m in moves:
            m.start()
        for ref in (xs, dys, gp, g1, g2, gv, gb1):
            ref[...] = jnp.zeros_like(ref)
        for m in moves:
            m.wait()

    for g in range(G):
        xs[g * TP : g * TP + WT, :] = tok[g].astype(f32)
        mask = (i * G + g < live[0]).astype(f32)
        dys[g * TP : g * TP + WT, :] = cot[g].astype(f32) * mask
    at = attn[...]
    wpv = wide(wp, 0, NG)
    x1 = xs[...] + dot(at, wpv) + vec[4:5, :]
    acc[...] = x1 + vec[7:8, :]
    xhat, r = norm(x1)
    n2 = (xhat * vec[5:6, :] + vec[6:7, :]).astype(bf16)
    n2t = n2.T
    dyf = dys[...]
    dy = dyf.astype(bf16)
    dyt = dy.T
    ns = FC // TL
    for c in range(FF // FC):
        cols = slice(c * FC, (c + 1) * FC)
        w1c = wide(w1, c * ns, ns)
        w2c = jnp.concatenate([w2[z, cols, :] for z in range(NG)], 1)
        u = dot(n2, w1c) + b1[:, cols]
        a, ga = gelu_both(u)
        a = a.astype(bf16)
        acc[...] += dot(a, w2c)
        du = (dot(dy, w2c, NT) * ga).astype(bf16)
        t2 = dot(dyt, a)
        t1 = dot(n2t, du)
        for k in range(ns):
            g2[c * ns + k] += t2[:, k * TL : (k + 1) * TL]
            g1[c * ns + k] += t1[:, k * TL : (k + 1) * TL]
        gb1[:, cols] += jnp.sum(du.astype(f32), 0, keepdims=True)
        d = dot(du, w1c, NT)
        if c == 0:
            dn2[...] = d
        else:
            dn2[...] += d
    for g in range(G):
        mask = (i * G + g < live[0]).astype(f32)
        out_o[g] = (acc[g * TP : g * TP + WT, :] * mask).astype(bf16)
    dn = dn2[...]
    gv[7:8, :] += jnp.sum(dyf, 0, keepdims=True)
    gv[5:6, :] += jnp.sum(dn * xhat, 0, keepdims=True)
    gv[6:7, :] += jnp.sum(dn, 0, keepdims=True)
    dx1 = dyf + norm_back(dn, xhat, r, vec[5:6, :])
    dx1_o[...] = dx1
    dl = dx1.astype(bf16)
    gv[4:5, :] += jnp.sum(dl.astype(f32), 0, keepdims=True)
    tp = dot(at.T, dl)
    for k in range(NG):
        gp[k] += tp[:, k * TL : (k + 1) * TL]
    da_o[...] = dot(dl, wpv, NT).astype(bf16)

    @pl.when(i == n - 1)
    def _():
        gv_o[...] = gv[...]
        gb1_o[...] = gb1[...]

        def rows(ref, n):
            def pick(ref, w, z):
                at = pl.multiple_of(w * geo.r, geo.r)
                return [ref[z * n + k, pl.ds(at, geo.r), :] for k in range(n)]

            return ref, pick

        def turned(ref, w, z):
            n, r = geo.r2 // TL, D // geo.nz
            at = pl.multiple_of(z * r, r)
            return [ref[w * n + k, pl.ds(at, r), :] for k in range(n)]

        scatter_out(geo, me, [rows(gp, geo.cp), rows(g1, geo.c1), (g2, turned)], outs)


def mlp(geo, me, live, tok, cot, attn, bufs, vec, b1, G=4, FC=512):
    B = tok.shape[0]
    R = B * TP
    M = G * TP
    blk = pl.BlockSpec((M, D), lambda i: (i, 0))
    win = pl.BlockSpec((G, WT, D), lambda i: (i, 0, 0))
    S = jax.ShapeDtypeStruct
    cores = 2 if geo.nw > 1 else 1
    gshape = (geo.nw // cores, geo.nz, geo.rows_b, TL)
    V = pltpu.VMEM
    return pl.pallas_call(
        functools.partial(mlp_body, geo, G, FC),
        grid=(B // G,),
        in_specs=[smem(), smem(), win, win, blk] + [anyspace()] * len(bufs) + [whole(vec.shape), whole(b1.shape)],
        out_specs=[win, blk, blk, whole((8, D)), whole((1, FF))] + [whole(gshape)] * cores,
        out_shape=[S(tok.shape, bf16), S((R, D), f32), S((R, D), bf16), S((8, D), f32), S((1, FF), f32)]
        + [S(gshape, bf16)] * cores,
        scratch_shapes=[
            V((M, D), f32),
            V((M, D), f32),
            V((NG, D, TL), f32),
            V((FF // TL, D, TL), f32),
            V((FF // TL, D, TL), f32),
            V((8, D), f32),
            V((1, FF), f32),
            V((M, D), f32),
            V((M, D), f32),
            V((NG, D, TL), bf16),
            V((FF // TL, D, TL), bf16),
            V((NG, FF, TL), bf16),
            pltpu.SemaphoreType.DMA,
        ],
        compiler_params=params(),
        cost_estimate=cost(44),
        name="mlp",
    )(me, live, tok, cot, attn, *bufs, vec, b1)


def attn_bwd_body(geo, G, *refs):
    nb = geo.nw
    me, q, k, v, p, da, xh, vec, gv2, gb1, place = refs[:11]
    bufs = refs[11 : 11 + nb]
    refs = refs[11 + nb :]
    cores = 2 if nb > 1 else 1
    dc_o, small_o = refs[:2]
    outs = refs[2 : 2 + cores]
    bdq, bda, gq, gb, gt, wq, rs, ex, sem = refs[2 + cores :]
    i = pl.program_id(0)
    n = pl.num_programs(0)

    @pl.when(i == 0)
    def _():
        for m in copies_a(geo, bufs, me, wq, sem):
            m.start()
        for ref in (bdq, bda, gq, gb, gt):
            ref[...] = jnp.zeros_like(ref)
        for m in copies_a(geo, bufs, me, wq, sem):
            m.wait()

    def window(g, carry):
        rows = pl.ds(pl.multiple_of(g * TP, 16), TP)
        for j in range(NG):
            cols = slice(j * TL, (j + 1) * TL)
            qg, kg, vg, dg = q[rows, cols], k[rows, cols], v[rows, cols], da[rows, cols]
            bq, ba = bdq.at[j], bda.at[j]
            fill_blocks(bq, qg)
            fill_blocks(ba, dg)
            pt = p[g, j]
            pf = pt.astype(f32)
            dp = dot(vg, ba[...], NT)
            t = pf * dp
            ds = (t - pf * jnp.sum(t, 0, keepdims=True)).astype(bf16)
            gt[j] += ds.astype(f32)
            dv = dot(pt, ba[...])
            dk = dot(ds, bq[...])
            dq = diag_t(dot(kg, ds, TN)).T[:TP] * SCALE
            dc_o[rows, j * TL : (j + 1) * TL] = dq.astype(bf16)
            dc_o[rows, D + j * TL : D + (j + 1) * TL] = dk.astype(bf16)
            dc_o[rows, 2 * D + j * TL : 2 * D + (j + 1) * TL] = dv.astype(bf16)
        return carry

    lax.fori_loop(0, G, window, 0)
    xt = xh[...].T
    for c in range(3):
        cols = slice(c * D, (c + 1) * D)
        dc = dc_o[:, cols]
        t = dot(xt, dc)
        for s in range(NG):
            gq[c * NG + s] += t[:, s * TL : (s + 1) * TL]
        gb[:, cols] += jnp.sum(dc.astype(f32), 0, keepdims=True)

    @pl.when(i == n - 1)
    def _():
        sums = gb[...]
        ones = jnp.ones((8, D), bf16)
        gain = jnp.zeros((8, D), f32)
        shift = jnp.zeros((8, D), f32)
        for c in range(3):
            w = wide(wq, c * NG, NG)
            prod = wide(gq, c * NG, NG) * w.astype(f32)
            for part in three(prod)[:2]:
                gain = gain + dot(ones, part, NT)
            part = [x.astype(f32) for x in three(sums[:, c * D : (c + 1) * D])]
            part = jnp.concatenate(part + [jnp.zeros((5, D), f32)], 0).astype(bf16)
            shift = shift + dot(part, w, NT)
        g_col = jnp.broadcast_to(vec[0:1, :], (TL, D)).T
        s_col = jnp.broadcast_to(vec[1:2, :], (TL, D)).T
        for s in range(3 * NG):
            gq[s] = gq[s] * g_col + s_col * sums[:, s * TL : (s + 1) * TL]
        small_o[0:1, :] = gain[0:1]
        small_o[1:2, :] = shift[0:1] + shift[1:2] + shift[2:3]
        small_o[2:3, :] = sums[:, :D]
        small_o[3:4, :] = sums[:, 2 * D :]
        small_o[4:8, :] = gv2[4:8, :]
        small_o[8:24, :TT] = table_sum(gt, place, rs)
        for k in range(FF // TL):
            small_o[8 + k : 9 + k, TT:] = gb1[:, k * TL : (k + 1) * TL]

        if nb > 1:
            for z in range(geo.nz):
                ex[z] = extra_rows(geo, small_o, gb1, z)

        def rows(ref, w, z):
            at = pl.multiple_of(w * geo.r, geo.r)
            parts = [ref[z * geo.cq + s, pl.ds(at, geo.r), :] for s in range(geo.cq)]
            return parts if nb == 1 else parts + [ex[z]]

        scatter_out(geo, me, [(gq, rows)], outs)


def extra_rows(geo, small, gb1, z):
    nh = HEADS // geo.nz
    vec = small[0:8, z * TL : (z + 1) * TL]
    first = z * (FF // geo.nz)
    bias = [gb1[:, first + k * TL : first + (k + 1) * TL] for k in range(FF // geo.nz // TL)]
    table = [small[8 + z * nh : 8 + (z + 1) * nh, k * TL : (k + 1) * TL] for k in range(TT // TL)]
    rows = [vec] + bias + table
    used = sum(r.shape[0] for r in rows)
    return jnp.concatenate(rows + [jnp.zeros((EXTRA - used, TL), f32)], 0)


def attn_bwd(geo, me, q, k, v, p, da, xh, vec, gv2, gb1, place, bufs, G=4):
    R = q.shape[0]
    B = R // TP
    blk = pl.BlockSpec((G * TP, D), lambda i: (i, 0))
    S = jax.ShapeDtypeStruct
    V = pltpu.VMEM
    cores = 2 if geo.nw > 1 else 1
    gshape = (geo.nw // cores, geo.nz, geo.rows_a + (EXTRA if cores == 2 else 0), TL)
    return pl.pallas_call(
        functools.partial(attn_bwd_body, geo, G),
        grid=(B // G,),
        in_specs=[smem(), blk, blk, blk, pl.BlockSpec((G, NG, TP, GH * TL), lambda i: (i, 0, 0, 0)), blk, blk]
        + [whole(x.shape) for x in (vec, gv2, gb1, place)]
        + [anyspace()] * len(bufs),
        out_specs=[pl.BlockSpec((G * TP, 3 * D), lambda i: (i, 0)), whole((24, D))] + [whole(gshape)] * cores,
        out_shape=[S((R, 3 * D), bf16), S((24, D), f32)] + [S(gshape, bf16)] * cores,
        scratch_shapes=[
            V((NG, GH * TL, TL), bf16),
            V((NG, GH * TL, TL), bf16),
            V((3 * NG, D, TL), f32),
            V((1, 3 * D), f32),
            V((NG, TP, GH * TL), f32),
            V((3 * NG, D, TL), bf16),
            V((2, HEADS * 16, TL), f32),
            V((geo.nz, EXTRA, TL), f32),
            pltpu.SemaphoreType.DMA,
        ],
        compiler_params=params(),
        cost_estimate=cost(30),
        name="attn_bwd",
    )(me, q, k, v, p, da, xh, vec, gv2, gb1, place, *bufs)


def input_bwd_body(geo, G, *refs):
    nb = geo.nw
    me, tok, dc, dx1, vec = refs[:5]
    bufs = refs[5 : 5 + nb]
    gt_o, xs, wq, sem = refs[5 + nb :]

    @pl.when(pl.program_id(0) == 0)
    def _():
        moves = copies_a(geo, bufs, me, wq, sem)
        for m in moves:
            m.start()
        xs[...] = jnp.zeros_like(xs)
        for m in moves:
            m.wait()

    for g in range(G):
        xs[g * TP : g * TP + WT, :] = tok[g].astype(f32)
    dn = dot(dc[...], wide(wq, 0, 3 * NG), NT)
    xhat, r = norm(xs[...])
    dx = dx1[...] + norm_back(dn, xhat, r, vec[0:1, :])
    for g in range(G):
        gt_o[g] = dx[g * TP : g * TP + WT].astype(bf16)


def input_bwd(geo, me, tok, dc, dx1, vec, bufs, G=4):
    B = tok.shape[0]
    blk = pl.BlockSpec((G * TP, D), lambda i: (i, 0))
    win = pl.BlockSpec((G, WT, D), lambda i: (i, 0, 0))
    S = jax.ShapeDtypeStruct
    V = pltpu.VMEM
    return pl.pallas_call(
        functools.partial(input_bwd_body, geo, G),
        grid=(B // G,),
        in_specs=[smem(), win, pl.BlockSpec((G * TP, 3 * D), lambda i: (i, 0)), blk, whole(vec.shape)]
        + [anyspace()] * len(bufs),
        out_specs=win,
        out_shape=S(tok.shape, bf16),
        scratch_shapes=[V((G * TP, D), f32), V((3 * NG, D, TL), bf16), pltpu.SemaphoreType.DMA],
        compiler_params=params(),
        cost_estimate=cost(10),
        name="input_bwd",
    )(me, tok, dc, dx1, vec, *bufs)


def finish_body(geo, nz, *refs):
    me, low_a, low_b = refs[:3]
    got_b = refs[3 : 2 + nz]
    got_a = refs[2 + nz : 1 + 2 * nz]
    gq_o, gp_o, g1_o, g2_o, vec_o, b1_o, tab_o, tab = refs[1 + 2 * nz :]
    r, r2 = geo.r, geo.r2
    rows = geo.rows_a + EXTRA

    def total(low, got, lo, n):
        out = low[0, lo : lo + n, :].astype(f32)
        for x in got:
            out = out + x[lo : lo + n, :].astype(f32)
        return out

    for i in range(geo.cq):
        gq_o[:, i * TL : (i + 1) * TL] = total(low_a, got_a, i * r, r)
    at = 0
    for ref, n in ((gp_o, geo.cp), (g1_o, geo.c1)):
        for i in range(n):
            ref[:, i * TL : (i + 1) * TL] = total(low_b, got_b, at, r)
            at += r
    wide_z = D // nz
    for k in range(r2 // TL):
        g2_o[k * TL : (k + 1) * TL, :] = total(low_b, got_b, at, wide_z).T
        at += wide_z
    nb = FF // nz // TL
    small = total(low_a, got_a, geo.rows_a, 16)
    own, own1 = vec_o.shape[1], b1_o.shape[1]
    vec_o[...] = pltpu.roll(small[:8], (TL - me[0] * own) % TL, 1)[:, :own]
    first = me[0] * own1
    b1 = pltpu.roll(small[8 : 8 + nb], (TL - first % TL) % TL, 1)
    row = lax.broadcasted_iota(jnp.int32, b1.shape, 0) == first // TL
    b1_o[...] = jnp.sum(jnp.where(row, b1, 0.0), 0, keepdims=True)[:, :own1]
    nh = HEADS // nz
    lo = 8 + nb
    for e in range(nz):
        t = low_a[e, geo.rows_a : rows, :].astype(f32)
        for d in range(1, nz):
            t = t + got_a[d - 1][rows + (e ^ d) * EXTRA : rows + ((e ^ d) + 1) * EXTRA, :].astype(f32)
        for k in range(TT // TL):
            tab[me[1] ^ e, :, k * TL : (k + 1) * TL] = t[lo + k * nh : lo + (k + 1) * nh]
    full = jnp.concatenate([tab[z] for z in range(nz)], 0)
    tab_o[...] = full.T[:TABLE]


def finish(geo, nw, nz, me, low_a, low_b, got_b, got_a):
    S = jax.ShapeDtypeStruct
    vmem = pl.BlockSpec(memory_space=pltpu.VMEM)
    return pl.pallas_call(
        functools.partial(finish_body, geo, nz),
        in_specs=[smem()] + [vmem] * (2 * nz),
        out_specs=[vmem] * 7,
        out_shape=[
            S((geo.r, geo.cq * TL), f32),
            S((geo.r, geo.cp * TL), f32),
            S((geo.r, geo.c1 * TL), f32),
            S((geo.r2, geo.cp * TL), f32),
            S((8, D // (nw * nz)), f32),
            S((1, FF // (nw * nz)), f32),
            S((TABLE, HEADS), f32),
        ],
        scratch_shapes=[pltpu.VMEM((nz, HEADS // nz, TT), f32)],
        compiler_params=pltpu.CompilerParams(vmem_limit_bytes=60 * 2**20),
        cost_estimate=cost(3),
        name="finish",
    )(me, low_a, low_b, *got_b, *got_a)


def swap(x, axis, size, d):
    return lax.ppermute(x, axis, [(i, i ^ d) for i in range(size)])


def after(x, *deps):
    return lax.optimization_barrier((x, *deps))[0]


def gather_z(buf, nz):
    return jnp.stack([buf] + [swap(buf, "fsdp", nz, e) for e in range(1, nz)])


def gather_xy(mine, nw):
    return [mine] + [swap(mine, "win", nw, 2 * d) for d in range(1, nw // 2)]


def gather_core(planes, nw):
    return [y for x in planes for y in (x, swap(x, "win", nw, 1))]


def sum_core(keep, got, nw):
    return [(keep[d].astype(f32) + got[d].astype(f32)).astype(bf16) for d in range(nw // 2)]


def swap_xy(sums, nw):
    return [sums[0]] + [swap(sums[d], "win", nw, 2 * d) for d in range(1, nw // 2)]


def sum_xy(parts):
    return functools.reduce(jnp.add, [x.astype(f32) for x in parts]).astype(bf16)


def swap_z(low, nz):
    return [swap(low[e], "fsdp", nz, e) for e in range(1, nz)]


def unslab(x, n):
    r = x.shape[0] // n
    return jnp.concatenate([x[i * r : (i + 1) * r] for i in range(n)], 1)


def split_b(geo, x):
    a, b = geo.cp * geo.r, (geo.cp + geo.c1) * geo.r
    two = x[b:].reshape(geo.r2 // TL, D // geo.nz, TL).transpose(0, 2, 1).reshape(geo.r2, D // geo.nz)
    return unslab(x[:a], geo.cp), unslab(x[a:b], geo.c1), two


def body(nw, nz, tokens, live, vectors, fc1_bias, w_qkv, w_proj, w_fc1, w_fc2, rel_table, cotangent):
    both = ("fsdp", "win")
    fast = D // nz == TL and FF // nw % TL == 0 and D // nw % 16 == 0 and nw > 1 and nz > 1
    fast = fast and nw & (nw - 1) == 0 and nz & (nz - 1) == 0
    place = offset_place()
    table = jnp.pad(rel_table.T, ((0, 0), (0, TT - TABLE)))
    dev = lax.axis_index(both)
    own, own1 = D // (nw * nz), FF // (nw * nz)
    if fast:
        geo = Geometry(nw, nz)
        me = jnp.stack([lax.axis_index("win"), lax.axis_index("fsdp")]).astype(jnp.int32)
        buf_a = pack(geo.rows_a + EXTRA, w_qkv, vectors, fc1_bias.reshape(1, -1))
        buf_b = pack(geo.rows_b, w_proj, w_fc1, w_fc2)
        mine_a = gather_z(buf_a, nz)
        pb = bias(table, place)
        planes_a = gather_xy(mine_a, nw)
        mine_b = gather_z(after(buf_b, mine_a), nz)
        bufs_a = gather_core(planes_a, nw)
        planes_b = gather_xy(after(mine_b, *bufs_a), nw)
        xh, q, k, v, p, att, vec, b1 = attn_fwd(geo, me, tokens, pb, bufs_a)
        planes_b = lax.optimization_barrier((*planes_b, att))[:-1]
        bufs_b = gather_core(planes_b, nw)
        out, dx1, da, gv2, gb1, keep_b, send_b = mlp(geo, me, live, tokens, cotangent, att, bufs_b, vec, b1)
        sums_b = sum_core(keep_b, swap(send_b, "win", nw, 1), nw)
        parts_b = swap_xy(sums_b, nw)
        da = after(da, *sums_b)
        dc, _, keep_a, send_a = attn_bwd(geo, me, q, k, v, p, da, xh, vec, gv2, gb1, place, bufs_a)
        *parts_b, send_a = lax.optimization_barrier((*parts_b, send_a))
        low_b = sum_xy(parts_b)
        sums_a = sum_core(keep_a, swap(send_a, "win", nw, 1), nw)
        parts_a = swap_xy(sums_a, nw)
        own_b = swap_z(low_b, nz)
        dc = after(dc, *sums_a)
        grad_tokens = input_bwd(geo, me, tokens, dc, dx1, vec, bufs_a)
        parts_a = lax.optimization_barrier((*parts_a, grad_tokens))[:-1]
        low_a = sum_xy(parts_a)
        tail = low_a[:, geo.rows_a :].reshape(nz * EXTRA, TL)
        own_a = [swap(jnp.concatenate([low_a[e], tail], 0), "fsdp", nz, e) for e in range(1, nz)]
        grad_qkv, grad_proj, grad_one, grad_two, grad_vectors, grad_bias, grad_table = finish(
            geo, nw, nz, me, low_a, low_b, own_b, own_a
        )
        grad_bias = grad_bias.reshape(-1)
    else:
        geo = Geometry(1, 1)
        me = jnp.zeros((2,), jnp.int32)

        def full(w):
            return lax.all_gather(lax.all_gather(w, "fsdp", axis=1, tiled=True), "win", axis=0, tiled=True)

        bufs_a = [slabs(full(w_qkv))[None]]
        bufs_b = [jnp.concatenate([slabs(full(w)) for w in (w_proj, w_fc1, w_fc2)], 0)[None]]
        vec = lax.all_gather(vectors, both, axis=1, tiled=True)
        b1 = lax.all_gather(fc1_bias, both, axis=0, tiled=True).reshape(1, -1)
        pb = bias(table, place)
        xh, q, k, v, p, att = attn_fwd(geo, me, tokens, pb, bufs_a, vec)
        out, dx1, da, gv2, gb1, gw = mlp(geo, me, live, tokens, cotangent, att, bufs_b, vec, b1)
        dc, small, gq = attn_bwd(geo, me, q, k, v, p, da, xh, vec, gv2, gb1, place, bufs_a)
        grad_tokens = input_bwd(geo, me, tokens, dc, dx1, vec, bufs_a)

        def down(g):
            g = lax.psum_scatter(g.astype(bf16), "win", scatter_dimension=0, tiled=True)
            return lax.psum_scatter(g, "fsdp", scatter_dimension=1, tiled=True).astype(f32)

        grad_qkv = down(unslab(gq[0, 0], geo.cq))
        grad_proj, grad_one, grad_two = [down(g) for g in split_b(geo, gw[0, 0])]
        small = lax.psum(small, both)
        grad_vectors = lax.dynamic_slice_in_dim(small[:8], dev * own, own, 1)
        grad_bias = lax.dynamic_slice_in_dim(small[8:, TT:].reshape(FF), dev * own1, own1, 0)
        grad_table = small[8:, :TABLE].T
    return out, grad_tokens, grad_vectors, grad_bias, grad_qkv, grad_proj, grad_one, grad_two, grad_table


def solution(mesh):
    split = P(("fsdp", "win"), None, None)
    vecs = P(None, ("fsdp", "win"))
    flat = P(("fsdp", "win"))
    cut = P("win", "fsdp")
    return jax.shard_map(
        functools.partial(body, mesh.shape["win"], mesh.shape["fsdp"]),
        mesh=mesh,
        in_specs=(split, flat, vecs, flat, cut, cut, cut, cut, P(), split),
        out_specs=(split, split, vecs, flat, cut, cut, cut, cut, P()),
        check_vma=False,
    )
```

```python
import functools

import jax
import jax.numpy as jnp
import numpy as np
from jax import lax
from jax.experimental import pallas as pl
from jax.experimental.pallas import tpu as pltpu
from jax.sharding import PartitionSpec as P

f32 = jnp.float32
bf16 = jnp.bfloat16
HEADS = 16
HD = 32
WS = 10
WT = WS * WS
D = HEADS * HD
FF = 4 * D
SIDE = 2 * WS - 1
TABLE = SIDE * SIDE
TP = 112
TL = 128
TT = 384
GH = 4
NG = HEADS // GH
EPS = 1e-5
SCALE = HD**-0.5
EXTRA = 32
NN = (((1,), (0,)), ((), ()))
NT = (((1,), (1,)), ((), ()))
TN = (((0,), (0,)), ((), ()))


def dot(a, b, dims=NN):
    return lax.dot_general(a, b, dims, preferred_element_type=f32)


def params(mib):
    return pltpu.CompilerParams(dimension_semantics=("arbitrary",), vmem_limit_bytes=mib * 2**20)


def cost(us):
    return pl.CostEstimate(flops=int(us * 1.1e9), bytes_accessed=int(us * 1e6), transcendentals=0)


def whole(shape):
    n = len(shape)
    return pl.BlockSpec(shape, lambda *a: (0,) * n, pipeline_mode=pl.Buffered(1))


def smem():
    return pl.BlockSpec(memory_space=pltpu.SMEM)


def anyspace():
    return pl.BlockSpec(memory_space=pl.ANY)


def three(x):
    hi = x.astype(bf16)
    rest = x - hi.astype(f32)
    mid = rest.astype(bf16)
    return hi, mid, (rest - mid.astype(f32)).astype(bf16)


def offset_place():
    cj = np.arange(WS)[:, None, None]
    r = np.arange(TT)[None, :, None]
    l = np.arange(256)[None, None, :]
    hit = (l < SIDE * WS) & (r == (l // WS) * SIDE + (l % WS) - cj + WS - 1)
    return jnp.asarray(hit, bf16)


class Geometry:
    def __init__(self, nw, nz):
        self.nw, self.nz = nw, nz
        self.r = D // nw
        self.cq, self.cp, self.c1 = 3 * D // nz // TL, D // nz // TL, FF // nz // TL
        self.r2 = FF // nw
        self.rows_a = self.cq * self.r
        self.rows_b = self.cp * self.r + self.c1 * self.r + self.cp * self.r2


def slabs(x):
    return jnp.concatenate([x[:, i : i + TL] for i in range(0, x.shape[1], TL)], 0)


def pack_body(count, *refs):
    srcs, out = refs[:count], refs[count]
    rest = refs[count + 1 :]
    stage, flat, sem = rest[: len(srcs)], rest[-2], rest[-1]
    moves = [pltpu.make_async_copy(x, y, sem.at[i]) for i, (x, y) in enumerate(zip(srcs, stage))]
    for m in moves:
        m.start()
    at = 0
    for m, w in zip(moves, stage):
        m.wait()
        if w.dtype == f32:
            part = [p.astype(f32) for p in three(w[...])]
            part = [jnp.concatenate([p, jnp.zeros((p.shape[0], TL - p.shape[1]), f32)], 1) for p in part]
            part = jnp.concatenate(part, 0)
            if part.shape[0] == 24:
                kept = part
                continue
            part = jnp.concatenate([kept, part, jnp.zeros((EXTRA - 27, TL), f32)], 0)
            flat[at : at + EXTRA, :] = part.astype(bf16)
            at += EXTRA
            continue
        for i in range(0, w.shape[1], TL):
            flat[at : at + w.shape[0], :] = w[:, i : i + TL]
            at += w.shape[0]
    last = pltpu.make_async_copy(flat, out, sem.at[count])
    last.start()
    last.wait()


def pack(rows, *arrays):
    V = pltpu.VMEM
    return pl.pallas_call(
        functools.partial(pack_body, len(arrays)),
        in_specs=[anyspace()] * len(arrays),
        out_specs=anyspace(),
        out_shape=jax.ShapeDtypeStruct((rows, TL), bf16),
        scratch_shapes=[V(x.shape, x.dtype) for x in arrays]
        + [V((rows, TL), bf16), pltpu.SemaphoreType.DMA((len(arrays) + 1,))],
        compiler_params=pltpu.CompilerParams(vmem_limit_bytes=60 * 2**20),
        cost_estimate=cost(2),
        name="pack",
    )(*arrays)


def copies_a(geo, bufs, me, wq, sem):
    out = []
    for d in range(geo.nw):
        row = pl.multiple_of((me[0] ^ d) * geo.r, geo.r)
        for e in range(geo.nz):
            col = (me[1] ^ e) * geo.cq
            for i in range(geo.cq):
                out.append(
                    pltpu.make_async_copy(
                        bufs[d].at[e, pl.ds(i * geo.r, geo.r), :],
                        wq.at[col + i, pl.ds(row, geo.r), :],
                        sem,
                    )
                )
    return out


def copies_b(geo, bufs, me, wp, w1, w2, sem):
    out = []
    for d in range(geo.nw):
        row = pl.multiple_of((me[0] ^ d) * geo.r, geo.r)
        row2 = pl.multiple_of((me[0] ^ d) * geo.r2, geo.r2)
        for e in range(geo.nz):
            z = me[1] ^ e
            at = 0
            for w, n, r, to in ((wp, geo.cp, geo.r, row), (w1, geo.c1, geo.r, row), (w2, geo.cp, geo.r2, row2)):
                for i in range(n):
                    out.append(
                        pltpu.make_async_copy(
                            bufs[d].at[e, pl.ds(at, r), :], w.at[z * n + i, pl.ds(to, r), :], sem
                        )
                    )
                    at += r
    return out


def wide(ref, lo, n):
    return jnp.concatenate([ref[lo + i] for i in range(n)], 1)


def strided(ref, first, count, step):
    return jnp.concatenate([ref[half, pl.ds(first, count, stride=step), :] for half in range(2)], 1)


def bias_body(table, place, pb_o, zs):
    parts = jnp.concatenate([p for p in three(table[...])], 0)
    for cj in range(WS):
        z = dot(parts, place[cj])
        z = z[:HEADS] + z[HEADS : 2 * HEADS] + z[2 * HEADS :]
        for half in range(2):
            zs[half, cj * HEADS : (cj + 1) * HEADS, :] = z[:, half * TL : (half + 1) * TL]
    for j in range(NG):
        pb_o[j, WT:TP, :] = jnp.zeros((TP - WT, GH * TL), f32)
        for h in range(GH):
            zh = strided(zs, j * GH + h, WS, HEADS)
            for rj in range(WS):
                off = (WS - 1 - rj) * WS
                part = zh if off == 0 else pltpu.roll(zh, 256 - off, 1)
                pb_o[j, rj * WS : (rj + 1) * WS, h * TL : (h + 1) * TL] = jnp.exp(part[:, :TL])


def bias(table, place):
    return pl.pallas_call(
        bias_body,
        out_shape=jax.ShapeDtypeStruct((NG, TP, GH * TL), f32),
        scratch_shapes=[pltpu.VMEM((2, WS * HEADS, TL), f32)],
        compiler_params=pltpu.CompilerParams(vmem_limit_bytes=24 * 2**20),
        cost_estimate=cost(4),
        name="position_bias",
    )(table, place)


def table_sum(gt, place, rs):
    for j in range(NG):
        for h in range(GH):
            total = None
            for rj in range(WS):
                part = gt[j, rj * WS : (rj + 1) * WS, h * TL : (h + 1) * TL]
                part = jnp.concatenate([part, jnp.zeros((WS, TL), f32)], 1)
                off = (WS - 1 - rj) * WS
                part = part if off == 0 else pltpu.roll(part, off, 1)
                total = part if total is None else total + part
            base = (j * GH + h) * 16
            for half in range(2):
                rs[half, base : base + WS, :] = total[:, half * TL : (half + 1) * TL]
    out = jnp.zeros((HEADS, TT), f32)
    for cj in range(WS):
        parts = jnp.concatenate([p for p in three(strided(rs, cj, HEADS, 16))], 0)
        z = dot(parts, place[cj], NT)
        out = out + (z[:HEADS] + z[HEADS : 2 * HEADS] + z[2 * HEADS :])
    return out


def norm(x):
    mean = jnp.sum(x, -1, keepdims=True) * (1.0 / D)
    c = x - mean
    var = jnp.sum(c * c, -1, keepdims=True) * (1.0 / D)
    r = lax.rsqrt(var + EPS)
    return c * r, r


def norm_back(dn, xhat, r, gain):
    t = dn * gain
    m1 = jnp.sum(t, -1, keepdims=True) * (1.0 / D)
    m2 = jnp.sum(t * xhat, -1, keepdims=True) * (1.0 / D)
    return (t - m1 - xhat * m2) * r


def spread(part):
    lane = lax.broadcasted_iota(jnp.int32, (1, TL), 1) // HD
    none = jnp.zeros((TL - TP, TL), part.dtype)
    return jnp.concatenate([x for h in range(GH) for x in (jnp.where(lane == h, part, jnp.zeros_like(part)), none)], 0)


def diag_t(full):
    return jnp.concatenate([full[h * HD : (h + 1) * HD, h * TL : (h + 1) * TL] for h in range(GH)], 0)


def gather_vectors(bufs, geo, me, vec_o, b1_o, tmp):
    own = D // (geo.nw * geo.nz)
    own1 = FF // (geo.nw * geo.nz)
    i32 = jnp.int32
    pick = (lax.broadcasted_iota(i32, (TL, D), 0) == lax.broadcasted_iota(i32, (TL, D), 1) % own).astype(bf16)
    pick1 = (lax.broadcasted_iota(i32, (TL, FF), 0) == lax.broadcasted_iota(i32, (TL, FF), 1) % own1).astype(bf16)
    slot = lax.broadcasted_iota(i32, (1, D), 1) // own
    slot1 = lax.broadcasted_iota(i32, (1, FF), 1) // own1
    vec = jnp.zeros((8, D), f32)
    b1 = jnp.zeros((8, FF), f32)
    for d in range(geo.nw):
        for e in range(geo.nz):
            dev = (me[1] ^ e) * geo.nw + (me[0] ^ d)
            x = tmp[d, e]
            y = dot(x[:24], pick)
            vec = vec + jnp.where(slot == dev, y[:8] + y[8:16] + y[16:24], 0.0)
            y1 = dot(x[24:], pick1)
            b1 = b1 + jnp.where(slot1 == dev, y1, 0.0)
    vec_o[...] = vec
    b1_o[...] = b1[0:1] + b1[1:2] + b1[2:3]


def attn_fwd_body(geo, G, vectors_in, *refs):
    nb = geo.nw
    me, tok, pb = refs[:3]
    bufs = refs[3 : 3 + nb]
    refs = refs[3 + nb :]
    if vectors_in:
        vec, refs = refs[0], refs[1:]
    n1_o, q_o, k_o, v_o, p_o, a_o = refs[:6]
    refs = refs[6:]
    if not vectors_in:
        vec, b1_o = refs[:2]
        refs = refs[2:]
    xs, wq, tmp, sem, sem2 = refs

    @pl.when(pl.program_id(0) == 0)
    def _():
        moves = copies_a(geo, bufs, me, wq, sem)
        for m in moves:
            m.start()
        if not vectors_in:
            small = [
                pltpu.make_async_copy(bufs[d].at[:, pl.ds(geo.rows_a, EXTRA), :], tmp.at[d], sem2)
                for d in range(geo.nw)
            ]
            for m in small:
                m.start()
        xs[...] = jnp.zeros_like(xs)
        if not vectors_in:
            for m in small:
                m.wait()
            gather_vectors(bufs, geo, me, vec, b1_o, tmp)
        for m in moves:
            m.wait()

    for g in range(G):
        xs[g * TP : g * TP + WT, :] = tok[g].astype(f32)
        xs[g * TP + WT : (g + 1) * TP, :] = tok[g, : TP - WT, :].astype(f32)
    xhat, _ = norm(xs[...])
    n1 = (xhat * vec[0:1, :] + vec[1:2, :]).astype(bf16)
    n1_o[...] = xhat.astype(bf16)
    q_o[...] = ((dot(n1, wide(wq, 0, NG)) + vec[2:3, :]) * SCALE).astype(bf16)
    k_o[...] = dot(n1, wide(wq, NG, NG)).astype(bf16)
    v_o[...] = (dot(n1, wide(wq, 2 * NG, NG)) + vec[3:4, :]).astype(bf16)

    def window(g, carry):
        rows = pl.ds(pl.multiple_of(g * TP, 16), TP)
        cols = [slice(j * TL, (j + 1) * TL) for j in range(NG)]
        ks = [k_o[rows, c] for c in cols]
        vs = [v_o[rows, c] for c in cols]
        qs = [spread(q_o[rows, c]) for c in cols]
        scores = [dot(ks[j], qs[j], NT) for j in range(NG)]
        ps, outs = [], []
        for j in range(NG):
            s = scores[j]
            e = jnp.exp(s - jnp.max(s, 0, keepdims=True)) * pb[j]
            p = (e * (1.0 / jnp.sum(e, 0, keepdims=True))).astype(bf16)
            ps.append(p)
            outs.append(diag_t(dot(vs[j], p, TN)).T[:TP].astype(bf16))
        for j in range(NG):
            p_o[g, j] = ps[j]
            a_o[rows, cols[j]] = outs[j]
        return carry

    lax.fori_loop(0, G, window, 0, unroll=G)


def attn_fwd(geo, me, tok, pb, bufs, vec=None, G=4):
    B = tok.shape[0]
    R = B * TP
    S = jax.ShapeDtypeStruct
    act = S((R, D), bf16)
    blk = pl.BlockSpec((G * TP, D), lambda i: (i, 0))
    given = [] if vec is None else [vec]
    out_specs = [blk, blk, blk, blk, pl.BlockSpec((G, NG, TP, GH * TL), lambda i: (i, 0, 0, 0)), blk]
    out_shape = [act, act, act, act, S((B, NG, TP, GH * TL), bf16), act]
    if vec is None:
        out_specs += [whole((8, D)), whole((1, FF))]
        out_shape += [S((8, D), f32), S((1, FF), f32)]
    return pl.pallas_call(
        functools.partial(attn_fwd_body, geo, G, vec is not None),
        grid=(B // G,),
        in_specs=[smem(), pl.BlockSpec((G, WT, D), lambda i: (i, 0, 0)), whole(pb.shape)]
        + [anyspace()] * len(bufs)
        + [whole(g.shape) for g in given],
        out_specs=out_specs,
        out_shape=out_shape,
        scratch_shapes=[
            pltpu.VMEM((G * TP, D), f32),
            pltpu.VMEM((3 * NG, D, TL), bf16),
            pltpu.VMEM((geo.nw, geo.nz, EXTRA, TL), bf16),
            pltpu.SemaphoreType.DMA,
            pltpu.SemaphoreType.DMA,
        ],
        compiler_params=params(28),
        cost_estimate=cost(30),
        name="attn_fwd",
    )(me, tok, pb, *bufs, *given)


GC = 0.7978845608028654
GA = 0.044715


def gelu_both(u):
    u2 = u * u
    t = jnp.tanh(u * (GC + (GC * GA) * u2))
    h = 0.5 + 0.5 * t
    act = u * h
    slope = h + (act * (2.0 - 2.0 * h)) * (GC + (3.0 * GC * GA) * u2)
    return act, slope


def scatter_out(geo, me, blocks, outs):
    cores = len(outs)
    for c in range(cores):
        for xy in range(geo.nw // cores):
            w = me[0] ^ (xy * cores + c)
            for e in range(geo.nz):
                z = me[1] ^ e
                at = 0
                for ref, pick in blocks:
                    for part in pick(ref, w, z):
                        outs[c][xy, e, at : at + part.shape[0], :] = part.astype(bf16)
                        at += part.shape[0]


def mlp_body(geo, G, FC, *refs):
    nb = geo.nw
    me, live, tok, cot, attn = refs[:5]
    bufs = refs[5 : 5 + nb]
    vec, b1 = refs[5 + nb : 7 + nb]
    refs = refs[7 + nb :]
    out_o, dx1_o, da_o, gv_o, gb1_o = refs[:5]
    cores = 2 if nb > 1 else 1
    outs = refs[5 : 5 + cores]
    xs, dys, gp, g1, g2, gv, gb1, acc, dn2, wp, w1, w2, sem = refs[5 + cores :]
    i = pl.program_id(0)
    n = pl.num_programs(0)

    @pl.when(i == 0)
    def _():
        moves = copies_b(geo, bufs, me, wp, w1, w2, sem)
        for m in moves:
            m.start()
        for ref in (xs, dys, gp, g1, g2, gv, gb1):
            ref[...] = jnp.zeros_like(ref)
        for m in moves:
            m.wait()

    for g in range(G):
        xs[g * TP : g * TP + WT, :] = tok[g].astype(f32)
        mask = (i * G + g < live[0]).astype(f32)
        dys[g * TP : g * TP + WT, :] = cot[g].astype(f32) * mask
    at = attn[...]
    wpv = wide(wp, 0, NG)
    x1 = xs[...] + dot(at, wpv) + vec[4:5, :]
    acc[...] = x1 + vec[7:8, :]
    xhat, r = norm(x1)
    n2 = (xhat * vec[5:6, :] + vec[6:7, :]).astype(bf16)
    n2t = n2.T
    dyf = dys[...]
    dy = dyf.astype(bf16)
    dyt = dy.T
    ns = FC // TL
    n = FF // FC

    def first(c):
        cols = slice(c * FC, (c + 1) * FC)
        w1c = wide(w1, c * ns, ns)
        w2c = jnp.concatenate([w2[z, cols, :] for z in range(NG)], 1)
        return w1c, w2c, dot(n2, w1c), dot(dy, w2c, NT)

    def last(c):
        cols = slice(c * FC, (c + 1) * FC)
        w1c, w2c = work[c][:2]
        a, du = mids[c]
        acc[...] += dot(a, w2c)
        t2 = dot(dyt, a)
        t1 = dot(n2t, du)
        for k in range(ns):
            g2[c * ns + k] += t2[:, k * TL : (k + 1) * TL]
            g1[c * ns + k] += t1[:, k * TL : (k + 1) * TL]
        gb1[:, cols] += jnp.sum(du.astype(f32), 0, keepdims=True)
        d = dot(du, w1c, NT)
        if c == 0:
            dn2[...] = d
        else:
            dn2[...] += d

    work = [first(c) for c in range(1)]
    mids = []
    for c in range(n + 1):
        if c + 1 < n:
            work.append(first(c + 1))
        if c < n:
            a, ga = gelu_both(work[c][2] + b1[:, c * FC : (c + 1) * FC])
            mids.append((a.astype(bf16), (work[c][3] * ga).astype(bf16)))
        if c >= 1:
            last(c - 1)
    n = pl.num_programs(0)
    for g in range(G):
        mask = (i * G + g < live[0]).astype(f32)
        out_o[g] = (acc[g * TP : g * TP + WT, :] * mask).astype(bf16)
    dn = dn2[...]
    gv[7:8, :] += jnp.sum(dyf, 0, keepdims=True)
    gv[5:6, :] += jnp.sum(dn * xhat, 0, keepdims=True)
    gv[6:7, :] += jnp.sum(dn, 0, keepdims=True)
    dx1 = dyf + norm_back(dn, xhat, r, vec[5:6, :])
    dx1_o[...] = dx1
    dl = dx1.astype(bf16)
    gv[4:5, :] += jnp.sum(dl.astype(f32), 0, keepdims=True)
    tp = dot(at.T, dl)
    for k in range(NG):
        gp[k] += tp[:, k * TL : (k + 1) * TL]
    da_o[...] = dot(dl, wpv, NT).astype(bf16)

    @pl.when(i == n - 1)
    def _():
        gv_o[...] = gv[...]
        gb1_o[...] = gb1[...]

        def rows(ref, n):
            def pick(ref, w, z):
                at = pl.multiple_of(w * geo.r, geo.r)
                return [ref[z * n + k, pl.ds(at, geo.r), :] for k in range(n)]

            return ref, pick

        def turned(ref, w, z):
            n, r = geo.r2 // TL, D // geo.nz
            at = pl.multiple_of(z * r, r)
            return [ref[w * n + k, pl.ds(at, r), :] for k in range(n)]

        scatter_out(geo, me, [rows(gp, geo.cp), rows(g1, geo.c1), (g2, turned)], outs)


def mlp(geo, me, live, tok, cot, attn, bufs, vec, b1, G=4, FC=512):
    B = tok.shape[0]
    R = B * TP
    M = G * TP
    blk = pl.BlockSpec((M, D), lambda i: (i, 0))
    win = pl.BlockSpec((G, WT, D), lambda i: (i, 0, 0))
    S = jax.ShapeDtypeStruct
    cores = 2 if geo.nw > 1 else 1
    gshape = (geo.nw // cores, geo.nz, geo.rows_b, TL)
    V = pltpu.VMEM
    return pl.pallas_call(
        functools.partial(mlp_body, geo, G, FC),
        grid=(B // G,),
        in_specs=[smem(), smem(), win, win, blk] + [anyspace()] * len(bufs) + [whole(vec.shape), whole(b1.shape)],
        out_specs=[win, blk, blk, whole((8, D)), whole((1, FF))] + [whole(gshape)] * cores,
        out_shape=[S(tok.shape, bf16), S((R, D), f32), S((R, D), bf16), S((8, D), f32), S((1, FF), f32)]
        + [S(gshape, bf16)] * cores,
        scratch_shapes=[
            V((M, D), f32),
            V((M, D), f32),
            V((NG, D, TL), f32),
            V((FF // TL, D, TL), f32),
            V((FF // TL, D, TL), f32),
            V((8, D), f32),
            V((1, FF), f32),
            V((M, D), f32),
            V((M, D), f32),
            V((NG, D, TL), bf16),
            V((FF // TL, D, TL), bf16),
            V((NG, FF, TL), bf16),
            pltpu.SemaphoreType.DMA,
        ],
        compiler_params=params(36),
        cost_estimate=cost(44),
        name="mlp",
    )(me, live, tok, cot, attn, *bufs, vec, b1)


def attn_bwd_body(geo, G, *refs):
    nb = geo.nw
    me, q, k, v, p, da, xh, vec, gv2, gb1, place = refs[:11]
    bufs = refs[11 : 11 + nb]
    refs = refs[11 + nb :]
    cores = 2 if nb > 1 else 1
    dc_o, small_o = refs[:2]
    outs = refs[2 : 2 + cores]
    gq, gb, gt, wq, rs, ex, sem = refs[2 + cores :]
    i = pl.program_id(0)
    n = pl.num_programs(0)

    @pl.when(i == 0)
    def _():
        for m in copies_a(geo, bufs, me, wq, sem):
            m.start()
        for ref in (gq, gb, gt):
            ref[...] = jnp.zeros_like(ref)
        for m in copies_a(geo, bufs, me, wq, sem):
            m.wait()

    def window(g, carry):
        rows = pl.ds(pl.multiple_of(g * TP, 16), TP)
        cols = [slice(j * TL, (j + 1) * TL) for j in range(NG)]
        ks = [k[rows, c] for c in cols]
        vs = [v[rows, c] for c in cols]
        bqs = [spread(q[rows, c]) for c in cols]
        bas = [spread(da[rows, c]) for c in cols]
        dps = [dot(vs[i], bas[i], NT) for i in range(2)]
        dqs, dks, dvs, dss = [], [], [], []
        pts = []
        for j in range(NG + 1):
            if j + 2 < NG:
                dps.append(dot(vs[j + 2], bas[j + 2], NT))
            if j < NG:
                pts.append(p[g, j])
                pf = pts[j].astype(f32)
                t = pf * dps[j]
                dss.append((t - pf * jnp.sum(t, 0, keepdims=True)).astype(bf16))
            if 0 <= j - 0 < NG:
                i = j - 0
                dvs.append(dot(pts[i], bas[i]).astype(bf16))
            if 0 <= j - 1 < NG:
                i = j - 1
                dks.append(dot(dss[i], bqs[i]).astype(bf16))
                dqs.append((diag_t(dot(ks[i], dss[i], TN)).T[:TP] * SCALE).astype(bf16))
        for j in range(NG):
            gt[j] += dss[j].astype(f32)
            dc_o[rows, j * TL : (j + 1) * TL] = dqs[j]
            dc_o[rows, D + j * TL : D + (j + 1) * TL] = dks[j]
            dc_o[rows, 2 * D + j * TL : 2 * D + (j + 1) * TL] = dvs[j]
        return carry

    lax.fori_loop(0, G, window, 0, unroll=G)
    xt = xh[...].T
    for c in range(3):
        cols = slice(c * D, (c + 1) * D)
        dc = dc_o[:, cols]
        t = dot(xt, dc)
        for s in range(NG):
            gq[c * NG + s] += t[:, s * TL : (s + 1) * TL]
        gb[:, cols] += jnp.sum(dc.astype(f32), 0, keepdims=True)

    @pl.when(i == n - 1)
    def _():
        sums = gb[...]
        ones = jnp.ones((8, D), bf16)
        gain = jnp.zeros((8, D), f32)
        shift = jnp.zeros((8, D), f32)
        for c in range(3):
            w = wide(wq, c * NG, NG)
            prod = wide(gq, c * NG, NG) * w.astype(f32)
            for part in three(prod)[:2]:
                gain = gain + dot(ones, part, NT)
            part = [x.astype(f32) for x in three(sums[:, c * D : (c + 1) * D])]
            part = jnp.concatenate(part + [jnp.zeros((5, D), f32)], 0).astype(bf16)
            shift = shift + dot(part, w, NT)
        g_col = jnp.broadcast_to(vec[0:1, :], (TL, D)).T
        s_col = jnp.broadcast_to(vec[1:2, :], (TL, D)).T
        for s in range(3 * NG):
            gq[s] = gq[s] * g_col + s_col * sums[:, s * TL : (s + 1) * TL]
        small_o[0:1, :] = gain[0:1]
        small_o[1:2, :] = shift[0:1] + shift[1:2] + shift[2:3]
        small_o[2:3, :] = sums[:, :D]
        small_o[3:4, :] = sums[:, 2 * D :]
        small_o[4:8, :] = gv2[4:8, :]
        small_o[8:24, :TT] = table_sum(gt, place, rs)
        for k in range(FF // TL):
            small_o[8 + k : 9 + k, TT:] = gb1[:, k * TL : (k + 1) * TL]

        if nb > 1:
            for z in range(geo.nz):
                ex[z] = extra_rows(geo, small_o, gb1, z)

        def rows(ref, w, z):
            at = pl.multiple_of(w * geo.r, geo.r)
            parts = [ref[z * geo.cq + s, pl.ds(at, geo.r), :] for s in range(geo.cq)]
            return parts if nb == 1 else parts + [ex[z]]

        scatter_out(geo, me, [(gq, rows)], outs)


def extra_rows(geo, small, gb1, z):
    nh = HEADS // geo.nz
    vec = small[0:8, z * TL : (z + 1) * TL]
    first = z * (FF // geo.nz)
    bias = [gb1[:, first + k * TL : first + (k + 1) * TL] for k in range(FF // geo.nz // TL)]
    table = [small[8 + z * nh : 8 + (z + 1) * nh, k * TL : (k + 1) * TL] for k in range(TT // TL)]
    rows = [vec] + bias + table
    used = sum(r.shape[0] for r in rows)
    return jnp.concatenate(rows + [jnp.zeros((EXTRA - used, TL), f32)], 0)


def attn_bwd(geo, me, q, k, v, p, da, xh, vec, gv2, gb1, place, bufs, G=4):
    R = q.shape[0]
    B = R // TP
    blk = pl.BlockSpec((G * TP, D), lambda i: (i, 0))
    S = jax.ShapeDtypeStruct
    V = pltpu.VMEM
    cores = 2 if geo.nw > 1 else 1
    gshape = (geo.nw // cores, geo.nz, geo.rows_a + (EXTRA if cores == 2 else 0), TL)
    return pl.pallas_call(
        functools.partial(attn_bwd_body, geo, G),
        grid=(B // G,),
        in_specs=[smem(), blk, blk, blk, pl.BlockSpec((G, NG, TP, GH * TL), lambda i: (i, 0, 0, 0)), blk, blk]
        + [whole(x.shape) for x in (vec, gv2, gb1, place)]
        + [anyspace()] * len(bufs),
        out_specs=[pl.BlockSpec((G * TP, 3 * D), lambda i: (i, 0)), whole((24, D))] + [whole(gshape)] * cores,
        out_shape=[S((R, 3 * D), bf16), S((24, D), f32)] + [S(gshape, bf16)] * cores,
        scratch_shapes=[
            V((3 * NG, D, TL), f32),
            V((1, 3 * D), f32),
            V((NG, TP, GH * TL), f32),
            V((3 * NG, D, TL), bf16),
            V((2, HEADS * 16, TL), f32),
            V((geo.nz, EXTRA, TL), f32),
            pltpu.SemaphoreType.DMA,
        ],
        compiler_params=params(32),
        cost_estimate=cost(30),
        name="attn_bwd",
    )(me, q, k, v, p, da, xh, vec, gv2, gb1, place, *bufs)


def input_bwd_body(geo, G, *refs):
    nb = geo.nw
    me, tok, dc, dx1, vec = refs[:5]
    bufs = refs[5 : 5 + nb]
    gt_o, xs, wq, sem = refs[5 + nb :]

    @pl.when(pl.program_id(0) == 0)
    def _():
        moves = copies_a(geo, bufs, me, wq, sem)
        for m in moves:
            m.start()
        xs[...] = jnp.zeros_like(xs)
        for m in moves:
            m.wait()

    for g in range(G):
        xs[g * TP : g * TP + WT, :] = tok[g].astype(f32)
    dn = dot(dc[...], wide(wq, 0, 3 * NG), NT)
    xhat, r = norm(xs[...])
    dx = dx1[...] + norm_back(dn, xhat, r, vec[0:1, :])
    for g in range(G):
        gt_o[g] = dx[g * TP : g * TP + WT].astype(bf16)


def input_bwd(geo, me, tok, dc, dx1, vec, bufs, G=4):
    B = tok.shape[0]
    blk = pl.BlockSpec((G * TP, D), lambda i: (i, 0))
    win = pl.BlockSpec((G, WT, D), lambda i: (i, 0, 0))
    S = jax.ShapeDtypeStruct
    V = pltpu.VMEM
    return pl.pallas_call(
        functools.partial(input_bwd_body, geo, G),
        grid=(B // G,),
        in_specs=[smem(), win, pl.BlockSpec((G * TP, 3 * D), lambda i: (i, 0)), blk, whole(vec.shape)]
        + [anyspace()] * len(bufs),
        out_specs=win,
        out_shape=S(tok.shape, bf16),
        scratch_shapes=[V((G * TP, D), f32), V((3 * NG, D, TL), bf16), pltpu.SemaphoreType.DMA],
        compiler_params=params(24),
        cost_estimate=cost(10),
        name="input_bwd",
    )(me, tok, dc, dx1, vec, *bufs)


def finish_body(geo, nz, *refs):
    me, low_a, low_b = refs[:3]
    got_b = refs[3 : 2 + nz]
    got_a = refs[2 + nz : 1 + 2 * nz]
    gq_o, gp_o, g1_o, g2_o, vec_o, b1_o, tab_o, tab = refs[1 + 2 * nz :]
    r, r2 = geo.r, geo.r2
    rows = geo.rows_a + EXTRA

    def total(low, got, lo, n):
        out = low[0, lo : lo + n, :].astype(f32)
        for x in got:
            out = out + x[lo : lo + n, :].astype(f32)
        return out

    for i in range(geo.cq):
        gq_o[:, i * TL : (i + 1) * TL] = total(low_a, got_a, i * r, r)
    at = 0
    for ref, n in ((gp_o, geo.cp), (g1_o, geo.c1)):
        for i in range(n):
            ref[:, i * TL : (i + 1) * TL] = total(low_b, got_b, at, r)
            at += r
    wide_z = D // nz
    for k in range(r2 // TL):
        g2_o[k * TL : (k + 1) * TL, :] = total(low_b, got_b, at, wide_z).T
        at += wide_z
    nb = FF // nz // TL
    small = total(low_a, got_a, geo.rows_a, 16)
    own, own1 = vec_o.shape[1], b1_o.shape[1]
    vec_o[...] = pltpu.roll(small[:8], (TL - me[0] * own) % TL, 1)[:, :own]
    first = me[0] * own1
    b1 = pltpu.roll(small[8 : 8 + nb], (TL - first % TL) % TL, 1)
    row = lax.broadcasted_iota(jnp.int32, b1.shape, 0) == first // TL
    b1_o[...] = jnp.sum(jnp.where(row, b1, 0.0), 0, keepdims=True)[:, :own1]
    nh = HEADS // nz
    lo = 8 + nb
    for e in range(nz):
        t = low_a[e, geo.rows_a : rows, :].astype(f32)
        for d in range(1, nz):
            t = t + got_a[d - 1][rows + (e ^ d) * EXTRA : rows + ((e ^ d) + 1) * EXTRA, :].astype(f32)
        for k in range(TT // TL):
            tab[me[1] ^ e, :, k * TL : (k + 1) * TL] = t[lo + k * nh : lo + (k + 1) * nh]
    full = jnp.concatenate([tab[z] for z in range(nz)], 0)
    tab_o[...] = full.T[:TABLE]


def finish(geo, nw, nz, me, low_a, low_b, got_b, got_a):
    S = jax.ShapeDtypeStruct
    vmem = pl.BlockSpec(memory_space=pltpu.VMEM)
    return pl.pallas_call(
        functools.partial(finish_body, geo, nz),
        in_specs=[smem()] + [vmem] * (2 * nz),
        out_specs=[vmem] * 7,
        out_shape=[
            S((geo.r, geo.cq * TL), f32),
            S((geo.r, geo.cp * TL), f32),
            S((geo.r, geo.c1 * TL), f32),
            S((geo.r2, geo.cp * TL), f32),
            S((8, D // (nw * nz)), f32),
            S((1, FF // (nw * nz)), f32),
            S((TABLE, HEADS), f32),
        ],
        scratch_shapes=[pltpu.VMEM((nz, HEADS // nz, TT), f32)],
        compiler_params=pltpu.CompilerParams(vmem_limit_bytes=60 * 2**20),
        cost_estimate=cost(3),
        name="finish",
    )(me, low_a, low_b, *got_b, *got_a)


def swap(x, axis, size, d):
    return lax.ppermute(x, axis, [(i, i ^ d) for i in range(size)])


def after(x, *deps):
    return lax.optimization_barrier((x, *deps))[0]


def gather_z(buf, nz):
    return jnp.stack([buf] + [swap(buf, "fsdp", nz, e) for e in range(1, nz)])


def gather_xy(mine, nw):
    return [mine] + [swap(mine, "win", nw, 2 * d) for d in range(1, nw // 2)]


def gather_core(planes, nw):
    return [y for x in planes for y in (x, swap(x, "win", nw, 1))]


def sum_core(keep, got, nw):
    return [(keep[d].astype(f32) + got[d].astype(f32)).astype(bf16) for d in range(nw // 2)]


def swap_xy(sums, nw):
    return [sums[0]] + [swap(sums[d], "win", nw, 2 * d) for d in range(1, nw // 2)]


def sum_xy(parts):
    return functools.reduce(jnp.add, [x.astype(f32) for x in parts]).astype(bf16)


def swap_z(low, nz):
    return [swap(low[e], "fsdp", nz, e) for e in range(1, nz)]


def unslab(x, n):
    r = x.shape[0] // n
    return jnp.concatenate([x[i * r : (i + 1) * r] for i in range(n)], 1)


def split_b(geo, x):
    a, b = geo.cp * geo.r, (geo.cp + geo.c1) * geo.r
    two = x[b:].reshape(geo.r2 // TL, D // geo.nz, TL).transpose(0, 2, 1).reshape(geo.r2, D // geo.nz)
    return unslab(x[:a], geo.cp), unslab(x[a:b], geo.c1), two


def body(nw, nz, tokens, live, vectors, fc1_bias, w_qkv, w_proj, w_fc1, w_fc2, rel_table, cotangent):
    both = ("fsdp", "win")
    fast = D // nz == TL and FF // nw % TL == 0 and D // nw % 16 == 0 and nw > 1 and nz > 1
    fast = fast and nw & (nw - 1) == 0 and nz & (nz - 1) == 0
    place = offset_place()
    table = jnp.pad(rel_table.T, ((0, 0), (0, TT - TABLE)))
    dev = lax.axis_index(both)
    own, own1 = D // (nw * nz), FF // (nw * nz)
    if fast:
        geo = Geometry(nw, nz)
        me = jnp.stack([lax.axis_index("win"), lax.axis_index("fsdp")]).astype(jnp.int32)
        buf_a = pack(geo.rows_a + EXTRA, w_qkv, vectors, fc1_bias.reshape(1, -1))
        buf_b = pack(geo.rows_b, w_proj, w_fc1, w_fc2)
        mine_a = gather_z(buf_a, nz)
        pb = bias(table, place)
        planes_a = gather_xy(mine_a, nw)
        mine_b = gather_z(after(buf_b, mine_a), nz)
        bufs_a = gather_core(planes_a, nw)
        planes_b = gather_xy(after(mine_b, *bufs_a), nw)
        xh, q, k, v, p, att, vec, b1 = attn_fwd(geo, me, tokens, pb, bufs_a)
        planes_b = lax.optimization_barrier((*planes_b, att))[:-1]
        bufs_b = gather_core(planes_b, nw)
        out, dx1, da, gv2, gb1, keep_b, send_b = mlp(geo, me, live, tokens, cotangent, att, bufs_b, vec, b1)
        sums_b = sum_core(keep_b, swap(send_b, "win", nw, 1), nw)
        parts_b = swap_xy(sums_b, nw)
        da = after(da, *sums_b)
        dc, _, keep_a, send_a = attn_bwd(geo, me, q, k, v, p, da, xh, vec, gv2, gb1, place, bufs_a)
        *parts_b, send_a = lax.optimization_barrier((*parts_b, send_a))
        low_b = sum_xy(parts_b)
        sums_a = sum_core(keep_a, swap(send_a, "win", nw, 1), nw)
        parts_a = swap_xy(sums_a, nw)
        own_b = swap_z(low_b, nz)
        dc = after(dc, *sums_a)
        grad_tokens = input_bwd(geo, me, tokens, dc, dx1, vec, bufs_a)
        parts_a = lax.optimization_barrier((*parts_a, grad_tokens))[:-1]
        low_a = sum_xy(parts_a)
        tail = low_a[:, geo.rows_a :].reshape(nz * EXTRA, TL)
        own_a = [swap(jnp.concatenate([low_a[e], tail], 0), "fsdp", nz, e) for e in range(1, nz)]
        grad_qkv, grad_proj, grad_one, grad_two, grad_vectors, grad_bias, grad_table = finish(
            geo, nw, nz, me, low_a, low_b, own_b, own_a
        )
        grad_bias = grad_bias.reshape(-1)
    else:
        geo = Geometry(1, 1)
        me = jnp.zeros((2,), jnp.int32)

        def full(w):
            return lax.all_gather(lax.all_gather(w, "fsdp", axis=1, tiled=True), "win", axis=0, tiled=True)

        bufs_a = [slabs(full(w_qkv))[None]]
        bufs_b = [jnp.concatenate([slabs(full(w)) for w in (w_proj, w_fc1, w_fc2)], 0)[None]]
        vec = lax.all_gather(vectors, both, axis=1, tiled=True)
        b1 = lax.all_gather(fc1_bias, both, axis=0, tiled=True).reshape(1, -1)
        pb = bias(table, place)
        xh, q, k, v, p, att = attn_fwd(geo, me, tokens, pb, bufs_a, vec)
        out, dx1, da, gv2, gb1, gw = mlp(geo, me, live, tokens, cotangent, att, bufs_b, vec, b1)
        dc, small, gq = attn_bwd(geo, me, q, k, v, p, da, xh, vec, gv2, gb1, place, bufs_a)
        grad_tokens = input_bwd(geo, me, tokens, dc, dx1, vec, bufs_a)

        def down(g):
            g = lax.psum_scatter(g.astype(bf16), "win", scatter_dimension=0, tiled=True)
            return lax.psum_scatter(g, "fsdp", scatter_dimension=1, tiled=True).astype(f32)

        grad_qkv = down(unslab(gq[0, 0], geo.cq))
        grad_proj, grad_one, grad_two = [down(g) for g in split_b(geo, gw[0, 0])]
        small = lax.psum(small, both)
        grad_vectors = lax.dynamic_slice_in_dim(small[:8], dev * own, own, 1)
        grad_bias = lax.dynamic_slice_in_dim(small[8:, TT:].reshape(FF), dev * own1, own1, 0)
        grad_table = small[8:, :TABLE].T
    return out, grad_tokens, grad_vectors, grad_bias, grad_qkv, grad_proj, grad_one, grad_two, grad_table


def solution(mesh):
    split = P(("fsdp", "win"), None, None)
    vecs = P(None, ("fsdp", "win"))
    flat = P(("fsdp", "win"))
    cut = P("win", "fsdp")
    return jax.shard_map(
        functools.partial(body, mesh.shape["win"], mesh.shape["fsdp"]),
        mesh=mesh,
        in_specs=(split, flat, vecs, flat, cut, cut, cut, cut, P(), split),
        out_specs=(split, split, vecs, flat, cut, cut, cut, cut, P()),
        check_vma=False,
    )
```

```python
import functools

import jax
import jax.numpy as jnp
import numpy as np
from jax import lax
from jax.experimental import pallas as pl
from jax.experimental.pallas import tpu as pltpu
from jax.sharding import PartitionSpec as P

f32 = jnp.float32
bf16 = jnp.bfloat16
HEADS = 16
HD = 32
WS = 10
WT = WS * WS
D = HEADS * HD
FF = 4 * D
SIDE = 2 * WS - 1
TABLE = SIDE * SIDE
TP = 112
TL = 128
TT = 384
GH = 4
NG = HEADS // GH
EPS = 1e-5
SCALE = HD**-0.5
EXTRA = 32
NN = (((1,), (0,)), ((), ()))
NT = (((1,), (1,)), ((), ()))
TN = (((0,), (0,)), ((), ()))


def dot(a, b, dims=NN):
    return lax.dot_general(a, b, dims, preferred_element_type=f32)


def params(mib):
    return pltpu.CompilerParams(dimension_semantics=("arbitrary",), vmem_limit_bytes=mib * 2**20)


def cost(us):
    return pl.CostEstimate(flops=int(us * 1.1e9), bytes_accessed=int(us * 1e6), transcendentals=0)


def whole(shape):
    n = len(shape)
    return pl.BlockSpec(shape, lambda *a: (0,) * n, pipeline_mode=pl.Buffered(1))


def smem():
    return pl.BlockSpec(memory_space=pltpu.SMEM)


def anyspace():
    return pl.BlockSpec(memory_space=pl.ANY)


def three(x):
    hi = x.astype(bf16)
    rest = x - hi.astype(f32)
    mid = rest.astype(bf16)
    return hi, mid, (rest - mid.astype(f32)).astype(bf16)


def offset_place():
    cj = np.arange(WS)[:, None, None]
    r = np.arange(TT)[None, :, None]
    l = np.arange(256)[None, None, :]
    hit = (l < SIDE * WS) & (r == (l // WS) * SIDE + (l % WS) - cj + WS - 1)
    return jnp.asarray(hit, bf16)


class Geometry:
    def __init__(self, nw, nz):
        self.nw, self.nz = nw, nz
        self.r = D // nw
        self.cq, self.cp, self.c1 = 3 * D // nz // TL, D // nz // TL, FF // nz // TL
        self.r2 = FF // nw
        self.rows_a = self.cq * self.r
        self.blocks = self.c1 + 5 * self.cp
        self.cores = 2 if nw > 1 else 1


def slabs(x):
    return jnp.concatenate([x[:, i : i + TL] for i in range(0, x.shape[1], TL)], 0)


def pack_body(count, *refs):
    srcs, out = refs[:count], refs[count]
    rest = refs[count + 1 :]
    stage, flat, sem = rest[:count], rest[-2], rest[-1]
    moves = [pltpu.make_async_copy(x, y, sem.at[i]) for i, (x, y) in enumerate(zip(srcs, stage))]
    for m in moves:
        m.start()
    parts = []
    r = flat.shape[-2]
    at = 0
    for m, w in zip(moves, stage):
        m.wait()
        if w.dtype == f32:
            part = [p.astype(f32) for p in three(w[...])]
            parts += [jnp.concatenate([p, jnp.zeros((p.shape[0], TL - p.shape[1]), f32)], 1) for p in part]
            continue
        for i in range(0, w.shape[1], TL):
            if len(flat.shape) == 2:
                flat[at : at + w.shape[0], :] = w[:, i : i + TL]
                at += w.shape[0]
                continue
            for k in range(0, w.shape[0], r):
                flat[at] = w[k : k + r, i : i + TL]
                at += 1
    if parts:
        used = sum(p.shape[0] for p in parts)
        flat[at : at + EXTRA, :] = jnp.concatenate(parts + [jnp.zeros((EXTRA - used, TL), f32)], 0).astype(bf16)
    last = pltpu.make_async_copy(flat, out, sem.at[count])
    last.start()
    last.wait()


def pack(shape, *arrays):
    V = pltpu.VMEM
    return pl.pallas_call(
        functools.partial(pack_body, len(arrays)),
        in_specs=[anyspace()] * len(arrays),
        out_specs=anyspace(),
        out_shape=jax.ShapeDtypeStruct(shape, bf16),
        scratch_shapes=[V(x.shape, x.dtype) for x in arrays]
        + [V(shape, bf16), pltpu.SemaphoreType.DMA((len(arrays) + 1,))],
        compiler_params=pltpu.CompilerParams(vmem_limit_bytes=60 * 2**20),
        cost_estimate=cost(2),
        name="pack",
    )(*arrays)


def copies_a(geo, bufs, me, wq, sem):
    out = []
    for d in range(geo.nw):
        row = pl.multiple_of((me[0] ^ d) * geo.r, geo.r)
        for e in range(geo.nz):
            col = (me[1] ^ e) * geo.cq
            for i in range(geo.cq):
                out.append(
                    pltpu.make_async_copy(
                        bufs[d].at[e, pl.ds(i * geo.r, geo.r), :],
                        wq.at[col + i, pl.ds(row, geo.r), :],
                        sem,
                    )
                )
    return out


def copies_b(geo, bufs, me, wp, w1, w2, sem):
    out = []
    for d in range(geo.nw):
        w = me[0] ^ d
        row = pl.multiple_of(w * geo.r, geo.r)
        for e in range(geo.nz):
            z = me[1] ^ e
            for ref, at, n in ((wp, 0, geo.cp), (w1, geo.cp, geo.c1)):
                src = bufs[d].at[e, pl.ds(at, n)]
                out.append(pltpu.make_async_copy(src, ref.at[pl.ds(z * n, n), pl.ds(row, geo.r), :], sem))
            for i in range(geo.cp):
                src = bufs[d].at[e, pl.ds(geo.cp + geo.c1 + 4 * i, 4)]
                out.append(pltpu.make_async_copy(src, w2.at[z * geo.cp + i, pl.ds(w * 4, 4)], sem))
    return out


def wide(ref, lo, n):
    return jnp.concatenate([ref[lo + i] for i in range(n)], 1)


def strided(ref, first, count, step):
    return jnp.concatenate([ref[half, pl.ds(first, count, stride=step), :] for half in range(2)], 1)


def bias_body(table, place, pb_o, zs):
    parts = jnp.concatenate([p for p in three(table[...])], 0)
    for cj in range(WS):
        z = dot(parts, place[cj])
        z = z[:HEADS] + z[HEADS : 2 * HEADS] + z[2 * HEADS :]
        for half in range(2):
            zs[half, cj * HEADS : (cj + 1) * HEADS, :] = z[:, half * TL : (half + 1) * TL]
    for j in range(NG):
        pb_o[j, WT:TP, :] = jnp.zeros((TP - WT, GH * TL), f32)
        for h in range(GH):
            zh = strided(zs, j * GH + h, WS, HEADS)
            for rj in range(WS):
                off = (WS - 1 - rj) * WS
                part = zh if off == 0 else pltpu.roll(zh, 256 - off, 1)
                pb_o[j, rj * WS : (rj + 1) * WS, h * TL : (h + 1) * TL] = jnp.exp(part[:, :TL])


def bias(table, place):
    return pl.pallas_call(
        bias_body,
        out_shape=jax.ShapeDtypeStruct((NG, TP, GH * TL), f32),
        scratch_shapes=[pltpu.VMEM((2, WS * HEADS, TL), f32)],
        compiler_params=pltpu.CompilerParams(vmem_limit_bytes=24 * 2**20),
        cost_estimate=cost(4),
        name="position_bias",
    )(table, place)


def table_sum(gt, place, rs):
    for j in range(NG):
        for h in range(GH):
            total = None
            for rj in range(WS):
                part = gt[j, rj * WS : (rj + 1) * WS, h * TL : (h + 1) * TL]
                part = jnp.concatenate([part, jnp.zeros((WS, TL), f32)], 1)
                off = (WS - 1 - rj) * WS
                part = part if off == 0 else pltpu.roll(part, off, 1)
                total = part if total is None else total + part
            base = (j * GH + h) * 16
            for half in range(2):
                rs[half, base : base + WS, :] = total[:, half * TL : (half + 1) * TL]
    columns = jnp.concatenate([strided(rs, cj, HEADS, 16) for cj in range(WS)], 1)
    z = dot(jnp.concatenate(three(columns), 0), jnp.concatenate([place[cj] for cj in range(WS)], 1), NT)
    return z[:HEADS] + z[HEADS : 2 * HEADS] + z[2 * HEADS :]


def norm(x):
    mean = jnp.sum(x, -1, keepdims=True) * (1.0 / D)
    c = x - mean
    var = jnp.sum(c * c, -1, keepdims=True) * (1.0 / D)
    r = lax.rsqrt(var + EPS)
    return c * r, r


def norm_back(dn, xhat, r, gain):
    t = dn * gain
    m1 = jnp.sum(t, -1, keepdims=True) * (1.0 / D)
    m2 = jnp.sum(t * xhat, -1, keepdims=True) * (1.0 / D)
    return (t - m1 - xhat * m2) * r


def spread(part):
    lane = lax.broadcasted_iota(jnp.int32, (1, TL), 1) // HD
    none = jnp.zeros((TL - TP, TL), part.dtype)
    return jnp.concatenate([x for h in range(GH) for x in (jnp.where(lane == h, part, jnp.zeros_like(part)), none)], 0)


def diag_t(full):
    return jnp.concatenate([full[h * HD : (h + 1) * HD, h * TL : (h + 1) * TL] for h in range(GH)], 0)


def gather_vectors(bufs, geo, me, vec_o, b1_o, tmp):
    own = D // (geo.nw * geo.nz)
    own1 = FF // (geo.nw * geo.nz)
    i32 = jnp.int32
    pick = (lax.broadcasted_iota(i32, (TL, D), 0) == lax.broadcasted_iota(i32, (TL, D), 1) % own).astype(bf16)
    pick1 = (lax.broadcasted_iota(i32, (TL, FF), 0) == lax.broadcasted_iota(i32, (TL, FF), 1) % own1).astype(bf16)
    slot = lax.broadcasted_iota(i32, (1, D), 1) // own
    slot1 = lax.broadcasted_iota(i32, (1, FF), 1) // own1
    vec = jnp.zeros((8, D), f32)
    b1 = jnp.zeros((8, FF), f32)
    for d in range(geo.nw):
        for e in range(geo.nz):
            dev = (me[1] ^ e) * geo.nw + (me[0] ^ d)
            x = tmp[d, e]
            y = dot(x[:24], pick)
            vec = vec + jnp.where(slot == dev, y[:8] + y[8:16] + y[16:24], 0.0)
            y1 = dot(x[24:], pick1)
            b1 = b1 + jnp.where(slot1 == dev, y1, 0.0)
    vec_o[...] = vec
    b1_o[...] = b1[0:1] + b1[1:2] + b1[2:3]


def attn_fwd_body(geo, G, vectors_in, *refs):
    nb = geo.nw
    me, tok, pb = refs[:3]
    bufs = refs[3 : 3 + nb]
    refs = refs[3 + nb :]
    if vectors_in:
        vec, refs = refs[0], refs[1:]
    n1_o, q_o, k_o, v_o, p_o, a_o = refs[:6]
    refs = refs[6:]
    if not vectors_in:
        vec, b1_o = refs[:2]
        refs = refs[2:]
    xs, wq, tmp, sem, sem2 = refs

    @pl.when(pl.program_id(0) == 0)
    def _():
        moves = copies_a(geo, bufs, me, wq, sem)
        for m in moves:
            m.start()
        if not vectors_in:
            small = [
                pltpu.make_async_copy(bufs[d].at[:, pl.ds(geo.rows_a, EXTRA), :], tmp.at[d], sem2)
                for d in range(geo.nw)
            ]
            for m in small:
                m.start()
        xs[...] = jnp.zeros_like(xs)
        if not vectors_in:
            for m in small:
                m.wait()
            gather_vectors(bufs, geo, me, vec, b1_o, tmp)
        for m in moves:
            m.wait()

    for g in range(G):
        xs[g * TP : g * TP + WT, :] = tok[g].astype(f32)
        xs[g * TP + WT : (g + 1) * TP, :] = tok[g, : TP - WT, :].astype(f32)
    xhat, _ = norm(xs[...])
    n1 = (xhat * vec[0:1, :] + vec[1:2, :]).astype(bf16)
    n1_o[...] = xhat.astype(bf16)
    q_o[...] = ((dot(n1, wide(wq, 0, NG)) + vec[2:3, :]) * SCALE).astype(bf16)
    k_o[...] = dot(n1, wide(wq, NG, NG)).astype(bf16)
    v_o[...] = (dot(n1, wide(wq, 2 * NG, NG)) + vec[3:4, :]).astype(bf16)

    def window(g, carry):
        rows = pl.ds(pl.multiple_of(g * TP, 16), TP)
        cols = [slice(j * TL, (j + 1) * TL) for j in range(NG)]
        ks = [k_o[rows, c] for c in cols]
        vs = [v_o[rows, c] for c in cols]
        qs = [spread(q_o[rows, c]) for c in cols]
        scores = [dot(ks[j], qs[j], NT) for j in range(NG)]
        ps, outs = [], []
        for j in range(NG):
            s = scores[j]
            e = jnp.exp(s - jnp.max(s, 0, keepdims=True)) * pb[j]
            p = (e * (1.0 / jnp.sum(e, 0, keepdims=True))).astype(bf16)
            ps.append(p)
            outs.append(diag_t(dot(vs[j], p, TN)).T[:TP].astype(bf16))
        for j in range(NG):
            p_o[g, j] = ps[j]
            a_o[rows, cols[j]] = outs[j]
        return carry

    lax.fori_loop(0, G, window, 0, unroll=G)


def attn_fwd(geo, me, tok, pb, bufs, vec=None, G=4):
    B = tok.shape[0]
    R = B * TP
    S = jax.ShapeDtypeStruct
    act = S((R, D), bf16)
    blk = pl.BlockSpec((G * TP, D), lambda i: (i, 0))
    given = [] if vec is None else [vec]
    out_specs = [blk, blk, blk, blk, pl.BlockSpec((G, NG, TP, GH * TL), lambda i: (i, 0, 0, 0)), blk]
    out_shape = [act, act, act, act, S((B, NG, TP, GH * TL), bf16), act]
    if vec is None:
        out_specs += [whole((8, D)), whole((1, FF))]
        out_shape += [S((8, D), f32), S((1, FF), f32)]
    return pl.pallas_call(
        functools.partial(attn_fwd_body, geo, G, vec is not None),
        grid=(B // G,),
        in_specs=[smem(), pl.BlockSpec((G, WT, D), lambda i: (i, 0, 0)), whole(pb.shape)]
        + [anyspace()] * len(bufs)
        + [whole(g.shape) for g in given],
        out_specs=out_specs,
        out_shape=out_shape,
        scratch_shapes=[
            pltpu.VMEM((G * TP, D), f32),
            pltpu.VMEM((3 * NG, D, TL), bf16),
            pltpu.VMEM((geo.nw, geo.nz, EXTRA, TL), bf16),
            pltpu.SemaphoreType.DMA,
            pltpu.SemaphoreType.DMA,
        ],
        compiler_params=params(28),
        cost_estimate=cost(30),
        name="attn_fwd",
    )(me, tok, pb, *bufs, *given)


GC = 0.7978845608028654
GA = 0.044715


def gelu_both(u):
    u2 = u * u
    t = jnp.tanh(u * (GC + (GC * GA) * u2))
    h = 0.5 + 0.5 * t
    act = u * h
    slope = h + (act * (2.0 - 2.0 * h)) * (GC + (3.0 * GC * GA) * u2)
    return act, slope


def scatter_out(geo, me, blocks, outs):
    cores = geo.cores
    for c in range(cores):
        for xy in range(geo.nw // cores):
            w = me[0] ^ (xy * cores + c)
            for e in range(geo.nz):
                z = me[1] ^ e
                at = 0
                for ref, pick in blocks:
                    for part in pick(ref, w, z):
                        outs[c * (geo.nw // cores) + xy][e, at : at + part.shape[0], :] = part.astype(bf16)
                        at += part.shape[0]


def mlp_body(geo, G, FC, *refs):
    nb = geo.nw
    me, live, tok, cot, attn = refs[:5]
    bufs = refs[5 : 5 + nb]
    vec, b1 = refs[5 + nb : 7 + nb]
    refs = refs[7 + nb :]
    out_o, dx1_o, da_o, gv_o, gb1_o = refs[:5]
    outs = refs[5 : 5 + geo.nw]
    xs, dys, gp, g1, g2, gv, gb1, acc, dn2, wp, w1, w2, sem = refs[5 + geo.nw :]
    i = pl.program_id(0)
    n = pl.num_programs(0)

    @pl.when(i == 0)
    def _():
        moves = copies_b(geo, bufs, me, wp, w1, w2, sem)
        for m in moves:
            m.start()
        for ref in (xs, dys, gp, g1, g2, gv, gb1):
            ref[...] = jnp.zeros_like(ref)
        for m in moves:
            m.wait()

    for g in range(G):
        xs[g * TP : g * TP + WT, :] = tok[g].astype(f32)
        mask = (i * G + g < live[0]).astype(f32)
        dys[g * TP : g * TP + WT, :] = cot[g].astype(f32) * mask
    at = attn[...]
    wpv = wide(wp, 0, NG)
    x1 = xs[...] + dot(at, wpv) + vec[4:5, :]
    acc[...] = x1 + vec[7:8, :]
    xhat, r = norm(x1)
    n2 = (xhat * vec[5:6, :] + vec[6:7, :]).astype(bf16)
    n2t = n2.T
    dyf = dys[...]
    dy = dyf.astype(bf16)
    dyt = dy.T
    ns = FC // TL
    n = FF // FC

    def first(c):
        cols = slice(c * FC, (c + 1) * FC)
        w1c = wide(w1, c * ns, ns)
        w2c = jnp.concatenate([w2[z, cols.start // geo.r : cols.stop // geo.r].reshape(FC, TL) for z in range(NG)], 1)
        return w1c, w2c, dot(n2, w1c), dot(dy, w2c, NT)

    def last(c):
        cols = slice(c * FC, (c + 1) * FC)
        w1c, w2c = work[c][:2]
        a, du = mids[c]
        acc[...] += dot(a, w2c)
        t2 = dot(dyt, a)
        t1 = dot(n2t, du)
        for k in range(ns):
            g2[c * ns + k] += t2[:, k * TL : (k + 1) * TL]
            g1[c * ns + k] += t1[:, k * TL : (k + 1) * TL]
        gb1[:, cols] += jnp.sum(du.astype(f32), 0, keepdims=True)
        d = dot(du, w1c, NT)
        if c == 0:
            dn2[...] = d
        else:
            dn2[...] += d

    work = [first(c) for c in range(1)]
    mids = []
    for c in range(n + 1):
        if c + 1 < n:
            work.append(first(c + 1))
        if c < n:
            a, ga = gelu_both(work[c][2] + b1[:, c * FC : (c + 1) * FC])
            mids.append((a.astype(bf16), (work[c][3] * ga).astype(bf16)))
        if c >= 1:
            last(c - 1)
    n = pl.num_programs(0)
    for g in range(G):
        mask = (i * G + g < live[0]).astype(f32)
        out_o[g] = (acc[g * TP : g * TP + WT, :] * mask).astype(bf16)
    dn = dn2[...]
    gv[7:8, :] += jnp.sum(dyf, 0, keepdims=True)
    gv[5:6, :] += jnp.sum(dn * xhat, 0, keepdims=True)
    gv[6:7, :] += jnp.sum(dn, 0, keepdims=True)
    dx1 = dyf + norm_back(dn, xhat, r, vec[5:6, :])
    dx1_o[...] = dx1
    dl = dx1.astype(bf16)
    gv[4:5, :] += jnp.sum(dl.astype(f32), 0, keepdims=True)
    tp = dot(at.T, dl)
    for k in range(NG):
        gp[k] += tp[:, k * TL : (k + 1) * TL]
    da_o[...] = dot(dl, wpv, NT).astype(bf16)

    @pl.when(i == n - 1)
    def _():
        gv_o[...] = gv[...]
        gb1_o[...] = gb1[...]

        def rows(ref, n):
            def pick(ref, w, z):
                at = pl.multiple_of(w * geo.r, geo.r)
                return [ref[z * n + k, pl.ds(at, geo.r), :] for k in range(n)]

            return ref, pick

        def turned(ref, w, z):
            n, r = geo.r2 // TL, D // geo.nz
            at = pl.multiple_of(z * r, r)
            return [ref[w * n + k, pl.ds(at, r), :] for k in range(n)]

        scatter_out(geo, me, [rows(gp, geo.cp), rows(g1, geo.c1), (g2, turned)], outs)


def mlp(geo, me, live, tok, cot, attn, bufs, vec, b1, G=4, FC=512):
    B = tok.shape[0]
    R = B * TP
    M = G * TP
    blk = pl.BlockSpec((M, D), lambda i: (i, 0))
    win = pl.BlockSpec((G, WT, D), lambda i: (i, 0, 0))
    S = jax.ShapeDtypeStruct
    gshape = (geo.nz, geo.blocks * geo.r, TL)
    V = pltpu.VMEM
    return pl.pallas_call(
        functools.partial(mlp_body, geo, G, FC),
        grid=(B // G,),
        in_specs=[smem(), smem(), win, win, blk] + [anyspace()] * len(bufs) + [whole(vec.shape), whole(b1.shape)],
        out_specs=[win, blk, blk, whole((8, D)), whole((1, FF))] + [whole(gshape)] * geo.nw,
        out_shape=[S(tok.shape, bf16), S((R, D), f32), S((R, D), bf16), S((8, D), f32), S((1, FF), f32)]
        + [S(gshape, bf16)] * geo.nw,
        scratch_shapes=[
            V((M, D), f32),
            V((M, D), f32),
            V((NG, D, TL), f32),
            V((FF // TL, D, TL), f32),
            V((FF // TL, D, TL), f32),
            V((8, D), f32),
            V((1, FF), f32),
            V((M, D), f32),
            V((M, D), f32),
            V((NG, D, TL), bf16),
            V((FF // TL, D, TL), bf16),
            V((NG, FF // geo.r, geo.r, TL), bf16),
            pltpu.SemaphoreType.DMA,
        ],
        compiler_params=params(36),
        cost_estimate=cost(44),
        name="mlp",
    )(me, live, tok, cot, attn, *bufs, vec, b1)


def attn_bwd_body(geo, G, *refs):
    nb = geo.nw
    me, q, k, v, p, da, xh, vec, gv2, gb1, place = refs[:11]
    bufs = refs[11 : 11 + nb]
    refs = refs[11 + nb :]
    dc_o, small_o = refs[:2]
    outs = refs[2 : 2 + geo.nw]
    gq, gb, gt, wq, rs, ex, sem = refs[2 + geo.nw :]
    i = pl.program_id(0)
    n = pl.num_programs(0)

    @pl.when(i == 0)
    def _():
        for m in copies_a(geo, bufs, me, wq, sem):
            m.start()
        for ref in (gq, gb, gt):
            ref[...] = jnp.zeros_like(ref)
        for m in copies_a(geo, bufs, me, wq, sem):
            m.wait()

    def window(g, carry):
        rows = pl.ds(pl.multiple_of(g * TP, 16), TP)
        cols = [slice(j * TL, (j + 1) * TL) for j in range(NG)]
        ks = [k[rows, c] for c in cols]
        vs = [v[rows, c] for c in cols]
        bqs = [spread(q[rows, c]) for c in cols]
        bas = [spread(da[rows, c]) for c in cols]
        dps = [dot(vs[i], bas[i], NT) for i in range(2)]
        dqs, dks, dvs, dss = [], [], [], []
        pts = []
        for j in range(NG + 1):
            if j + 2 < NG:
                dps.append(dot(vs[j + 2], bas[j + 2], NT))
            if j < NG:
                pts.append(p[g, j])
                pf = pts[j].astype(f32)
                t = pf * dps[j]
                dss.append((t - pf * jnp.sum(t, 0, keepdims=True)).astype(bf16))
            if 0 <= j - 0 < NG:
                i = j - 0
                dvs.append(dot(pts[i], bas[i]).astype(bf16))
            if 0 <= j - 1 < NG:
                i = j - 1
                dks.append(dot(dss[i], bqs[i]).astype(bf16))
                dqs.append((diag_t(dot(ks[i], dss[i], TN)).T[:TP] * SCALE).astype(bf16))
        for j in range(NG):
            gt[j] += dss[j].astype(f32)
            dc_o[rows, j * TL : (j + 1) * TL] = dqs[j]
            dc_o[rows, D + j * TL : D + (j + 1) * TL] = dks[j]
            dc_o[rows, 2 * D + j * TL : 2 * D + (j + 1) * TL] = dvs[j]
        return carry

    lax.fori_loop(0, G, window, 0, unroll=G)
    xt = xh[...].T
    for c in range(3):
        cols = slice(c * D, (c + 1) * D)
        dc = dc_o[:, cols]
        t = dot(xt, dc)
        for s in range(NG):
            gq[c * NG + s] += t[:, s * TL : (s + 1) * TL]
        gb[:, cols] += jnp.sum(dc.astype(f32), 0, keepdims=True)

    @pl.when(i == n - 1)
    def _():
        sums = gb[...]
        g_col = jnp.broadcast_to(vec[0:1, :], (TL, D)).T
        s_col = jnp.broadcast_to(vec[1:2, :], (TL, D)).T
        gain = jnp.zeros((D, TL), f32)
        shift = jnp.zeros((D, TL), f32)
        for s in range(3 * NG):
            part = gq[s]
            w = wq[s].astype(f32)
            total = sums[:, s * TL : (s + 1) * TL]
            gain = gain + part * w
            shift = shift + w * total
            gq[s] = part * g_col + s_col * total
        gain = jnp.sum(gain.T, 0, keepdims=True)
        shift = jnp.sum(shift.T, 0, keepdims=True)
        small_o[0:1, :] = gain
        small_o[1:2, :] = shift
        small_o[2:3, :] = sums[:, :D]
        small_o[3:4, :] = sums[:, 2 * D :]
        small_o[4:8, :] = gv2[4:8, :]
        small_o[8:24, :TT] = table_sum(gt, place, rs)
        for k in range(FF // TL):
            small_o[8 + k : 9 + k, TT:] = gb1[:, k * TL : (k + 1) * TL]

        if nb > 1:
            for z in range(geo.nz):
                ex[z] = extra_rows(geo, small_o, gb1, z)

        def rows(ref, w, z):
            at = pl.multiple_of(w * geo.r, geo.r)
            parts = [ref[z * geo.cq + s, pl.ds(at, geo.r), :] for s in range(geo.cq)]
            return parts if nb == 1 else parts + [ex[z]]

        scatter_out(geo, me, [(gq, rows)], outs)


def extra_rows(geo, small, gb1, z):
    nh = HEADS // geo.nz
    vec = small[0:8, z * TL : (z + 1) * TL]
    first = z * (FF // geo.nz)
    bias = [gb1[:, first + k * TL : first + (k + 1) * TL] for k in range(FF // geo.nz // TL)]
    table = [small[8 + z * nh : 8 + (z + 1) * nh, k * TL : (k + 1) * TL] for k in range(TT // TL)]
    rows = [vec] + bias + table
    used = sum(r.shape[0] for r in rows)
    return jnp.concatenate(rows + [jnp.zeros((EXTRA - used, TL), f32)], 0)


def attn_bwd(geo, me, q, k, v, p, da, xh, vec, gv2, gb1, place, bufs, G=4):
    R = q.shape[0]
    B = R // TP
    blk = pl.BlockSpec((G * TP, D), lambda i: (i, 0))
    S = jax.ShapeDtypeStruct
    V = pltpu.VMEM
    gshape = (geo.nz, geo.rows_a + (EXTRA if geo.cores == 2 else 0), TL)
    return pl.pallas_call(
        functools.partial(attn_bwd_body, geo, G),
        grid=(B // G,),
        in_specs=[smem(), blk, blk, blk, pl.BlockSpec((G, NG, TP, GH * TL), lambda i: (i, 0, 0, 0)), blk, blk]
        + [whole(x.shape) for x in (vec, gv2, gb1, place)]
        + [anyspace()] * len(bufs),
        out_specs=[pl.BlockSpec((G * TP, 3 * D), lambda i: (i, 0)), whole((24, D))] + [whole(gshape)] * geo.nw,
        out_shape=[S((R, 3 * D), bf16), S((24, D), f32)] + [S(gshape, bf16)] * geo.nw,
        scratch_shapes=[
            V((3 * NG, D, TL), f32),
            V((1, 3 * D), f32),
            V((NG, TP, GH * TL), f32),
            V((3 * NG, D, TL), bf16),
            V((2, HEADS * 16, TL), f32),
            V((geo.nz, EXTRA, TL), f32),
            pltpu.SemaphoreType.DMA,
        ],
        compiler_params=params(32),
        cost_estimate=cost(30),
        name="attn_bwd",
    )(me, q, k, v, p, da, xh, vec, gv2, gb1, place, *bufs)


def input_bwd_body(geo, G, *refs):
    nb = geo.nw
    me, tok, dc, dx1, vec = refs[:5]
    bufs = refs[5 : 5 + nb]
    gt_o, xs, wq, sem = refs[5 + nb :]

    @pl.when(pl.program_id(0) == 0)
    def _():
        moves = copies_a(geo, bufs, me, wq, sem)
        for m in moves:
            m.start()
        xs[...] = jnp.zeros_like(xs)
        for m in moves:
            m.wait()

    for g in range(G):
        xs[g * TP : g * TP + WT, :] = tok[g].astype(f32)
    dn = dot(dc[...], wide(wq, 0, 3 * NG), NT)
    xhat, r = norm(xs[...])
    dx = dx1[...] + norm_back(dn, xhat, r, vec[0:1, :])
    for g in range(G):
        gt_o[g] = dx[g * TP : g * TP + WT].astype(bf16)


def input_bwd(geo, me, tok, dc, dx1, vec, bufs, G=4):
    B = tok.shape[0]
    blk = pl.BlockSpec((G * TP, D), lambda i: (i, 0))
    win = pl.BlockSpec((G, WT, D), lambda i: (i, 0, 0))
    S = jax.ShapeDtypeStruct
    V = pltpu.VMEM
    return pl.pallas_call(
        functools.partial(input_bwd_body, geo, G),
        grid=(B // G,),
        in_specs=[smem(), win, pl.BlockSpec((G * TP, 3 * D), lambda i: (i, 0)), blk, whole(vec.shape)]
        + [anyspace()] * len(bufs),
        out_specs=win,
        out_shape=S(tok.shape, bf16),
        scratch_shapes=[V((G * TP, D), f32), V((3 * NG, D, TL), bf16), pltpu.SemaphoreType.DMA],
        compiler_params=params(24),
        cost_estimate=cost(10),
        name="input_bwd",
    )(me, tok, dc, dx1, vec, *bufs)


def finish_body(geo, nz, *refs):
    me, low_a, low_b = refs[:3]
    got_b = refs[3 : 2 + nz]
    got_a = refs[2 + nz : 1 + 2 * nz]
    gq_o, gp_o, g1_o, g2_o, vec_o, b1_o, tab_o, tab = refs[1 + 2 * nz :]
    r, r2 = geo.r, geo.r2
    rows = geo.rows_a + EXTRA

    def total(low, got, lo, n):
        out = low[0, lo : lo + n, :].astype(f32)
        for x in got:
            out = out + x[lo : lo + n, :].astype(f32)
        return out

    for i in range(geo.cq):
        gq_o[:, i * TL : (i + 1) * TL] = total(low_a, got_a, i * r, r)
    at = 0
    for ref, n in ((gp_o, geo.cp), (g1_o, geo.c1)):
        for i in range(n):
            ref[:, i * TL : (i + 1) * TL] = total(low_b, got_b, at, r)
            at += r
    wide_z = D // nz
    for k in range(r2 // TL):
        g2_o[k * TL : (k + 1) * TL, :] = total(low_b, got_b, at, wide_z).T
        at += wide_z
    nb = FF // nz // TL
    small = total(low_a, got_a, geo.rows_a, 16)
    own, own1 = vec_o.shape[1], b1_o.shape[1]
    vec_o[...] = pltpu.roll(small[:8], (TL - me[0] * own) % TL, 1)[:, :own]
    first = me[0] * own1
    b1 = pltpu.roll(small[8 : 8 + nb], (TL - first % TL) % TL, 1)
    row = lax.broadcasted_iota(jnp.int32, b1.shape, 0) == first // TL
    b1_o[...] = jnp.sum(jnp.where(row, b1, 0.0), 0, keepdims=True)[:, :own1]
    nh = HEADS // nz
    lo = 8 + nb
    for e in range(nz):
        t = low_a[e, geo.rows_a : rows, :].astype(f32)
        for d in range(1, nz):
            t = t + got_a[d - 1][rows + (e ^ d) * EXTRA : rows + ((e ^ d) + 1) * EXTRA, :].astype(f32)
        for k in range(TT // TL):
            tab[me[1] ^ e, :, k * TL : (k + 1) * TL] = t[lo + k * nh : lo + (k + 1) * nh]
    full = jnp.concatenate([tab[z] for z in range(nz)], 0)
    tab_o[...] = full[:, :TABLE]


def finish(geo, nw, nz, me, low_a, low_b, got_b, got_a):
    S = jax.ShapeDtypeStruct
    vmem = pl.BlockSpec(memory_space=pltpu.VMEM)
    return pl.pallas_call(
        functools.partial(finish_body, geo, nz),
        in_specs=[smem()] + [vmem] * (2 * nz),
        out_specs=[vmem] * 7,
        out_shape=[
            S((geo.r, geo.cq * TL), f32),
            S((geo.r, geo.cp * TL), f32),
            S((geo.r, geo.c1 * TL), f32),
            S((geo.r2, geo.cp * TL), f32),
            S((8, D // (nw * nz)), f32),
            S((1, FF // (nw * nz)), f32),
            S((HEADS, TABLE), f32),
        ],
        scratch_shapes=[pltpu.VMEM((nz, HEADS // nz, TT), f32)],
        compiler_params=pltpu.CompilerParams(vmem_limit_bytes=12 * 2**20),
        cost_estimate=cost(3),
        name="finish",
    )(me, low_a, low_b, *got_b, *got_a)


def swap(x, axis, size, d):
    return lax.ppermute(x, axis, [(i, i ^ d) for i in range(size)])


def after(x, *deps):
    return lax.optimization_barrier((x, *deps))[0]


def gather_z(buf, nz):
    return jnp.stack([buf] + [swap(buf, "fsdp", nz, e) for e in range(1, nz)])


def gather_xy(mine, nw):
    return [mine] + [swap(mine, "win", nw, 2 * d) for d in range(1, nw // 2)]


def gather_core(planes, nw):
    return [y for x in planes for y in (x, swap(x, "win", nw, 1))]


def sum_core(parts, nw):
    n = nw // 2
    out = [None] * n
    for d in reversed(range(n)):
        out[d] = (parts[d].astype(f32) + swap(parts[n + d], "win", nw, 1).astype(f32)).astype(bf16)
    return out


def swap_xy(sums, nw):
    return [sums[0]] + [swap(sums[d], "win", nw, 2 * d) for d in range(1, nw // 2)]


def sum_xy(parts):
    return functools.reduce(jnp.add, [x.astype(f32) for x in parts]).astype(bf16)


def swap_z(low, nz):
    return [swap(low[e], "fsdp", nz, e) for e in range(1, nz)]


def unslab(x, n):
    r = x.shape[0] // n
    return jnp.concatenate([x[i * r : (i + 1) * r] for i in range(n)], 1)


def split_b(geo, x):
    a, b = geo.cp * geo.r, (geo.cp + geo.c1) * geo.r
    two = x[b:].reshape(geo.r2 // TL, D // geo.nz, TL).transpose(0, 2, 1).reshape(geo.r2, D // geo.nz)
    return unslab(x[:a], geo.cp), unslab(x[a:b], geo.c1), two


def body(nw, nz, tokens, live, vectors, fc1_bias, w_qkv, w_proj, w_fc1, w_fc2, rel_table, cotangent):
    both = ("fsdp", "win")
    fast = D // nz == TL and FF // nw % TL == 0 and D // nw % 16 == 0 and nw > 1 and nz > 1
    fast = fast and nw & (nw - 1) == 0 and nz & (nz - 1) == 0
    place = offset_place()
    table = jnp.pad(rel_table.T, ((0, 0), (0, TT - TABLE)))
    dev = lax.axis_index(both)
    own, own1 = D // (nw * nz), FF // (nw * nz)
    if fast:
        geo = Geometry(nw, nz)
        me = jnp.stack([lax.axis_index("win"), lax.axis_index("fsdp")]).astype(jnp.int32)
        buf_a = pack((geo.rows_a + EXTRA, TL), w_qkv, vectors, fc1_bias.reshape(1, -1))
        buf_b = pack((geo.blocks, geo.r, TL), w_proj, w_fc1, w_fc2)
        mine_a = gather_z(buf_a, nz)
        pb = bias(table, place)
        planes_a = gather_xy(mine_a, nw)
        mine_b = gather_z(after(buf_b, mine_a), nz)
        bufs_a = gather_core(planes_a, nw)
        planes_b = gather_xy(mine_b, nw)
        own_core = swap(planes_b[0], "win", nw, 1)
        xh, q, k, v, p, att, vec, b1 = attn_fwd(geo, me, tokens, pb, bufs_a)
        rest = lax.optimization_barrier((*planes_b[1:], att))[:-1]
        bufs_b = [planes_b[0], own_core] + gather_core(rest, nw)
        out, dx1, da, gv2, gb1, *gw = mlp(geo, me, live, tokens, cotangent, att, bufs_b, vec, b1)
        sums_b = sum_core(gw, nw)
        parts_b = swap_xy(sums_b, nw)
        gv2 = after(gv2, *sums_b)
        dc, _, *gq = attn_bwd(geo, me, q, k, v, p, da, xh, vec, gv2, gb1, place, bufs_a)
        res = lax.optimization_barrier((*parts_b, *gq))
        parts_b, gq = res[: len(parts_b)], res[len(parts_b) :]
        low_b = sum_xy(parts_b)
        sums_a = sum_core(gq, nw)
        parts_a = swap_xy(sums_a, nw)
        own_b = swap_z(low_b, nz)
        grad_tokens = input_bwd(geo, me, tokens, dc, dx1, after(vec, *sums_a), bufs_a)
        parts_a = lax.optimization_barrier((*parts_a, grad_tokens))[:-1]
        low_a = sum_xy(parts_a)
        tail = low_a[:, geo.rows_a :].reshape(nz * EXTRA, TL)
        own_a = [swap(jnp.concatenate([low_a[e], tail], 0), "fsdp", nz, e) for e in range(1, nz)]
        grad_qkv, grad_proj, grad_one, grad_two, grad_vectors, grad_bias, grad_table = finish(
            geo, nw, nz, me, low_a, low_b, own_b, own_a
        )
        grad_bias = grad_bias.reshape(-1)
        grad_table = grad_table.T
    else:
        geo = Geometry(1, 1)
        me = jnp.zeros((2,), jnp.int32)

        def full(w):
            return lax.all_gather(lax.all_gather(w, "fsdp", axis=1, tiled=True), "win", axis=0, tiled=True)

        bufs_a = [slabs(full(w_qkv))[None]]
        bufs_b = [jnp.concatenate([slabs(full(w)) for w in (w_proj, w_fc1, w_fc2)], 0).reshape(1, geo.blocks, D, TL)]
        vec = lax.all_gather(vectors, both, axis=1, tiled=True)
        b1 = lax.all_gather(fc1_bias, both, axis=0, tiled=True).reshape(1, -1)
        pb = bias(table, place)
        xh, q, k, v, p, att = attn_fwd(geo, me, tokens, pb, bufs_a, vec)
        out, dx1, da, gv2, gb1, gw = mlp(geo, me, live, tokens, cotangent, att, bufs_b, vec, b1)
        dc, small, gq = attn_bwd(geo, me, q, k, v, p, da, xh, vec, gv2, gb1, place, bufs_a)
        grad_tokens = input_bwd(geo, me, tokens, dc, dx1, vec, bufs_a)

        def down(g):
            g = lax.psum_scatter(g.astype(bf16), "win", scatter_dimension=0, tiled=True)
            return lax.psum_scatter(g, "fsdp", scatter_dimension=1, tiled=True).astype(f32)

        grad_qkv = down(unslab(gq[0], geo.cq))
        grad_proj, grad_one, grad_two = [down(g) for g in split_b(geo, gw[0])]
        small = lax.psum(small, both)
        grad_vectors = lax.dynamic_slice_in_dim(small[:8], dev * own, own, 1)
        grad_bias = lax.dynamic_slice_in_dim(small[8:, TT:].reshape(FF), dev * own1, own1, 0)
        grad_table = small[8:, :TABLE].T
    return out, grad_tokens, grad_vectors, grad_bias, grad_qkv, grad_proj, grad_one, grad_two, grad_table


def solution(mesh):
    split = P(("fsdp", "win"), None, None)
    vecs = P(None, ("fsdp", "win"))
    flat = P(("fsdp", "win"))
    cut = P("win", "fsdp")
    return jax.shard_map(
        functools.partial(body, mesh.shape["win"], mesh.shape["fsdp"]),
        mesh=mesh,
        in_specs=(split, flat, vecs, flat, cut, cut, cut, cut, P(), split),
        out_specs=(split, split, vecs, flat, cut, cut, cut, cut, P()),
        check_vma=False,
    )
```

```python
import functools

import jax
import jax.numpy as jnp
import numpy as np
from jax import lax
from jax.experimental import pallas as pl
from jax.experimental.pallas import tpu as pltpu
from jax.sharding import PartitionSpec as P

f32 = jnp.float32
bf16 = jnp.bfloat16
HEADS = 16
HD = 32
WS = 10
WT = WS * WS
D = HEADS * HD
FF = 4 * D
SIDE = 2 * WS - 1
TABLE = SIDE * SIDE
TP = 112
TL = 128
TT = 384
GH = 4
NG = HEADS // GH
EPS = 1e-5
SCALE = HD**-0.5
EXTRA = 32
NN = (((1,), (0,)), ((), ()))
NT = (((1,), (1,)), ((), ()))
TN = (((0,), (0,)), ((), ()))


def dot(a, b, dims=NN):
    return lax.dot_general(a, b, dims, preferred_element_type=f32)


def params(mib):
    return pltpu.CompilerParams(dimension_semantics=("arbitrary",), vmem_limit_bytes=mib * 2**20)


def cost(us):
    return pl.CostEstimate(flops=int(us * 1.1e9), bytes_accessed=int(us * 1e6), transcendentals=0)


def whole(shape):
    n = len(shape)
    return pl.BlockSpec(shape, lambda *a: (0,) * n, pipeline_mode=pl.Buffered(1))


def smem():
    return pl.BlockSpec(memory_space=pltpu.SMEM)


def anyspace():
    return pl.BlockSpec(memory_space=pl.ANY)


def three(x):
    hi = x.astype(bf16)
    rest = x - hi.astype(f32)
    mid = rest.astype(bf16)
    return hi, mid, (rest - mid.astype(f32)).astype(bf16)


def offset_place():
    cj = np.arange(WS)[:, None, None]
    r = np.arange(TT)[None, :, None]
    l = np.arange(256)[None, None, :]
    hit = (l < SIDE * WS) & (r == (l // WS) * SIDE + (l % WS) - cj + WS - 1)
    return jnp.asarray(hit, bf16)


class Geometry:
    def __init__(self, nw, nz):
        self.nw, self.nz = nw, nz
        self.r = D // nw
        self.cq, self.cp, self.c1 = 3 * D // nz // TL, D // nz // TL, FF // nz // TL
        self.r2 = FF // nw
        self.rows_a = self.cq * self.r
        self.blocks = self.c1 + 5 * self.cp
        self.cores = 2 if nw > 1 else 1


def slabs(x):
    return jnp.concatenate([x[:, i : i + TL] for i in range(0, x.shape[1], TL)], 0)


def pack_body(count, *refs):
    srcs, out = refs[:count], refs[count]
    rest = refs[count + 1 :]
    stage, flat, sem = rest[:count], rest[-2], rest[-1]
    moves = [pltpu.make_async_copy(x, y, sem.at[i]) for i, (x, y) in enumerate(zip(srcs, stage))]
    for m in moves:
        m.start()
    parts = []
    r = flat.shape[-2]
    at = 0
    for m, w in zip(moves, stage):
        m.wait()
        if w.dtype == f32:
            part = [p.astype(f32) for p in three(w[...])]
            parts += [jnp.concatenate([p, jnp.zeros((p.shape[0], TL - p.shape[1]), f32)], 1) for p in part]
            continue
        for i in range(0, w.shape[1], TL):
            if len(flat.shape) == 2:
                flat[at : at + w.shape[0], :] = w[:, i : i + TL]
                at += w.shape[0]
                continue
            for k in range(0, w.shape[0], r):
                flat[at] = w[k : k + r, i : i + TL]
                at += 1
    if parts:
        used = sum(p.shape[0] for p in parts)
        flat[at : at + EXTRA, :] = jnp.concatenate(parts + [jnp.zeros((EXTRA - used, TL), f32)], 0).astype(bf16)
    last = pltpu.make_async_copy(flat, out, sem.at[count])
    last.start()
    last.wait()


def pack(shape, *arrays):
    V = pltpu.VMEM
    return pl.pallas_call(
        functools.partial(pack_body, len(arrays)),
        in_specs=[anyspace()] * len(arrays),
        out_specs=anyspace(),
        out_shape=jax.ShapeDtypeStruct(shape, bf16),
        scratch_shapes=[V(x.shape, x.dtype) for x in arrays]
        + [V(shape, bf16), pltpu.SemaphoreType.DMA((len(arrays) + 1,))],
        compiler_params=pltpu.CompilerParams(vmem_limit_bytes=60 * 2**20),
        cost_estimate=cost(2),
        name="pack",
    )(*arrays)


def copies_a(geo, bufs, me, wq, sem):
    out = []
    for d in range(geo.nw):
        row = pl.multiple_of((me[0] ^ d) * geo.r, geo.r)
        for e in range(geo.nz):
            col = (me[1] ^ e) * geo.cq
            for i in range(geo.cq):
                out.append(
                    pltpu.make_async_copy(
                        bufs[d].at[e, pl.ds(i * geo.r, geo.r), :],
                        wq.at[col + i, pl.ds(row, geo.r), :],
                        sem,
                    )
                )
    return out


def copies_b(geo, bufs, me, wp, w1, w2, sem):
    out = []
    for d in range(geo.nw):
        w = me[0] ^ d
        row = pl.multiple_of(w * geo.r, geo.r)
        for e in range(geo.nz):
            z = me[1] ^ e
            for ref, at, n in ((wp, 0, geo.cp), (w1, geo.cp, geo.c1)):
                src = bufs[d].at[e, pl.ds(at, n)]
                out.append(pltpu.make_async_copy(src, ref.at[pl.ds(z * n, n), pl.ds(row, geo.r), :], sem))
            for i in range(geo.cp):
                src = bufs[d].at[e, pl.ds(geo.cp + geo.c1 + 4 * i, 4)]
                out.append(pltpu.make_async_copy(src, w2.at[z * geo.cp + i, pl.ds(w * 4, 4)], sem))
    return out


def wide(ref, lo, n):
    return jnp.concatenate([ref[lo + i] for i in range(n)], 1)


def strided(ref, first, count, step):
    return jnp.concatenate([ref[half, pl.ds(first, count, stride=step), :] for half in range(2)], 1)


def bias_body(table, place, pb_o, zs):
    parts = jnp.concatenate([p for p in three(table[...])], 0)
    for cj in range(WS):
        z = dot(parts, place[cj])
        z = z[:HEADS] + z[HEADS : 2 * HEADS] + z[2 * HEADS :]
        for half in range(2):
            zs[half, cj * HEADS : (cj + 1) * HEADS, :] = z[:, half * TL : (half + 1) * TL]
    for j in range(NG):
        pb_o[j, WT:TP, :] = jnp.zeros((TP - WT, GH * TL), f32)
        for h in range(GH):
            zh = strided(zs, j * GH + h, WS, HEADS)
            for rj in range(WS):
                off = (WS - 1 - rj) * WS
                part = zh if off == 0 else pltpu.roll(zh, 256 - off, 1)
                pb_o[j, rj * WS : (rj + 1) * WS, h * TL : (h + 1) * TL] = jnp.exp(part[:, :TL])


def bias(table, place):
    return pl.pallas_call(
        bias_body,
        out_shape=jax.ShapeDtypeStruct((NG, TP, GH * TL), f32),
        scratch_shapes=[pltpu.VMEM((2, WS * HEADS, TL), f32)],
        compiler_params=pltpu.CompilerParams(vmem_limit_bytes=24 * 2**20),
        cost_estimate=cost(4),
        name="position_bias",
    )(table, place)


def table_sum(gt, place, rs):
    for j in range(NG):
        for h in range(GH):
            total = None
            for rj in range(WS):
                part = gt[j, rj * WS : (rj + 1) * WS, h * TL : (h + 1) * TL]
                part = jnp.concatenate([part, jnp.zeros((WS, TL), f32)], 1)
                off = (WS - 1 - rj) * WS
                part = part if off == 0 else pltpu.roll(part, off, 1)
                total = part if total is None else total + part
            base = (j * GH + h) * 16
            for half in range(2):
                rs[half, base : base + WS, :] = total[:, half * TL : (half + 1) * TL]
    columns = jnp.concatenate([strided(rs, cj, HEADS, 16) for cj in range(WS)], 1)
    z = dot(jnp.concatenate(three(columns), 0), jnp.concatenate([place[cj] for cj in range(WS)], 1), NT)
    return z[:HEADS] + z[HEADS : 2 * HEADS] + z[2 * HEADS :]


def norm(x):
    mean = jnp.sum(x, -1, keepdims=True) * (1.0 / D)
    c = x - mean
    var = jnp.sum(c * c, -1, keepdims=True) * (1.0 / D)
    r = lax.rsqrt(var + EPS)
    return c * r, r


def norm_back(dn, xhat, r, gain):
    t = dn * gain
    m1 = jnp.sum(t, -1, keepdims=True) * (1.0 / D)
    m2 = jnp.sum(t * xhat, -1, keepdims=True) * (1.0 / D)
    return (t - m1 - xhat * m2) * r


def spread(part):
    lane = lax.broadcasted_iota(jnp.int32, (1, TL), 1) // HD
    none = jnp.zeros((TL - TP, TL), part.dtype)
    return jnp.concatenate([x for h in range(GH) for x in (jnp.where(lane == h, part, jnp.zeros_like(part)), none)], 0)


def diag_t(full):
    return jnp.concatenate([full[h * HD : (h + 1) * HD, h * TL : (h + 1) * TL] for h in range(GH)], 0)


def gather_vectors(bufs, geo, me, vec_o, b1_o, tmp):
    own = D // (geo.nw * geo.nz)
    own1 = FF // (geo.nw * geo.nz)
    i32 = jnp.int32
    pick = (lax.broadcasted_iota(i32, (TL, D), 0) == lax.broadcasted_iota(i32, (TL, D), 1) % own).astype(bf16)
    pick1 = (lax.broadcasted_iota(i32, (TL, FF), 0) == lax.broadcasted_iota(i32, (TL, FF), 1) % own1).astype(bf16)
    slot = lax.broadcasted_iota(i32, (1, D), 1) // own
    slot1 = lax.broadcasted_iota(i32, (1, FF), 1) // own1
    vec = jnp.zeros((8, D), f32)
    b1 = jnp.zeros((8, FF), f32)
    for d in range(geo.nw):
        for e in range(geo.nz):
            dev = (me[1] ^ e) * geo.nw + (me[0] ^ d)
            x = tmp[d, e]
            y = dot(x[:24], pick)
            vec = vec + jnp.where(slot == dev, y[:8] + y[8:16] + y[16:24], 0.0)
            y1 = dot(x[24:], pick1)
            b1 = b1 + jnp.where(slot1 == dev, y1, 0.0)
    vec_o[...] = vec
    b1_o[...] = b1[0:1] + b1[1:2] + b1[2:3]


def attn_fwd_body(geo, G, vectors_in, *refs):
    nb = geo.nw
    me, tok, pb = refs[:3]
    bufs = refs[3 : 3 + nb]
    refs = refs[3 + nb :]
    if vectors_in:
        vec, refs = refs[0], refs[1:]
    n1_o, q_o, k_o, v_o, p_o, a_o = refs[:6]
    refs = refs[6:]
    if not vectors_in:
        vec, b1_o = refs[:2]
        refs = refs[2:]
    xs, wq, tmp, sem, sem2 = refs

    @pl.when(pl.program_id(0) == 0)
    def _():
        moves = copies_a(geo, bufs, me, wq, sem)
        for m in moves:
            m.start()
        if not vectors_in:
            small = [
                pltpu.make_async_copy(bufs[d].at[:, pl.ds(geo.rows_a, EXTRA), :], tmp.at[d], sem2)
                for d in range(geo.nw)
            ]
            for m in small:
                m.start()
        xs[...] = jnp.zeros_like(xs)
        if not vectors_in:
            for m in small:
                m.wait()
            gather_vectors(bufs, geo, me, vec, b1_o, tmp)
        for m in moves:
            m.wait()

    for g in range(G):
        xs[g * TP : g * TP + WT, :] = tok[g].astype(f32)
        xs[g * TP + WT : (g + 1) * TP, :] = tok[g, : TP - WT, :].astype(f32)
    xhat, _ = norm(xs[...])
    n1 = (xhat * vec[0:1, :] + vec[1:2, :]).astype(bf16)
    n1_o[...] = xhat.astype(bf16)
    q_o[...] = ((dot(n1, wide(wq, 0, NG)) + vec[2:3, :]) * SCALE).astype(bf16)
    k_o[...] = dot(n1, wide(wq, NG, NG)).astype(bf16)
    v_o[...] = (dot(n1, wide(wq, 2 * NG, NG)) + vec[3:4, :]).astype(bf16)

    def window(g, carry):
        rows = pl.ds(pl.multiple_of(g * TP, 16), TP)
        cols = [slice(j * TL, (j + 1) * TL) for j in range(NG)]
        ks = [k_o[rows, c] for c in cols]
        vs = [v_o[rows, c] for c in cols]
        qs = [spread(q_o[rows, c]) for c in cols]
        scores = [dot(ks[j], qs[j], NT) for j in range(NG)]
        ps, outs = [], []
        for j in range(NG):
            s = scores[j]
            e = jnp.exp(s - jnp.max(s, 0, keepdims=True)) * pb[j]
            p = (e * (1.0 / jnp.sum(e, 0, keepdims=True))).astype(bf16)
            ps.append(p)
            outs.append(diag_t(dot(vs[j], p, TN)).T[:TP].astype(bf16))
        for j in range(NG):
            p_o[g, j] = ps[j]
            a_o[rows, cols[j]] = outs[j]
        return carry

    lax.fori_loop(0, G, window, 0, unroll=G)


def attn_fwd(geo, me, tok, pb, bufs, vec=None, G=4):
    B = tok.shape[0]
    R = B * TP
    S = jax.ShapeDtypeStruct
    act = S((R, D), bf16)
    blk = pl.BlockSpec((G * TP, D), lambda i: (i, 0))
    given = [] if vec is None else [vec]
    out_specs = [blk, blk, blk, blk, pl.BlockSpec((G, NG, TP, GH * TL), lambda i: (i, 0, 0, 0)), blk]
    out_shape = [act, act, act, act, S((B, NG, TP, GH * TL), bf16), act]
    if vec is None:
        out_specs += [whole((8, D)), whole((1, FF))]
        out_shape += [S((8, D), f32), S((1, FF), f32)]
    return pl.pallas_call(
        functools.partial(attn_fwd_body, geo, G, vec is not None),
        grid=(B // G,),
        in_specs=[smem(), pl.BlockSpec((G, WT, D), lambda i: (i, 0, 0)), whole(pb.shape)]
        + [anyspace()] * len(bufs)
        + [whole(g.shape) for g in given],
        out_specs=out_specs,
        out_shape=out_shape,
        scratch_shapes=[
            pltpu.VMEM((G * TP, D), f32),
            pltpu.VMEM((3 * NG, D, TL), bf16),
            pltpu.VMEM((geo.nw, geo.nz, EXTRA, TL), bf16),
            pltpu.SemaphoreType.DMA,
            pltpu.SemaphoreType.DMA,
        ],
        compiler_params=params(28),
        cost_estimate=cost(30),
        name="attn_fwd",
    )(me, tok, pb, *bufs, *given)


GC = 0.7978845608028654
GA = 0.044715


def gelu_both(u):
    u2 = u * u
    t = jnp.tanh(u * (GC + (GC * GA) * u2))
    h = 0.5 + 0.5 * t
    act = u * h
    slope = h + (act * (2.0 - 2.0 * h)) * (GC + (3.0 * GC * GA) * u2)
    return act, slope


def scatter_out(geo, me, blocks, outs):
    cores = geo.cores
    for c in range(cores):
        for xy in range(geo.nw // cores):
            w = me[0] ^ (xy * cores + c)
            for e in range(geo.nz):
                z = me[1] ^ e
                at = 0
                for ref, pick in blocks:
                    for part in pick(ref, w, z):
                        outs[c * (geo.nw // cores) + xy][e, at : at + part.shape[0], :] = part.astype(bf16)
                        at += part.shape[0]


def mlp_body(geo, G, FC, *refs):
    nb = geo.nw
    me, live, tok, cot, attn = refs[:5]
    bufs = refs[5 : 5 + nb]
    vec, b1 = refs[5 + nb : 7 + nb]
    refs = refs[7 + nb :]
    out_o, dx1_o, da_o, gv_o, gb1_o = refs[:5]
    outs = refs[5 : 5 + geo.nw]
    xs, dys, gp, g1, g2, gv, gb1, acc, dn2, wp, w1, w2, sem = refs[5 + geo.nw :]
    i = pl.program_id(0)
    n = pl.num_programs(0)

    @pl.when(i == 0)
    def _():
        moves = copies_b(geo, bufs, me, wp, w1, w2, sem)
        for m in moves:
            m.start()
        for ref in (xs, dys, gp, g1, g2, gv, gb1):
            ref[...] = jnp.zeros_like(ref)
        for m in moves:
            m.wait()

    for g in range(G):
        xs[g * TP : g * TP + WT, :] = tok[g].astype(f32)
        mask = (i * G + g < live[0]).astype(f32)
        dys[g * TP : g * TP + WT, :] = cot[g].astype(f32) * mask
    at = attn[...]
    wpv = wide(wp, 0, NG)
    x1 = xs[...] + dot(at, wpv) + vec[4:5, :]
    acc[...] = x1 + vec[7:8, :]
    xhat, r = norm(x1)
    n2 = (xhat * vec[5:6, :] + vec[6:7, :]).astype(bf16)
    n2t = n2.T
    dyf = dys[...]
    dy = dyf.astype(bf16)
    dyt = dy.T
    ns = FC // TL
    n = FF // FC

    def first(c):
        cols = slice(c * FC, (c + 1) * FC)
        w1c = wide(w1, c * ns, ns)
        w2c = jnp.concatenate([w2[z, cols.start // geo.r : cols.stop // geo.r].reshape(FC, TL) for z in range(NG)], 1)
        return w1c, w2c, dot(n2, w1c), dot(dy, w2c, NT)

    def last(c):
        cols = slice(c * FC, (c + 1) * FC)
        w1c, w2c = work[c][:2]
        a, du = mids[c]
        acc[...] += dot(a, w2c)
        t2 = dot(dyt, a)
        t1 = dot(n2t, du)
        for k in range(ns):
            g2[c * ns + k] += t2[:, k * TL : (k + 1) * TL]
            g1[c * ns + k] += t1[:, k * TL : (k + 1) * TL]
        gb1[:, cols] += jnp.sum(du.astype(f32), 0, keepdims=True)
        d = dot(du, w1c, NT)
        if c == 0:
            dn2[...] = d
        else:
            dn2[...] += d

    work = [first(c) for c in range(1)]
    mids = []
    for c in range(n + 1):
        if c + 1 < n:
            work.append(first(c + 1))
        if c < n:
            a, ga = gelu_both(work[c][2] + b1[:, c * FC : (c + 1) * FC])
            mids.append((a.astype(bf16), (work[c][3] * ga).astype(bf16)))
        if c >= 1:
            last(c - 1)
    n = pl.num_programs(0)
    for g in range(G):
        mask = (i * G + g < live[0]).astype(f32)
        out_o[g] = (acc[g * TP : g * TP + WT, :] * mask).astype(bf16)
    dn = dn2[...]
    gv[7:8, :] += jnp.sum(dyf, 0, keepdims=True)
    gv[5:6, :] += jnp.sum(dn * xhat, 0, keepdims=True)
    gv[6:7, :] += jnp.sum(dn, 0, keepdims=True)
    dx1 = dyf + norm_back(dn, xhat, r, vec[5:6, :])
    dx1_o[...] = dx1
    dl = dx1.astype(bf16)
    gv[4:5, :] += jnp.sum(dl.astype(f32), 0, keepdims=True)
    tp = dot(at.T, dl)
    for k in range(NG):
        gp[k] += tp[:, k * TL : (k + 1) * TL]
    da_o[...] = dot(dl, wpv, NT).astype(bf16)

    @pl.when(i == n - 1)
    def _():
        gv_o[...] = gv[...]
        gb1_o[...] = gb1[...]

        def rows(ref, n):
            def pick(ref, w, z):
                at = pl.multiple_of(w * geo.r, geo.r)
                return [ref[z * n + k, pl.ds(at, geo.r), :] for k in range(n)]

            return ref, pick

        def turned(ref, w, z):
            n, r = geo.r2 // TL, D // geo.nz
            at = pl.multiple_of(z * r, r)
            return [ref[w * n + k, pl.ds(at, r), :] for k in range(n)]

        scatter_out(geo, me, [rows(gp, geo.cp), rows(g1, geo.c1), (g2, turned)], outs)


def mlp(geo, me, live, tok, cot, attn, bufs, vec, b1, G=4, FC=512):
    B = tok.shape[0]
    R = B * TP
    M = G * TP
    blk = pl.BlockSpec((M, D), lambda i: (i, 0))
    win = pl.BlockSpec((G, WT, D), lambda i: (i, 0, 0))
    S = jax.ShapeDtypeStruct
    gshape = (geo.nz, geo.blocks * geo.r, TL)
    V = pltpu.VMEM
    return pl.pallas_call(
        functools.partial(mlp_body, geo, G, FC),
        grid=(B // G,),
        in_specs=[smem(), smem(), win, win, blk] + [anyspace()] * len(bufs) + [whole(vec.shape), whole(b1.shape)],
        out_specs=[win, blk, blk, whole((8, D)), whole((1, FF))] + [whole(gshape)] * geo.nw,
        out_shape=[S(tok.shape, bf16), S((R, D), f32), S((R, D), bf16), S((8, D), f32), S((1, FF), f32)]
        + [S(gshape, bf16)] * geo.nw,
        scratch_shapes=[
            V((M, D), f32),
            V((M, D), f32),
            V((NG, D, TL), f32),
            V((FF // TL, D, TL), f32),
            V((FF // TL, D, TL), f32),
            V((8, D), f32),
            V((1, FF), f32),
            V((M, D), f32),
            V((M, D), f32),
            V((NG, D, TL), bf16),
            V((FF // TL, D, TL), bf16),
            V((NG, FF // geo.r, geo.r, TL), bf16),
            pltpu.SemaphoreType.DMA,
        ],
        compiler_params=params(40),
        cost_estimate=cost(44),
        name="mlp",
    )(me, live, tok, cot, attn, *bufs, vec, b1)


def attn_bwd_body(geo, G, *refs):
    nb = geo.nw
    me, q, k, v, p, da, xh, vec, gv2, gb1, place = refs[:11]
    bufs = refs[11 : 11 + nb]
    refs = refs[11 + nb :]
    dc_o, small_o = refs[:2]
    outs = refs[2 : 2 + geo.nw]
    gq, gb, gt, wq, rs, ex, sem = refs[2 + geo.nw :]
    i = pl.program_id(0)
    n = pl.num_programs(0)

    @pl.when(i == 0)
    def _():
        for m in copies_a(geo, bufs, me, wq, sem):
            m.start()
        for ref in (gq, gb, gt):
            ref[...] = jnp.zeros_like(ref)
        for m in copies_a(geo, bufs, me, wq, sem):
            m.wait()

    def window(g, carry):
        rows = pl.ds(pl.multiple_of(g * TP, 16), TP)
        cols = [slice(j * TL, (j + 1) * TL) for j in range(NG)]
        ks = [k[rows, c] for c in cols]
        vs = [v[rows, c] for c in cols]
        bqs = [spread(q[rows, c]) for c in cols]
        bas = [spread(da[rows, c]) for c in cols]
        dps = [dot(vs[i], bas[i], NT) for i in range(2)]
        dqs, dks, dvs, dss = [], [], [], []
        pts = []
        for j in range(NG + 1):
            if j + 2 < NG:
                dps.append(dot(vs[j + 2], bas[j + 2], NT))
            if j < NG:
                pts.append(p[g, j])
                pf = pts[j].astype(f32)
                t = pf * dps[j]
                dss.append((t - pf * jnp.sum(t, 0, keepdims=True)).astype(bf16))
            if 0 <= j - 0 < NG:
                i = j - 0
                dvs.append(dot(pts[i], bas[i]).astype(bf16))
            if 0 <= j - 1 < NG:
                i = j - 1
                dks.append(dot(dss[i], bqs[i]).astype(bf16))
                dqs.append((diag_t(dot(ks[i], dss[i], TN)).T[:TP] * SCALE).astype(bf16))
        for j in range(NG):
            gt[j] += dss[j].astype(f32)
            dc_o[rows, j * TL : (j + 1) * TL] = dqs[j]
            dc_o[rows, D + j * TL : D + (j + 1) * TL] = dks[j]
            dc_o[rows, 2 * D + j * TL : 2 * D + (j + 1) * TL] = dvs[j]
        return carry

    lax.fori_loop(0, G, window, 0, unroll=G)
    xt = xh[...].T
    for c in range(3):
        cols = slice(c * D, (c + 1) * D)
        dc = dc_o[:, cols]
        t = dot(xt, dc)
        for s in range(NG):
            gq[c * NG + s] += t[:, s * TL : (s + 1) * TL]
        gb[:, cols] += jnp.sum(dc.astype(f32), 0, keepdims=True)

    @pl.when(i == n - 1)
    def _():
        sums = gb[...]
        g_col = jnp.broadcast_to(vec[0:1, :], (TL, D)).T
        s_col = jnp.broadcast_to(vec[1:2, :], (TL, D)).T
        gain = jnp.zeros((D, TL), f32)
        shift = jnp.zeros((D, TL), f32)
        for s in range(3 * NG):
            part = gq[s]
            w = wq[s].astype(f32)
            total = sums[:, s * TL : (s + 1) * TL]
            gain = gain + part * w
            shift = shift + w * total
            gq[s] = part * g_col + s_col * total
        gain = jnp.sum(gain.T, 0, keepdims=True)
        shift = jnp.sum(shift.T, 0, keepdims=True)
        small_o[0:1, :] = gain
        small_o[1:2, :] = shift
        small_o[2:3, :] = sums[:, :D]
        small_o[3:4, :] = sums[:, 2 * D :]
        small_o[4:8, :] = gv2[4:8, :]
        small_o[8:24, :TT] = table_sum(gt, place, rs)
        for k in range(FF // TL):
            small_o[8 + k : 9 + k, TT:] = gb1[:, k * TL : (k + 1) * TL]

        if nb > 1:
            for z in range(geo.nz):
                ex[z] = extra_rows(geo, small_o, gb1, z)

        def rows(ref, w, z):
            at = pl.multiple_of(w * geo.r, geo.r)
            parts = [ref[z * geo.cq + s, pl.ds(at, geo.r), :] for s in range(geo.cq)]
            return parts if nb == 1 else parts + [ex[z]]

        scatter_out(geo, me, [(gq, rows)], outs)


def extra_rows(geo, small, gb1, z):
    nh = HEADS // geo.nz
    vec = small[0:8, z * TL : (z + 1) * TL]
    first = z * (FF // geo.nz)
    bias = [gb1[:, first + k * TL : first + (k + 1) * TL] for k in range(FF // geo.nz // TL)]
    table = [small[8 + z * nh : 8 + (z + 1) * nh, k * TL : (k + 1) * TL] for k in range(TT // TL)]
    rows = [vec] + bias + table
    used = sum(r.shape[0] for r in rows)
    return jnp.concatenate(rows + [jnp.zeros((EXTRA - used, TL), f32)], 0)


def attn_bwd(geo, me, q, k, v, p, da, xh, vec, gv2, gb1, place, bufs, G=4):
    R = q.shape[0]
    B = R // TP
    blk = pl.BlockSpec((G * TP, D), lambda i: (i, 0))
    S = jax.ShapeDtypeStruct
    V = pltpu.VMEM
    gshape = (geo.nz, geo.rows_a + (EXTRA if geo.cores == 2 else 0), TL)
    return pl.pallas_call(
        functools.partial(attn_bwd_body, geo, G),
        grid=(B // G,),
        in_specs=[smem(), blk, blk, blk, pl.BlockSpec((G, NG, TP, GH * TL), lambda i: (i, 0, 0, 0)), blk, blk]
        + [whole(x.shape) for x in (vec, gv2, gb1, place)]
        + [anyspace()] * len(bufs),
        out_specs=[pl.BlockSpec((G * TP, 3 * D), lambda i: (i, 0)), whole((24, D))] + [whole(gshape)] * geo.nw,
        out_shape=[S((R, 3 * D), bf16), S((24, D), f32)] + [S(gshape, bf16)] * geo.nw,
        scratch_shapes=[
            V((3 * NG, D, TL), f32),
            V((1, 3 * D), f32),
            V((NG, TP, GH * TL), f32),
            V((3 * NG, D, TL), bf16),
            V((2, HEADS * 16, TL), f32),
            V((geo.nz, EXTRA, TL), f32),
            pltpu.SemaphoreType.DMA,
        ],
        compiler_params=params(32),
        cost_estimate=cost(30),
        name="attn_bwd",
    )(me, q, k, v, p, da, xh, vec, gv2, gb1, place, *bufs)


def input_bwd_body(geo, G, *refs):
    nb = geo.nw
    me, tok, dc, dx1, vec = refs[:5]
    bufs = refs[5 : 5 + nb]
    gt_o, xs, wq, sem = refs[5 + nb :]

    @pl.when(pl.program_id(0) == 0)
    def _():
        moves = copies_a(geo, bufs, me, wq, sem)
        for m in moves:
            m.start()
        xs[...] = jnp.zeros_like(xs)
        for m in moves:
            m.wait()

    for g in range(G):
        xs[g * TP : g * TP + WT, :] = tok[g].astype(f32)
    dn = dot(dc[...], wide(wq, 0, 3 * NG), NT)
    xhat, r = norm(xs[...])
    dx = dx1[...] + norm_back(dn, xhat, r, vec[0:1, :])
    for g in range(G):
        gt_o[g] = dx[g * TP : g * TP + WT].astype(bf16)


def input_bwd(geo, me, tok, dc, dx1, vec, bufs, G=4):
    B = tok.shape[0]
    blk = pl.BlockSpec((G * TP, D), lambda i: (i, 0))
    win = pl.BlockSpec((G, WT, D), lambda i: (i, 0, 0))
    S = jax.ShapeDtypeStruct
    V = pltpu.VMEM
    return pl.pallas_call(
        functools.partial(input_bwd_body, geo, G),
        grid=(B // G,),
        in_specs=[smem(), win, pl.BlockSpec((G * TP, 3 * D), lambda i: (i, 0)), blk, whole(vec.shape)]
        + [anyspace()] * len(bufs),
        out_specs=win,
        out_shape=S(tok.shape, bf16),
        scratch_shapes=[V((G * TP, D), f32), V((3 * NG, D, TL), bf16), pltpu.SemaphoreType.DMA],
        compiler_params=params(24),
        cost_estimate=cost(10),
        name="input_bwd",
    )(me, tok, dc, dx1, vec, *bufs)


def finish_body(geo, nz, *refs):
    me, low_a, low_b = refs[:3]
    got_b = refs[3 : 2 + nz]
    got_a = refs[2 + nz : 1 + 2 * nz]
    gq_o, gp_o, g1_o, g2_o, vec_o, b1_o, tab_o, tab = refs[1 + 2 * nz :]
    r, r2 = geo.r, geo.r2
    rows = geo.rows_a + EXTRA

    def total(low, got, lo, n):
        out = low[0, lo : lo + n, :].astype(f32)
        for x in got:
            out = out + x[lo : lo + n, :].astype(f32)
        return out

    for i in range(geo.cq):
        gq_o[:, i * TL : (i + 1) * TL] = total(low_a, got_a, i * r, r)
    at = 0
    for ref, n in ((gp_o, geo.cp), (g1_o, geo.c1)):
        for i in range(n):
            ref[:, i * TL : (i + 1) * TL] = total(low_b, got_b, at, r)
            at += r
    wide_z = D // nz
    for k in range(r2 // TL):
        g2_o[k * TL : (k + 1) * TL, :] = total(low_b, got_b, at, wide_z).T
        at += wide_z
    nb = FF // nz // TL
    small = total(low_a, got_a, geo.rows_a, 16)
    own, own1 = vec_o.shape[1], b1_o.shape[1]
    vec_o[...] = pltpu.roll(small[:8], (TL - me[0] * own) % TL, 1)[:, :own]
    first = me[0] * own1
    b1 = pltpu.roll(small[8 : 8 + nb], (TL - first % TL) % TL, 1)
    row = lax.broadcasted_iota(jnp.int32, b1.shape, 0) == first // TL
    b1_o[...] = jnp.sum(jnp.where(row, b1, 0.0), 0, keepdims=True)[:, :own1]
    nh = HEADS // nz
    lo = 8 + nb
    for e in range(nz):
        t = low_a[e, geo.rows_a : rows, :].astype(f32)
        for d in range(1, nz):
            t = t + got_a[d - 1][rows + (e ^ d) * EXTRA : rows + ((e ^ d) + 1) * EXTRA, :].astype(f32)
        for k in range(TT // TL):
            tab[me[1] ^ e, :, k * TL : (k + 1) * TL] = t[lo + k * nh : lo + (k + 1) * nh]
    full = jnp.concatenate([tab[z] for z in range(nz)], 0)
    tab_o[...] = full[:, :TABLE]


def finish(geo, nw, nz, me, low_a, low_b, got_b, got_a):
    S = jax.ShapeDtypeStruct
    vmem = pl.BlockSpec(memory_space=pltpu.VMEM)
    return pl.pallas_call(
        functools.partial(finish_body, geo, nz),
        in_specs=[smem()] + [vmem] * (2 * nz),
        out_specs=[vmem] * 7,
        out_shape=[
            S((geo.r, geo.cq * TL), f32),
            S((geo.r, geo.cp * TL), f32),
            S((geo.r, geo.c1 * TL), f32),
            S((geo.r2, geo.cp * TL), f32),
            S((8, D // (nw * nz)), f32),
            S((1, FF // (nw * nz)), f32),
            S((HEADS, TABLE), f32),
        ],
        scratch_shapes=[pltpu.VMEM((nz, HEADS // nz, TT), f32)],
        compiler_params=pltpu.CompilerParams(vmem_limit_bytes=12 * 2**20),
        cost_estimate=cost(3),
        name="finish",
    )(me, low_a, low_b, *got_b, *got_a)


def swap(x, axis, size, d):
    return lax.ppermute(x, axis, [(i, i ^ d) for i in range(size)])


def after(x, *deps):
    return lax.optimization_barrier((x, *deps))[0]


def gather_z(buf, nz):
    return jnp.stack([buf] + [swap(buf, "fsdp", nz, e) for e in range(1, nz)])


def gather_xy(mine, nw):
    return [mine] + [swap(mine, "win", nw, 2 * d) for d in range(1, nw // 2)]


def gather_core(planes, nw):
    return [y for x in planes for y in (x, swap(x, "win", nw, 1))]


def sum_core(parts, nw):
    n = nw // 2
    out = [None] * n
    for d in reversed(range(n)):
        out[d] = (parts[d].astype(f32) + swap(parts[n + d], "win", nw, 1).astype(f32)).astype(bf16)
    return out


def swap_xy(sums, nw):
    return [sums[0]] + [swap(sums[d], "win", nw, 2 * d) for d in range(1, nw // 2)]


def sum_xy(parts):
    return functools.reduce(jnp.add, [x.astype(f32) for x in parts]).astype(bf16)


def swap_z(low, nz):
    return [swap(low[e], "fsdp", nz, e) for e in range(1, nz)]


def unslab(x, n):
    r = x.shape[0] // n
    return jnp.concatenate([x[i * r : (i + 1) * r] for i in range(n)], 1)


def split_b(geo, x):
    a, b = geo.cp * geo.r, (geo.cp + geo.c1) * geo.r
    two = x[b:].reshape(geo.r2 // TL, D // geo.nz, TL).transpose(0, 2, 1).reshape(geo.r2, D // geo.nz)
    return unslab(x[:a], geo.cp), unslab(x[a:b], geo.c1), two


def body(nw, nz, tokens, live, vectors, fc1_bias, w_qkv, w_proj, w_fc1, w_fc2, rel_table, cotangent):
    both = ("fsdp", "win")
    fast = D // nz == TL and FF // nw % TL == 0 and D // nw % 16 == 0 and nw > 1 and nz > 1
    fast = fast and nw & (nw - 1) == 0 and nz & (nz - 1) == 0
    place = offset_place()
    table = jnp.pad(rel_table.T, ((0, 0), (0, TT - TABLE)))
    dev = lax.axis_index(both)
    own, own1 = D // (nw * nz), FF // (nw * nz)
    if fast:
        geo = Geometry(nw, nz)
        me = jnp.stack([lax.axis_index("win"), lax.axis_index("fsdp")]).astype(jnp.int32)
        buf_a = pack((geo.rows_a + EXTRA, TL), w_qkv, vectors, fc1_bias.reshape(1, -1))
        buf_b = pack((geo.blocks, geo.r, TL), w_proj, w_fc1, w_fc2)
        mine_a = gather_z(buf_a, nz)
        pb = bias(table, place)
        planes_a = gather_xy(mine_a, nw)
        mine_b = gather_z(buf_b, nz)
        bufs_a = gather_core(planes_a, nw)
        planes_b = gather_xy(mine_b, nw)
        own_core = swap(planes_b[0], "win", nw, 1)
        xh, q, k, v, p, att, vec, b1 = attn_fwd(geo, me, tokens, pb, bufs_a)
        rest = lax.optimization_barrier((*planes_b[1:], att))[:-1]
        bufs_b = [planes_b[0], own_core] + gather_core(rest, nw)
        out, dx1, da, gv2, gb1, *gw = mlp(geo, me, live, tokens, cotangent, att, bufs_b, vec, b1)
        sums_b = sum_core(gw, nw)
        parts_b = swap_xy(sums_b, nw)
        gv2 = after(gv2, *sums_b)
        dc, _, *gq = attn_bwd(geo, me, q, k, v, p, da, xh, vec, gv2, gb1, place, bufs_a)
        res = lax.optimization_barrier((*parts_b, *gq))
        parts_b, gq = res[: len(parts_b)], res[len(parts_b) :]
        low_b = sum_xy(parts_b)
        sums_a = sum_core(gq, nw)
        parts_a = swap_xy(sums_a, nw)
        held = after(low_b, *sums_a)
        own_b = [swap((low_b if e == nz - 1 else held)[e], "fsdp", nz, e) for e in range(1, nz)]
        grad_tokens = input_bwd(geo, me, tokens, dc, dx1, after(vec, *sums_a), bufs_a)
        parts_a = lax.optimization_barrier((*parts_a, grad_tokens))[:-1]
        low_a = sum_xy(parts_a)
        tail = low_a[:, geo.rows_a :].reshape(nz * EXTRA, TL)
        own_a = [swap(jnp.concatenate([low_a[e], tail], 0), "fsdp", nz, e) for e in range(1, nz)]
        grad_qkv, grad_proj, grad_one, grad_two, grad_vectors, grad_bias, grad_table = finish(
            geo, nw, nz, me, low_a, low_b, own_b, own_a
        )
        grad_bias = grad_bias.reshape(-1)
        grad_table = grad_table.T
    else:
        geo = Geometry(1, 1)
        me = jnp.zeros((2,), jnp.int32)

        def full(w):
            return lax.all_gather(lax.all_gather(w, "fsdp", axis=1, tiled=True), "win", axis=0, tiled=True)

        bufs_a = [slabs(full(w_qkv))[None]]
        bufs_b = [jnp.concatenate([slabs(full(w)) for w in (w_proj, w_fc1, w_fc2)], 0).reshape(1, geo.blocks, D, TL)]
        vec = lax.all_gather(vectors, both, axis=1, tiled=True)
        b1 = lax.all_gather(fc1_bias, both, axis=0, tiled=True).reshape(1, -1)
        pb = bias(table, place)
        xh, q, k, v, p, att = attn_fwd(geo, me, tokens, pb, bufs_a, vec)
        out, dx1, da, gv2, gb1, gw = mlp(geo, me, live, tokens, cotangent, att, bufs_b, vec, b1)
        dc, small, gq = attn_bwd(geo, me, q, k, v, p, da, xh, vec, gv2, gb1, place, bufs_a)
        grad_tokens = input_bwd(geo, me, tokens, dc, dx1, vec, bufs_a)

        def down(g):
            g = lax.psum_scatter(g.astype(bf16), "win", scatter_dimension=0, tiled=True)
            return lax.psum_scatter(g, "fsdp", scatter_dimension=1, tiled=True).astype(f32)

        grad_qkv = down(unslab(gq[0], geo.cq))
        grad_proj, grad_one, grad_two = [down(g) for g in split_b(geo, gw[0])]
        small = lax.psum(small, both)
        grad_vectors = lax.dynamic_slice_in_dim(small[:8], dev * own, own, 1)
        grad_bias = lax.dynamic_slice_in_dim(small[8:, TT:].reshape(FF), dev * own1, own1, 0)
        grad_table = small[8:, :TABLE].T
    return out, grad_tokens, grad_vectors, grad_bias, grad_qkv, grad_proj, grad_one, grad_two, grad_table


def solution(mesh):
    split = P(("fsdp", "win"), None, None)
    vecs = P(None, ("fsdp", "win"))
    flat = P(("fsdp", "win"))
    cut = P("win", "fsdp")
    return jax.shard_map(
        functools.partial(body, mesh.shape["win"], mesh.shape["fsdp"]),
        mesh=mesh,
        in_specs=(split, flat, vecs, flat, cut, cut, cut, cut, P(), split),
        out_specs=(split, split, vecs, flat, cut, cut, cut, cut, P()),
        check_vma=False,
    )
```

```python
import functools

import jax
import jax.numpy as jnp
import numpy as np
from jax import lax
from jax.experimental import pallas as pl
from jax.experimental.pallas import tpu as pltpu
from jax.sharding import PartitionSpec as P

f32 = jnp.float32
bf16 = jnp.bfloat16
HEADS = 16
HD = 32
WS = 10
WT = WS * WS
D = HEADS * HD
FF = 4 * D
SIDE = 2 * WS - 1
TABLE = SIDE * SIDE
TP = 112
TL = 128
TT = 384
GH = 4
NG = HEADS // GH
EPS = 1e-5
SCALE = HD**-0.5
EXTRA = 32
NN = (((1,), (0,)), ((), ()))
NT = (((1,), (1,)), ((), ()))
TN = (((0,), (0,)), ((), ()))


def dot(a, b, dims=NN):
    return lax.dot_general(a, b, dims, preferred_element_type=f32)


def params(mib):
    return pltpu.CompilerParams(dimension_semantics=("arbitrary",), vmem_limit_bytes=mib * 2**20)


def cost(us):
    return pl.CostEstimate(flops=int(us * 1.1e9), bytes_accessed=int(us * 1e6), transcendentals=0)


def whole(shape):
    n = len(shape)
    return pl.BlockSpec(shape, lambda *a: (0,) * n, pipeline_mode=pl.Buffered(1))


def smem():
    return pl.BlockSpec(memory_space=pltpu.SMEM)


def anyspace():
    return pl.BlockSpec(memory_space=pl.ANY)


def three(x):
    hi = x.astype(bf16)
    rest = x - hi.astype(f32)
    mid = rest.astype(bf16)
    return hi, mid, (rest - mid.astype(f32)).astype(bf16)


def offset_place():
    cj = np.arange(WS)[:, None, None]
    r = np.arange(TT)[None, :, None]
    l = np.arange(256)[None, None, :]
    hit = (l < SIDE * WS) & (r == (l // WS) * SIDE + (l % WS) - cj + WS - 1)
    return jnp.asarray(hit, bf16)


class Geometry:
    def __init__(self, nw, nz):
        self.nw, self.nz = nw, nz
        self.r = D // nw
        self.cq, self.cp, self.c1 = 3 * D // nz // TL, D // nz // TL, FF // nz // TL
        self.r2 = FF // nw
        self.rows_a = self.cq * self.r
        self.blocks = self.c1 + 5 * self.cp
        self.cores = 2 if nw > 1 else 1


def slabs(x):
    return jnp.concatenate([x[:, i : i + TL] for i in range(0, x.shape[1], TL)], 0)


def pack_body(count, *refs):
    srcs, out = refs[:count], refs[count]
    rest = refs[count + 1 :]
    stage, flat, sem = rest[:count], rest[-2], rest[-1]
    moves = [pltpu.make_async_copy(x, y, sem.at[i]) for i, (x, y) in enumerate(zip(srcs, stage))]
    for m in moves:
        m.start()
    parts = []
    r = flat.shape[-2]
    at = 0
    for m, w in zip(moves, stage):
        m.wait()
        if w.dtype == f32:
            part = [p.astype(f32) for p in three(w[...])]
            parts += [jnp.concatenate([p, jnp.zeros((p.shape[0], TL - p.shape[1]), f32)], 1) for p in part]
            continue
        for i in range(0, w.shape[1], TL):
            if len(flat.shape) == 2:
                flat[at : at + w.shape[0], :] = w[:, i : i + TL]
                at += w.shape[0]
                continue
            for k in range(0, w.shape[0], r):
                flat[at] = w[k : k + r, i : i + TL]
                at += 1
    if parts:
        used = sum(p.shape[0] for p in parts)
        flat[at : at + EXTRA, :] = jnp.concatenate(parts + [jnp.zeros((EXTRA - used, TL), f32)], 0).astype(bf16)
    last = pltpu.make_async_copy(flat, out, sem.at[count])
    last.start()
    last.wait()


def pack(shape, *arrays):
    V = pltpu.VMEM
    return pl.pallas_call(
        functools.partial(pack_body, len(arrays)),
        in_specs=[anyspace()] * len(arrays),
        out_specs=anyspace(),
        out_shape=jax.ShapeDtypeStruct(shape, bf16),
        scratch_shapes=[V(x.shape, x.dtype) for x in arrays]
        + [V(shape, bf16), pltpu.SemaphoreType.DMA((len(arrays) + 1,))],
        compiler_params=pltpu.CompilerParams(vmem_limit_bytes=60 * 2**20),
        cost_estimate=cost(2),
        name="pack",
    )(*arrays)


def copies_a(geo, bufs, me, wq, sem):
    out = []
    for d in range(geo.nw):
        row = pl.multiple_of((me[0] ^ d) * geo.r, geo.r)
        for e in range(geo.nz):
            col = (me[1] ^ e) * geo.cq
            for i in range(geo.cq):
                out.append(
                    pltpu.make_async_copy(
                        bufs[d].at[e, pl.ds(i * geo.r, geo.r), :],
                        wq.at[col + i, pl.ds(row, geo.r), :],
                        sem,
                    )
                )
    return out


def copies_b(geo, bufs, me, wp, w1, w2, sem):
    out = []
    for d in range(geo.nw):
        w = me[0] ^ d
        row = pl.multiple_of(w * geo.r, geo.r)
        for e in range(geo.nz):
            z = me[1] ^ e
            for ref, at, n in ((wp, 0, geo.cp), (w1, geo.cp, geo.c1)):
                src = bufs[d].at[e, pl.ds(at, n)]
                out.append(pltpu.make_async_copy(src, ref.at[pl.ds(z * n, n), pl.ds(row, geo.r), :], sem))
            for i in range(geo.cp):
                src = bufs[d].at[e, pl.ds(geo.cp + geo.c1 + 4 * i, 4)]
                out.append(pltpu.make_async_copy(src, w2.at[z * geo.cp + i, pl.ds(w * 4, 4)], sem))
    return out


def wide(ref, lo, n):
    return jnp.concatenate([ref[lo + i] for i in range(n)], 1)


def strided(ref, first, count, step):
    return jnp.concatenate([ref[half, pl.ds(first, count, stride=step), :] for half in range(2)], 1)


def bias_body(table, place, pb_o, zs):
    parts = jnp.concatenate([p for p in three(table[...])], 0)
    for cj in range(WS):
        z = dot(parts, place[cj])
        z = z[:HEADS] + z[HEADS : 2 * HEADS] + z[2 * HEADS :]
        for half in range(2):
            zs[half, cj * HEADS : (cj + 1) * HEADS, :] = z[:, half * TL : (half + 1) * TL]
    for j in range(NG):
        pb_o[j, WT:TP, :] = jnp.zeros((TP - WT, GH * TL), f32)
        for h in range(GH):
            zh = strided(zs, j * GH + h, WS, HEADS)
            for rj in range(WS):
                off = (WS - 1 - rj) * WS
                part = zh if off == 0 else pltpu.roll(zh, 256 - off, 1)
                pb_o[j, rj * WS : (rj + 1) * WS, h * TL : (h + 1) * TL] = jnp.exp(part[:, :TL])


def bias(table, place):
    return pl.pallas_call(
        bias_body,
        out_shape=jax.ShapeDtypeStruct((NG, TP, GH * TL), f32),
        scratch_shapes=[pltpu.VMEM((2, WS * HEADS, TL), f32)],
        compiler_params=pltpu.CompilerParams(vmem_limit_bytes=24 * 2**20),
        cost_estimate=cost(4),
        name="position_bias",
    )(table, place)


def table_sum(gt, place, rs):
    for j in range(NG):
        for h in range(GH):
            total = None
            for rj in range(WS):
                part = gt[j, rj * WS : (rj + 1) * WS, h * TL : (h + 1) * TL]
                part = jnp.concatenate([part, jnp.zeros((WS, TL), f32)], 1)
                off = (WS - 1 - rj) * WS
                part = part if off == 0 else pltpu.roll(part, off, 1)
                total = part if total is None else total + part
            base = (j * GH + h) * 16
            for half in range(2):
                rs[half, base : base + WS, :] = total[:, half * TL : (half + 1) * TL]
    columns = jnp.concatenate([strided(rs, cj, HEADS, 16) for cj in range(WS)], 1)
    z = dot(jnp.concatenate(three(columns), 0), jnp.concatenate([place[cj] for cj in range(WS)], 1), NT)
    return z[:HEADS] + z[HEADS : 2 * HEADS] + z[2 * HEADS :]


def norm(x):
    mean = jnp.sum(x, -1, keepdims=True) * (1.0 / D)
    c = x - mean
    var = jnp.sum(c * c, -1, keepdims=True) * (1.0 / D)
    r = lax.rsqrt(var + EPS)
    return c * r, r


def norm_back(dn, xhat, r, gain):
    t = dn * gain
    m1 = jnp.sum(t, -1, keepdims=True) * (1.0 / D)
    m2 = jnp.sum(t * xhat, -1, keepdims=True) * (1.0 / D)
    return (t - m1 - xhat * m2) * r


def spread(part):
    lane = lax.broadcasted_iota(jnp.int32, (1, TL), 1) // HD
    none = jnp.zeros((TL - TP, TL), part.dtype)
    return jnp.concatenate([x for h in range(GH) for x in (jnp.where(lane == h, part, jnp.zeros_like(part)), none)], 0)


def diag_t(full):
    return jnp.concatenate([full[h * HD : (h + 1) * HD, h * TL : (h + 1) * TL] for h in range(GH)], 0)


def gather_vectors(bufs, geo, me, vec_o, b1_o, tmp):
    own = D // (geo.nw * geo.nz)
    own1 = FF // (geo.nw * geo.nz)
    i32 = jnp.int32
    pick = (lax.broadcasted_iota(i32, (TL, D), 0) == lax.broadcasted_iota(i32, (TL, D), 1) % own).astype(bf16)
    pick1 = (lax.broadcasted_iota(i32, (TL, FF), 0) == lax.broadcasted_iota(i32, (TL, FF), 1) % own1).astype(bf16)
    slot = lax.broadcasted_iota(i32, (1, D), 1) // own
    slot1 = lax.broadcasted_iota(i32, (1, FF), 1) // own1
    vec = jnp.zeros((8, D), f32)
    b1 = jnp.zeros((8, FF), f32)
    for d in range(geo.nw):
        for e in range(geo.nz):
            dev = (me[1] ^ e) * geo.nw + (me[0] ^ d)
            x = tmp[d, e]
            y = dot(x[:24], pick)
            vec = vec + jnp.where(slot == dev, y[:8] + y[8:16] + y[16:24], 0.0)
            y1 = dot(x[24:], pick1)
            b1 = b1 + jnp.where(slot1 == dev, y1, 0.0)
    vec_o[...] = vec
    b1_o[...] = b1[0:1] + b1[1:2] + b1[2:3]


def attn_fwd_body(geo, G, vectors_in, *refs):
    nb = geo.nw
    me, tok, pb = refs[:3]
    bufs = refs[3 : 3 + nb]
    refs = refs[3 + nb :]
    if vectors_in:
        vec, refs = refs[0], refs[1:]
    n1_o, q_o, k_o, v_o, p_o, a_o = refs[:6]
    refs = refs[6:]
    if not vectors_in:
        vec, b1_o = refs[:2]
        refs = refs[2:]
    xs, wq, tmp, sem, sem2 = refs

    @pl.when(pl.program_id(0) == 0)
    def _():
        moves = copies_a(geo, bufs, me, wq, sem)
        for m in moves:
            m.start()
        if not vectors_in:
            small = [
                pltpu.make_async_copy(bufs[d].at[:, pl.ds(geo.rows_a, EXTRA), :], tmp.at[d], sem2)
                for d in range(geo.nw)
            ]
            for m in small:
                m.start()
        xs[...] = jnp.zeros_like(xs)
        if not vectors_in:
            for m in small:
                m.wait()
            gather_vectors(bufs, geo, me, vec, b1_o, tmp)
        for m in moves:
            m.wait()

    for g in range(G):
        xs[g * TP : g * TP + WT, :] = tok[g].astype(f32)
        xs[g * TP + WT : (g + 1) * TP, :] = tok[g, : TP - WT, :].astype(f32)
    xhat, _ = norm(xs[...])
    n1 = (xhat * vec[0:1, :] + vec[1:2, :]).astype(bf16)
    n1_o[...] = xhat.astype(bf16)
    q_o[...] = ((dot(n1, wide(wq, 0, NG)) + vec[2:3, :]) * SCALE).astype(bf16)
    k_o[...] = dot(n1, wide(wq, NG, NG)).astype(bf16)
    v_o[...] = (dot(n1, wide(wq, 2 * NG, NG)) + vec[3:4, :]).astype(bf16)

    def window(g, carry):
        rows = pl.ds(pl.multiple_of(g * TP, 16), TP)
        cols = [slice(j * TL, (j + 1) * TL) for j in range(NG)]
        ks = [k_o[rows, c] for c in cols]
        vs = [v_o[rows, c] for c in cols]
        qs = [spread(q_o[rows, c]) for c in cols]
        scores = [dot(ks[j], qs[j], NT) for j in range(NG)]
        ps, outs = [], []
        for j in range(NG):
            s = scores[j]
            e = jnp.exp(s - jnp.max(s, 0, keepdims=True)) * pb[j]
            p = (e * (1.0 / jnp.sum(e, 0, keepdims=True))).astype(bf16)
            ps.append(p)
            outs.append(diag_t(dot(vs[j], p, TN)).T[:TP].astype(bf16))
        for j in range(NG):
            p_o[g, j] = ps[j]
            a_o[rows, cols[j]] = outs[j]
        return carry

    lax.fori_loop(0, G, window, 0, unroll=G)


def attn_fwd(geo, me, tok, pb, bufs, vec=None, G=4):
    B = tok.shape[0]
    R = B * TP
    S = jax.ShapeDtypeStruct
    act = S((R, D), bf16)
    blk = pl.BlockSpec((G * TP, D), lambda i: (i, 0))
    given = [] if vec is None else [vec]
    out_specs = [blk, blk, blk, blk, pl.BlockSpec((G, NG, TP, GH * TL), lambda i: (i, 0, 0, 0)), blk]
    out_shape = [act, act, act, act, S((B, NG, TP, GH * TL), bf16), act]
    if vec is None:
        out_specs += [whole((8, D)), whole((1, FF))]
        out_shape += [S((8, D), f32), S((1, FF), f32)]
    return pl.pallas_call(
        functools.partial(attn_fwd_body, geo, G, vec is not None),
        grid=(B // G,),
        in_specs=[smem(), pl.BlockSpec((G, WT, D), lambda i: (i, 0, 0)), whole(pb.shape)]
        + [anyspace()] * len(bufs)
        + [whole(g.shape) for g in given],
        out_specs=out_specs,
        out_shape=out_shape,
        scratch_shapes=[
            pltpu.VMEM((G * TP, D), f32),
            pltpu.VMEM((3 * NG, D, TL), bf16),
            pltpu.VMEM((geo.nw, geo.nz, EXTRA, TL), bf16),
            pltpu.SemaphoreType.DMA,
            pltpu.SemaphoreType.DMA,
        ],
        compiler_params=params(28),
        cost_estimate=cost(30),
        name="attn_fwd",
    )(me, tok, pb, *bufs, *given)


GC = 0.7978845608028654
GA = 0.044715


def gelu_both(u):
    u2 = u * u
    t = jnp.tanh(u * (GC + (GC * GA) * u2))
    h = 0.5 + 0.5 * t
    act = u * h
    slope = h + (act * (2.0 - 2.0 * h)) * (GC + (3.0 * GC * GA) * u2)
    return act, slope


def scatter_out(geo, me, blocks, outs):
    cores = geo.cores
    for c in range(cores):
        for xy in range(geo.nw // cores):
            w = me[0] ^ (xy * cores + c)
            for e in range(geo.nz):
                z = me[1] ^ e
                at = 0
                for ref, pick in blocks:
                    for part in pick(ref, w, z):
                        outs[c * (geo.nw // cores) + xy][e, at : at + part.shape[0], :] = part.astype(bf16)
                        at += part.shape[0]


def mlp_body(geo, G, FC, *refs):
    nb = geo.nw
    me, live, tok, cot, attn = refs[:5]
    bufs = refs[5 : 5 + nb]
    vec, b1 = refs[5 + nb : 7 + nb]
    refs = refs[7 + nb :]
    out_o, dx1_o, da_o, gv_o, gb1_o = refs[:5]
    outs = refs[5 : 5 + geo.nw]
    xs, dys, gp, g1, g2, gv, gb1, acc, dn2, wp, w1, w2, sem = refs[5 + geo.nw :]
    i = pl.program_id(0)
    n = pl.num_programs(0)

    @pl.when(i == 0)
    def _():
        moves = copies_b(geo, bufs, me, wp, w1, w2, sem)
        for m in moves:
            m.start()
        for ref in (xs, dys, gp, g1, g2, gv, gb1):
            ref[...] = jnp.zeros_like(ref)
        for m in moves:
            m.wait()

    for g in range(G):
        xs[g * TP : g * TP + WT, :] = tok[g].astype(f32)
        mask = (i * G + g < live[0]).astype(f32)
        dys[g * TP : g * TP + WT, :] = cot[g].astype(f32) * mask
    at = attn[...]
    wpv = wide(wp, 0, NG)
    x1 = xs[...] + dot(at, wpv) + vec[4:5, :]
    acc[...] = x1 + vec[7:8, :]
    xhat, r = norm(x1)
    n2 = (xhat * vec[5:6, :] + vec[6:7, :]).astype(bf16)
    n2t = n2.T
    dyf = dys[...]
    dy = dyf.astype(bf16)
    dyt = dy.T
    ns = FC // TL
    n = FF // FC

    def first(c):
        cols = slice(c * FC, (c + 1) * FC)
        w1c = wide(w1, c * ns, ns)
        w2c = jnp.concatenate([w2[z, cols.start // geo.r : cols.stop // geo.r].reshape(FC, TL) for z in range(NG)], 1)
        return w1c, w2c, dot(n2, w1c), dot(dy, w2c, NT)

    def last(c):
        cols = slice(c * FC, (c + 1) * FC)
        w1c, w2c = work[c][:2]
        a, du = mids[c]
        acc[...] += dot(a, w2c)
        t2 = dot(dyt, a)
        t1 = dot(n2t, du)
        for k in range(ns):
            g2[c * ns + k] += t2[:, k * TL : (k + 1) * TL]
            g1[c * ns + k] += t1[:, k * TL : (k + 1) * TL]
        gb1[:, cols] += jnp.sum(du.astype(f32), 0, keepdims=True)
        d = dot(du, w1c, NT)
        if c == 0:
            dn2[...] = d
        else:
            dn2[...] += d

    work = [first(c) for c in range(1)]
    mids = []
    for c in range(n + 1):
        if c + 1 < n:
            work.append(first(c + 1))
        if c < n:
            a, ga = gelu_both(work[c][2] + b1[:, c * FC : (c + 1) * FC])
            mids.append((a.astype(bf16), (work[c][3] * ga).astype(bf16)))
        if c >= 1:
            last(c - 1)
    n = pl.num_programs(0)
    for g in range(G):
        mask = (i * G + g < live[0]).astype(f32)
        out_o[g] = (acc[g * TP : g * TP + WT, :] * mask).astype(bf16)
    dn = dn2[...]
    gv[7:8, :] += jnp.sum(dyf, 0, keepdims=True)
    gv[5:6, :] += jnp.sum(dn * xhat, 0, keepdims=True)
    gv[6:7, :] += jnp.sum(dn, 0, keepdims=True)
    dx1 = dyf + norm_back(dn, xhat, r, vec[5:6, :])
    dx1_o[...] = dx1
    dl = dx1.astype(bf16)
    gv[4:5, :] += jnp.sum(dl.astype(f32), 0, keepdims=True)
    tp = dot(at.T, dl)
    for k in range(NG):
        gp[k] += tp[:, k * TL : (k + 1) * TL]
    da_o[...] = dot(dl, wpv, NT).astype(bf16)

    @pl.when(i == n - 1)
    def _():
        gv_o[...] = gv[...]
        gb1_o[...] = gb1[...]

        def rows(ref, n):
            def pick(ref, w, z):
                at = pl.multiple_of(w * geo.r, geo.r)
                return [ref[z * n + k, pl.ds(at, geo.r), :] for k in range(n)]

            return ref, pick

        def turned(ref, w, z):
            n, r = geo.r2 // TL, D // geo.nz
            at = pl.multiple_of(z * r, r)
            return [ref[w * n + k, pl.ds(at, r), :] for k in range(n)]

        scatter_out(geo, me, [rows(gp, geo.cp), rows(g1, geo.c1), (g2, turned)], outs)


def mlp(geo, me, live, tok, cot, attn, bufs, vec, b1, G=4, FC=512):
    B = tok.shape[0]
    R = B * TP
    M = G * TP
    blk = pl.BlockSpec((M, D), lambda i: (i, 0))
    win = pl.BlockSpec((G, WT, D), lambda i: (i, 0, 0))
    S = jax.ShapeDtypeStruct
    gshape = (geo.nz, geo.blocks * geo.r, TL)
    V = pltpu.VMEM
    return pl.pallas_call(
        functools.partial(mlp_body, geo, G, FC),
        grid=(B // G,),
        in_specs=[smem(), smem(), win, win, blk] + [anyspace()] * len(bufs) + [whole(vec.shape), whole(b1.shape)],
        out_specs=[win, blk, blk, whole((8, D)), whole((1, FF))] + [whole(gshape)] * geo.nw,
        out_shape=[S(tok.shape, bf16), S((R, D), f32), S((R, D), bf16), S((8, D), f32), S((1, FF), f32)]
        + [S(gshape, bf16)] * geo.nw,
        scratch_shapes=[
            V((M, D), f32),
            V((M, D), f32),
            V((NG, D, TL), f32),
            V((FF // TL, D, TL), f32),
            V((FF // TL, D, TL), f32),
            V((8, D), f32),
            V((1, FF), f32),
            V((M, D), f32),
            V((M, D), f32),
            V((NG, D, TL), bf16),
            V((FF // TL, D, TL), bf16),
            V((NG, FF // geo.r, geo.r, TL), bf16),
            pltpu.SemaphoreType.DMA,
        ],
        compiler_params=params(40),
        cost_estimate=cost(44),
        name="mlp",
    )(me, live, tok, cot, attn, *bufs, vec, b1)


def attn_bwd_body(geo, G, *refs):
    nb = geo.nw
    me, q, k, v, p, da, xh, vec, gv2, gb1, place = refs[:11]
    bufs = refs[11 : 11 + nb]
    refs = refs[11 + nb :]
    dc_o, small_o = refs[:2]
    outs = refs[2 : 2 + geo.nw]
    gq, gb, gt, wq, rs, ex, sem = refs[2 + geo.nw :]
    i = pl.program_id(0)
    n = pl.num_programs(0)

    @pl.when(i == 0)
    def _():
        for m in copies_a(geo, bufs, me, wq, sem):
            m.start()
        for ref in (gq, gb, gt):
            ref[...] = jnp.zeros_like(ref)

    def window(g, carry):
        rows = pl.ds(pl.multiple_of(g * TP, 16), TP)
        cols = [slice(j * TL, (j + 1) * TL) for j in range(NG)]
        ks = [k[rows, c] for c in cols]
        vs = [v[rows, c] for c in cols]
        bqs = [spread(q[rows, c]) for c in cols]
        bas = [spread(da[rows, c]) for c in cols]
        dps = [dot(vs[i], bas[i], NT) for i in range(2)]
        dqs, dks, dvs, dss = [], [], [], []
        pts = []
        for j in range(NG + 1):
            if j + 2 < NG:
                dps.append(dot(vs[j + 2], bas[j + 2], NT))
            if j < NG:
                pts.append(p[g, j])
                pf = pts[j].astype(f32)
                t = pf * dps[j]
                dss.append((t - pf * jnp.sum(t, 0, keepdims=True)).astype(bf16))
            if 0 <= j - 0 < NG:
                i = j - 0
                dvs.append(dot(pts[i], bas[i]).astype(bf16))
            if 0 <= j - 1 < NG:
                i = j - 1
                dks.append(dot(dss[i], bqs[i]).astype(bf16))
                dqs.append((diag_t(dot(ks[i], dss[i], TN)).T[:TP] * SCALE).astype(bf16))
        for j in range(NG):
            gt[j] += dss[j].astype(f32)
            dc_o[rows, j * TL : (j + 1) * TL] = dqs[j]
            dc_o[rows, D + j * TL : D + (j + 1) * TL] = dks[j]
            dc_o[rows, 2 * D + j * TL : 2 * D + (j + 1) * TL] = dvs[j]
        return carry

    lax.fori_loop(0, G, window, 0, unroll=G)
    xt = xh[...].T
    for c in range(3):
        cols = slice(c * D, (c + 1) * D)
        dc = dc_o[:, cols]
        t = dot(xt, dc)
        for s in range(NG):
            gq[c * NG + s] += t[:, s * TL : (s + 1) * TL]
        gb[:, cols] += jnp.sum(dc.astype(f32), 0, keepdims=True)

    @pl.when(i == n - 1)
    def _():
        for m in copies_a(geo, bufs, me, wq, sem):
            m.wait()
        sums = gb[...]
        g_col = jnp.broadcast_to(vec[0:1, :], (TL, D)).T
        s_col = jnp.broadcast_to(vec[1:2, :], (TL, D)).T
        gain = jnp.zeros((D, TL), f32)
        shift = jnp.zeros((D, TL), f32)
        for s in range(3 * NG):
            part = gq[s]
            w = wq[s].astype(f32)
            total = sums[:, s * TL : (s + 1) * TL]
            gain = gain + part * w
            shift = shift + w * total
            gq[s] = part * g_col + s_col * total
        gain = jnp.sum(gain.T, 0, keepdims=True)
        shift = jnp.sum(shift.T, 0, keepdims=True)
        small_o[0:1, :] = gain
        small_o[1:2, :] = shift
        small_o[2:3, :] = sums[:, :D]
        small_o[3:4, :] = sums[:, 2 * D :]
        small_o[4:8, :] = gv2[4:8, :]
        small_o[8:24, :TT] = table_sum(gt, place, rs)
        for k in range(FF // TL):
            small_o[8 + k : 9 + k, TT:] = gb1[:, k * TL : (k + 1) * TL]

        if nb > 1:
            for z in range(geo.nz):
                ex[z] = extra_rows(geo, small_o, gb1, z)

        def rows(ref, w, z):
            at = pl.multiple_of(w * geo.r, geo.r)
            parts = [ref[z * geo.cq + s, pl.ds(at, geo.r), :] for s in range(geo.cq)]
            return parts if nb == 1 else parts + [ex[z]]

        scatter_out(geo, me, [(gq, rows)], outs)


def extra_rows(geo, small, gb1, z):
    nh = HEADS // geo.nz
    vec = small[0:8, z * TL : (z + 1) * TL]
    first = z * (FF // geo.nz)
    bias = [gb1[:, first + k * TL : first + (k + 1) * TL] for k in range(FF // geo.nz // TL)]
    table = [small[8 + z * nh : 8 + (z + 1) * nh, k * TL : (k + 1) * TL] for k in range(TT // TL)]
    rows = [vec] + bias + table
    used = sum(r.shape[0] for r in rows)
    return jnp.concatenate(rows + [jnp.zeros((EXTRA - used, TL), f32)], 0)


def attn_bwd(geo, me, q, k, v, p, da, xh, vec, gv2, gb1, place, bufs, G=4):
    R = q.shape[0]
    B = R // TP
    blk = pl.BlockSpec((G * TP, D), lambda i: (i, 0))
    S = jax.ShapeDtypeStruct
    V = pltpu.VMEM
    gshape = (geo.nz, geo.rows_a + (EXTRA if geo.cores == 2 else 0), TL)
    return pl.pallas_call(
        functools.partial(attn_bwd_body, geo, G),
        grid=(B // G,),
        in_specs=[smem(), blk, blk, blk, pl.BlockSpec((G, NG, TP, GH * TL), lambda i: (i, 0, 0, 0)), blk, blk]
        + [whole(x.shape) for x in (vec, gv2, gb1, place)]
        + [anyspace()] * len(bufs),
        out_specs=[pl.BlockSpec((G * TP, 3 * D), lambda i: (i, 0)), whole((24, D))] + [whole(gshape)] * geo.nw,
        out_shape=[S((R, 3 * D), bf16), S((24, D), f32)] + [S(gshape, bf16)] * geo.nw,
        scratch_shapes=[
            V((3 * NG, D, TL), f32),
            V((1, 3 * D), f32),
            V((NG, TP, GH * TL), f32),
            V((3 * NG, D, TL), bf16),
            V((2, HEADS * 16, TL), f32),
            V((geo.nz, EXTRA, TL), f32),
            pltpu.SemaphoreType.DMA,
        ],
        compiler_params=params(32),
        cost_estimate=cost(30),
        name="attn_bwd",
    )(me, q, k, v, p, da, xh, vec, gv2, gb1, place, *bufs)


def input_bwd_body(geo, G, *refs):
    nb = geo.nw
    me, tok, dc, dx1, vec = refs[:5]
    bufs = refs[5 : 5 + nb]
    gt_o, xs, wq, sem = refs[5 + nb :]

    @pl.when(pl.program_id(0) == 0)
    def _():
        moves = copies_a(geo, bufs, me, wq, sem)
        for m in moves:
            m.start()
        xs[...] = jnp.zeros_like(xs)
        for m in moves:
            m.wait()

    for g in range(G):
        xs[g * TP : g * TP + WT, :] = tok[g].astype(f32)
    dn = dot(dc[...], wide(wq, 0, 3 * NG), NT)
    xhat, r = norm(xs[...])
    dx = dx1[...] + norm_back(dn, xhat, r, vec[0:1, :])
    for g in range(G):
        gt_o[g] = dx[g * TP : g * TP + WT].astype(bf16)


def input_bwd(geo, me, tok, dc, dx1, vec, bufs, G=4):
    B = tok.shape[0]
    blk = pl.BlockSpec((G * TP, D), lambda i: (i, 0))
    win = pl.BlockSpec((G, WT, D), lambda i: (i, 0, 0))
    S = jax.ShapeDtypeStruct
    V = pltpu.VMEM
    return pl.pallas_call(
        functools.partial(input_bwd_body, geo, G),
        grid=(B // G,),
        in_specs=[smem(), win, pl.BlockSpec((G * TP, 3 * D), lambda i: (i, 0)), blk, whole(vec.shape)]
        + [anyspace()] * len(bufs),
        out_specs=win,
        out_shape=S(tok.shape, bf16),
        scratch_shapes=[V((G * TP, D), f32), V((3 * NG, D, TL), bf16), pltpu.SemaphoreType.DMA],
        compiler_params=params(24),
        cost_estimate=cost(10),
        name="input_bwd",
    )(me, tok, dc, dx1, vec, *bufs)


def finish_body(geo, nz, *refs):
    me, low_a, low_b = refs[:3]
    got_b = refs[3 : 2 + nz]
    got_a = refs[2 + nz : 1 + 2 * nz]
    gq_o, gp_o, g1_o, g2_o, vec_o, b1_o, tab_o, tab = refs[1 + 2 * nz :]
    r, r2 = geo.r, geo.r2
    rows = geo.rows_a + EXTRA

    def total(low, got, lo, n):
        out = low[0, lo : lo + n, :].astype(f32)
        for x in got:
            out = out + x[lo : lo + n, :].astype(f32)
        return out

    for i in range(geo.cq):
        gq_o[:, i * TL : (i + 1) * TL] = total(low_a, got_a, i * r, r)
    at = 0
    for ref, n in ((gp_o, geo.cp), (g1_o, geo.c1)):
        for i in range(n):
            ref[:, i * TL : (i + 1) * TL] = total(low_b, got_b, at, r)
            at += r
    wide_z = D // nz
    for k in range(r2 // TL):
        g2_o[k * TL : (k + 1) * TL, :] = total(low_b, got_b, at, wide_z).T
        at += wide_z
    nb = FF // nz // TL
    small = total(low_a, got_a, geo.rows_a, 16)
    own, own1 = vec_o.shape[1], b1_o.shape[1]
    vec_o[...] = pltpu.roll(small[:8], (TL - me[0] * own) % TL, 1)[:, :own]
    first = me[0] * own1
    b1 = pltpu.roll(small[8 : 8 + nb], (TL - first % TL) % TL, 1)
    row = lax.broadcasted_iota(jnp.int32, b1.shape, 0) == first // TL
    b1_o[...] = jnp.sum(jnp.where(row, b1, 0.0), 0, keepdims=True)[:, :own1]
    nh = HEADS // nz
    lo = 8 + nb
    for e in range(nz):
        t = low_a[e, geo.rows_a : rows, :].astype(f32)
        for d in range(1, nz):
            t = t + got_a[d - 1][rows + (e ^ d) * EXTRA : rows + ((e ^ d) + 1) * EXTRA, :].astype(f32)
        for k in range(TT // TL):
            tab[me[1] ^ e, :, k * TL : (k + 1) * TL] = t[lo + k * nh : lo + (k + 1) * nh]
    full = jnp.concatenate([tab[z] for z in range(nz)], 0)
    tab_o[...] = full[:, :TABLE]


def finish(geo, nw, nz, me, low_a, low_b, got_b, got_a):
    S = jax.ShapeDtypeStruct
    vmem = pl.BlockSpec(memory_space=pltpu.VMEM)
    return pl.pallas_call(
        functools.partial(finish_body, geo, nz),
        in_specs=[smem()] + [vmem] * (2 * nz),
        out_specs=[vmem] * 7,
        out_shape=[
            S((geo.r, geo.cq * TL), f32),
            S((geo.r, geo.cp * TL), f32),
            S((geo.r, geo.c1 * TL), f32),
            S((geo.r2, geo.cp * TL), f32),
            S((8, D // (nw * nz)), f32),
            S((1, FF // (nw * nz)), f32),
            S((HEADS, TABLE), f32),
        ],
        scratch_shapes=[pltpu.VMEM((nz, HEADS // nz, TT), f32)],
        compiler_params=pltpu.CompilerParams(vmem_limit_bytes=12 * 2**20),
        cost_estimate=cost(3),
        name="finish",
    )(me, low_a, low_b, *got_b, *got_a)


def swap(x, axis, size, d):
    return lax.ppermute(x, axis, [(i, i ^ d) for i in range(size)])


def after(x, *deps):
    return lax.optimization_barrier((x, *deps))[0]


def gather_z(buf, nz):
    return jnp.stack([buf] + [swap(buf, "fsdp", nz, e) for e in range(1, nz)])


def gather_xy(mine, nw):
    return [mine] + [swap(mine, "win", nw, 2 * d) for d in range(1, nw // 2)]


def gather_core(planes, nw):
    return [y for x in planes for y in (x, swap(x, "win", nw, 1))]


def sum_core(parts, nw):
    n = nw // 2
    out = [None] * n
    for d in reversed(range(n)):
        out[d] = (parts[d].astype(f32) + swap(parts[n + d], "win", nw, 1).astype(f32)).astype(bf16)
    return out


def swap_xy(sums, nw):
    return [sums[0]] + [swap(sums[d], "win", nw, 2 * d) for d in range(1, nw // 2)]


def sum_xy(parts):
    return functools.reduce(jnp.add, [x.astype(f32) for x in parts]).astype(bf16)


def swap_z(low, nz):
    return [swap(low[e], "fsdp", nz, e) for e in range(1, nz)]


def unslab(x, n):
    r = x.shape[0] // n
    return jnp.concatenate([x[i * r : (i + 1) * r] for i in range(n)], 1)


def split_b(geo, x):
    a, b = geo.cp * geo.r, (geo.cp + geo.c1) * geo.r
    two = x[b:].reshape(geo.r2 // TL, D // geo.nz, TL).transpose(0, 2, 1).reshape(geo.r2, D // geo.nz)
    return unslab(x[:a], geo.cp), unslab(x[a:b], geo.c1), two


def body(nw, nz, tokens, live, vectors, fc1_bias, w_qkv, w_proj, w_fc1, w_fc2, rel_table, cotangent):
    both = ("fsdp", "win")
    fast = D // nz == TL and FF // nw % TL == 0 and D // nw % 16 == 0 and nw > 1 and nz > 1
    fast = fast and nw & (nw - 1) == 0 and nz & (nz - 1) == 0
    place = offset_place()
    table = jnp.pad(rel_table.T, ((0, 0), (0, TT - TABLE)))
    dev = lax.axis_index(both)
    own, own1 = D // (nw * nz), FF // (nw * nz)
    if fast:
        geo = Geometry(nw, nz)
        me = jnp.stack([lax.axis_index("win"), lax.axis_index("fsdp")]).astype(jnp.int32)
        buf_a = pack((geo.rows_a + EXTRA, TL), w_qkv, vectors, fc1_bias.reshape(1, -1))
        buf_b = pack((geo.blocks, geo.r, TL), w_proj, w_fc1, w_fc2)
        mine_a = gather_z(buf_a, nz)
        pb = bias(table, place)
        planes_a = gather_xy(mine_a, nw)
        mine_b = gather_z(buf_b, nz)
        bufs_a = gather_core(planes_a, nw)
        planes_b = gather_xy(mine_b, nw)
        own_core = swap(planes_b[0], "win", nw, 1)
        xh, q, k, v, p, att, vec, b1 = attn_fwd(geo, me, tokens, pb, bufs_a)
        rest = lax.optimization_barrier((*planes_b[1:], att))[:-1]
        bufs_b = [planes_b[0], own_core] + gather_core(rest, nw)
        out, dx1, da, gv2, gb1, *gw = mlp(geo, me, live, tokens, cotangent, att, bufs_b, vec, b1)
        sums_b = sum_core(gw, nw)
        parts_b = swap_xy(sums_b, nw)
        gv2 = after(gv2, *sums_b)
        dc, _, *gq = attn_bwd(geo, me, q, k, v, p, da, xh, vec, gv2, gb1, place, bufs_a)
        res = lax.optimization_barrier((*parts_b, *gq))
        parts_b, gq = res[: len(parts_b)], res[len(parts_b) :]
        low_b = sum_xy(parts_b)
        sums_a = sum_core(gq, nw)
        parts_a = swap_xy(sums_a, nw)
        held = after(low_b, *sums_a)
        own_b = [swap((low_b if e == nz - 1 else held)[e], "fsdp", nz, e) for e in range(1, nz)]
        grad_tokens = input_bwd(geo, me, tokens, dc, dx1, after(vec, *sums_a), bufs_a)
        parts_a = lax.optimization_barrier((*parts_a, grad_tokens))[:-1]
        low_a = sum_xy(parts_a)
        tail = low_a[:, geo.rows_a :].reshape(nz * EXTRA, TL)
        own_a = [swap(jnp.concatenate([low_a[e], tail], 0), "fsdp", nz, e) for e in range(1, nz)]
        grad_qkv, grad_proj, grad_one, grad_two, grad_vectors, grad_bias, grad_table = finish(
            geo, nw, nz, me, low_a, low_b, own_b, own_a
        )
        grad_bias = grad_bias.reshape(-1)
        grad_table = grad_table.T
    else:
        geo = Geometry(1, 1)
        me = jnp.zeros((2,), jnp.int32)

        def full(w):
            return lax.all_gather(lax.all_gather(w, "fsdp", axis=1, tiled=True), "win", axis=0, tiled=True)

        bufs_a = [slabs(full(w_qkv))[None]]
        bufs_b = [jnp.concatenate([slabs(full(w)) for w in (w_proj, w_fc1, w_fc2)], 0).reshape(1, geo.blocks, D, TL)]
        vec = lax.all_gather(vectors, both, axis=1, tiled=True)
        b1 = lax.all_gather(fc1_bias, both, axis=0, tiled=True).reshape(1, -1)
        pb = bias(table, place)
        xh, q, k, v, p, att = attn_fwd(geo, me, tokens, pb, bufs_a, vec)
        out, dx1, da, gv2, gb1, gw = mlp(geo, me, live, tokens, cotangent, att, bufs_b, vec, b1)
        dc, small, gq = attn_bwd(geo, me, q, k, v, p, da, xh, vec, gv2, gb1, place, bufs_a)
        grad_tokens = input_bwd(geo, me, tokens, dc, dx1, vec, bufs_a)

        def down(g):
            g = lax.psum_scatter(g.astype(bf16), "win", scatter_dimension=0, tiled=True)
            return lax.psum_scatter(g, "fsdp", scatter_dimension=1, tiled=True).astype(f32)

        grad_qkv = down(unslab(gq[0], geo.cq))
        grad_proj, grad_one, grad_two = [down(g) for g in split_b(geo, gw[0])]
        small = lax.psum(small, both)
        grad_vectors = lax.dynamic_slice_in_dim(small[:8], dev * own, own, 1)
        grad_bias = lax.dynamic_slice_in_dim(small[8:, TT:].reshape(FF), dev * own1, own1, 0)
        grad_table = small[8:, :TABLE].T
    return out, grad_tokens, grad_vectors, grad_bias, grad_qkv, grad_proj, grad_one, grad_two, grad_table


def solution(mesh):
    split = P(("fsdp", "win"), None, None)
    vecs = P(None, ("fsdp", "win"))
    flat = P(("fsdp", "win"))
    cut = P("win", "fsdp")
    return jax.shard_map(
        functools.partial(body, mesh.shape["win"], mesh.shape["fsdp"]),
        mesh=mesh,
        in_specs=(split, flat, vecs, flat, cut, cut, cut, cut, P(), split),
        out_specs=(split, split, vecs, flat, cut, cut, cut, cut, P()),
        check_vma=False,
    )
```

```python
import functools

import jax
import jax.numpy as jnp
import numpy as np
from jax import lax
from jax.experimental import pallas as pl
from jax.experimental.pallas import tpu as pltpu
from jax.sharding import PartitionSpec as P

f32 = jnp.float32
bf16 = jnp.bfloat16
HEADS = 16
HD = 32
WS = 10
WT = WS * WS
D = HEADS * HD
FF = 4 * D
SIDE = 2 * WS - 1
TABLE = SIDE * SIDE
TP = 112
TL = 128
TT = 384
GH = 4
NG = HEADS // GH
EPS = 1e-5
SCALE = HD**-0.5
EXTRA = 32
NN = (((1,), (0,)), ((), ()))
NT = (((1,), (1,)), ((), ()))
TN = (((0,), (0,)), ((), ()))


def dot(a, b, dims=NN):
    return lax.dot_general(a, b, dims, preferred_element_type=f32)


def params(mib):
    return pltpu.CompilerParams(dimension_semantics=("arbitrary",), vmem_limit_bytes=mib * 2**20)


def cost(us):
    return pl.CostEstimate(flops=int(us * 1.1e9), bytes_accessed=int(us * 1e6), transcendentals=0)


def whole(shape):
    n = len(shape)
    return pl.BlockSpec(shape, lambda *a: (0,) * n, pipeline_mode=pl.Buffered(1))


def smem():
    return pl.BlockSpec(memory_space=pltpu.SMEM)


def anyspace():
    return pl.BlockSpec(memory_space=pl.ANY)


def three(x):
    hi = x.astype(bf16)
    rest = x - hi.astype(f32)
    mid = rest.astype(bf16)
    return hi, mid, (rest - mid.astype(f32)).astype(bf16)


def offset_place():
    cj = np.arange(WS)[:, None, None]
    r = np.arange(TT)[None, :, None]
    l = np.arange(256)[None, None, :]
    hit = (l < SIDE * WS) & (r == (l // WS) * SIDE + (l % WS) - cj + WS - 1)
    return jnp.asarray(hit, bf16)


class Geometry:
    def __init__(self, nw, nz):
        self.nw, self.nz = nw, nz
        self.r = D // nw
        self.cq, self.cp, self.c1 = 3 * D // nz // TL, D // nz // TL, FF // nz // TL
        self.r2 = FF // nw
        self.rows_a = self.cq * self.r
        self.blocks = self.c1 + 5 * self.cp
        self.cores = 2 if nw > 1 else 1


def slabs(x):
    return jnp.concatenate([x[:, i : i + TL] for i in range(0, x.shape[1], TL)], 0)


def pack_body(count, *refs):
    srcs, out = refs[:count], refs[count]
    rest = refs[count + 1 :]
    stage, flat, sem = rest[:count], rest[-2], rest[-1]
    moves = [pltpu.make_async_copy(x, y, sem.at[i]) for i, (x, y) in enumerate(zip(srcs, stage))]
    for m in moves:
        m.start()
    parts = []
    r = flat.shape[-2]
    at = 0
    for m, w in zip(moves, stage):
        m.wait()
        if w.dtype == f32:
            part = [p.astype(f32) for p in three(w[...])]
            parts += [jnp.concatenate([p, jnp.zeros((p.shape[0], TL - p.shape[1]), f32)], 1) for p in part]
            continue
        for i in range(0, w.shape[1], TL):
            if len(flat.shape) == 2:
                flat[at : at + w.shape[0], :] = w[:, i : i + TL]
                at += w.shape[0]
                continue
            for k in range(0, w.shape[0], r):
                flat[at] = w[k : k + r, i : i + TL]
                at += 1
    if parts:
        used = sum(p.shape[0] for p in parts)
        flat[at : at + EXTRA, :] = jnp.concatenate(parts + [jnp.zeros((EXTRA - used, TL), f32)], 0).astype(bf16)
    last = pltpu.make_async_copy(flat, out, sem.at[count])
    last.start()
    last.wait()


def pack(shape, *arrays):
    V = pltpu.VMEM
    return pl.pallas_call(
        functools.partial(pack_body, len(arrays)),
        in_specs=[anyspace()] * len(arrays),
        out_specs=anyspace(),
        out_shape=jax.ShapeDtypeStruct(shape, bf16),
        scratch_shapes=[V(x.shape, x.dtype) for x in arrays]
        + [V(shape, bf16), pltpu.SemaphoreType.DMA((len(arrays) + 1,))],
        compiler_params=pltpu.CompilerParams(vmem_limit_bytes=60 * 2**20),
        cost_estimate=cost(2),
        name="pack",
    )(*arrays)


def copies_a(geo, bufs, me, wq, sem):
    out = []
    for d in range(geo.nw):
        row = pl.multiple_of((me[0] ^ d) * geo.r, geo.r)
        for e in range(geo.nz):
            col = (me[1] ^ e) * geo.cq
            for i in range(geo.cq):
                out.append(
                    pltpu.make_async_copy(
                        bufs[d].at[e, pl.ds(i * geo.r, geo.r), :],
                        wq.at[col + i, pl.ds(row, geo.r), :],
                        sem,
                    )
                )
    return out


def copies_b(geo, bufs, me, wp, w1, w2, sem):
    out = []
    for d in range(geo.nw):
        w = me[0] ^ d
        row = pl.multiple_of(w * geo.r, geo.r)
        for e in range(geo.nz):
            z = me[1] ^ e
            for ref, at, n in ((wp, 0, geo.cp), (w1, geo.cp, geo.c1)):
                src = bufs[d].at[e, pl.ds(at, n)]
                out.append(pltpu.make_async_copy(src, ref.at[pl.ds(z * n, n), pl.ds(row, geo.r), :], sem))
            for i in range(geo.cp):
                src = bufs[d].at[e, pl.ds(geo.cp + geo.c1 + 4 * i, 4)]
                out.append(pltpu.make_async_copy(src, w2.at[z * geo.cp + i, pl.ds(w * 4, 4)], sem))
    return out


def wide(ref, lo, n):
    return jnp.concatenate([ref[lo + i] for i in range(n)], 1)


def strided(ref, first, count, step):
    return jnp.concatenate([ref[half, pl.ds(first, count, stride=step), :] for half in range(2)], 1)


def bias_body(table, place, pb_o, zs):
    parts = jnp.concatenate([p for p in three(table[...])], 0)
    for cj in range(WS):
        z = dot(parts, place[cj])
        z = z[:HEADS] + z[HEADS : 2 * HEADS] + z[2 * HEADS :]
        for half in range(2):
            zs[half, cj * HEADS : (cj + 1) * HEADS, :] = z[:, half * TL : (half + 1) * TL]
    for j in range(NG):
        pb_o[j, WT:TP, :] = jnp.zeros((TP - WT, GH * TL), f32)
        for h in range(GH):
            zh = strided(zs, j * GH + h, WS, HEADS)
            for rj in range(WS):
                off = (WS - 1 - rj) * WS
                part = zh if off == 0 else pltpu.roll(zh, 256 - off, 1)
                pb_o[j, rj * WS : (rj + 1) * WS, h * TL : (h + 1) * TL] = jnp.exp(part[:, :TL])


def bias(table, place):
    return pl.pallas_call(
        bias_body,
        out_shape=jax.ShapeDtypeStruct((NG, TP, GH * TL), f32),
        scratch_shapes=[pltpu.VMEM((2, WS * HEADS, TL), f32)],
        compiler_params=pltpu.CompilerParams(vmem_limit_bytes=24 * 2**20),
        cost_estimate=cost(4),
        name="position_bias",
    )(table, place)


def table_sum(gt, place, rs):
    for j in range(NG):
        for h in range(GH):
            total = None
            for rj in range(WS):
                part = gt[j, rj * WS : (rj + 1) * WS, h * TL : (h + 1) * TL]
                part = jnp.concatenate([part, jnp.zeros((WS, TL), f32)], 1)
                off = (WS - 1 - rj) * WS
                part = part if off == 0 else pltpu.roll(part, off, 1)
                total = part if total is None else total + part
            base = (j * GH + h) * 16
            for half in range(2):
                rs[half, base : base + WS, :] = total[:, half * TL : (half + 1) * TL]
    columns = jnp.concatenate([strided(rs, cj, HEADS, 16) for cj in range(WS)], 1)
    z = dot(jnp.concatenate(three(columns), 0), jnp.concatenate([place[cj] for cj in range(WS)], 1), NT)
    return z[:HEADS] + z[HEADS : 2 * HEADS] + z[2 * HEADS :]


def norm(x):
    mean = jnp.sum(x, -1, keepdims=True) * (1.0 / D)
    c = x - mean
    var = jnp.sum(c * c, -1, keepdims=True) * (1.0 / D)
    r = lax.rsqrt(var + EPS)
    return c * r, r


def norm_back(dn, xhat, r, gain):
    t = dn * gain
    m1 = jnp.sum(t, -1, keepdims=True) * (1.0 / D)
    m2 = jnp.sum(t * xhat, -1, keepdims=True) * (1.0 / D)
    return (t - m1 - xhat * m2) * r


def spread(part):
    lane = lax.broadcasted_iota(jnp.int32, (1, TL), 1) // HD
    none = jnp.zeros((TL - TP, TL), part.dtype)
    return jnp.concatenate([x for h in range(GH) for x in (jnp.where(lane == h, part, jnp.zeros_like(part)), none)], 0)


def diag_t(full):
    return jnp.concatenate([full[h * HD : (h + 1) * HD, h * TL : (h + 1) * TL] for h in range(GH)], 0)


def gather_vectors(bufs, geo, me, vec_o, b1_o, tmp):
    own = D // (geo.nw * geo.nz)
    own1 = FF // (geo.nw * geo.nz)
    i32 = jnp.int32
    pick = (lax.broadcasted_iota(i32, (TL, D), 0) == lax.broadcasted_iota(i32, (TL, D), 1) % own).astype(bf16)
    pick1 = (lax.broadcasted_iota(i32, (TL, FF), 0) == lax.broadcasted_iota(i32, (TL, FF), 1) % own1).astype(bf16)
    slot = lax.broadcasted_iota(i32, (1, D), 1) // own
    slot1 = lax.broadcasted_iota(i32, (1, FF), 1) // own1
    vec = jnp.zeros((8, D), f32)
    b1 = jnp.zeros((8, FF), f32)
    for d in range(geo.nw):
        for e in range(geo.nz):
            dev = (me[1] ^ e) * geo.nw + (me[0] ^ d)
            x = tmp[d, e]
            y = dot(x[:24], pick)
            vec = vec + jnp.where(slot == dev, y[:8] + y[8:16] + y[16:24], 0.0)
            y1 = dot(x[24:], pick1)
            b1 = b1 + jnp.where(slot1 == dev, y1, 0.0)
    vec_o[...] = vec
    b1_o[...] = b1[0:1] + b1[1:2] + b1[2:3]


def attn_fwd_body(geo, G, vectors_in, *refs):
    nb = geo.nw
    me, tok, pb = refs[:3]
    bufs = refs[3 : 3 + nb]
    refs = refs[3 + nb :]
    if vectors_in:
        vec, refs = refs[0], refs[1:]
    n1_o, q_o, k_o, v_o, p_o, a_o = refs[:6]
    refs = refs[6:]
    if not vectors_in:
        vec, b1_o = refs[:2]
        refs = refs[2:]
    xs, wq, tmp, sem, sem2 = refs

    @pl.when(pl.program_id(0) == 0)
    def _():
        moves = copies_a(geo, bufs, me, wq, sem)
        for m in moves:
            m.start()
        if not vectors_in:
            small = [
                pltpu.make_async_copy(bufs[d].at[:, pl.ds(geo.rows_a, EXTRA), :], tmp.at[d], sem2)
                for d in range(geo.nw)
            ]
            for m in small:
                m.start()
        xs[...] = jnp.zeros_like(xs)
        if not vectors_in:
            for m in small:
                m.wait()
            gather_vectors(bufs, geo, me, vec, b1_o, tmp)
        for m in moves:
            m.wait()

    for g in range(G):
        xs[g * TP : g * TP + WT, :] = tok[g].astype(f32)
        xs[g * TP + WT : (g + 1) * TP, :] = tok[g, : TP - WT, :].astype(f32)
    xhat, _ = norm(xs[...])
    n1 = (xhat * vec[0:1, :] + vec[1:2, :]).astype(bf16)
    n1_o[...] = xhat.astype(bf16)
    q_o[...] = ((dot(n1, wide(wq, 0, NG)) + vec[2:3, :]) * SCALE).astype(bf16)
    k_o[...] = dot(n1, wide(wq, NG, NG)).astype(bf16)
    v_o[...] = (dot(n1, wide(wq, 2 * NG, NG)) + vec[3:4, :]).astype(bf16)

    def window(g, carry):
        rows = pl.ds(pl.multiple_of(g * TP, 16), TP)
        cols = [slice(j * TL, (j + 1) * TL) for j in range(NG)]
        ks = [k_o[rows, c] for c in cols]
        vs = [v_o[rows, c] for c in cols]
        qs = [spread(q_o[rows, c]) for c in cols]
        scores = [dot(ks[j], qs[j], NT) for j in range(NG)]
        ps, outs = [], []
        for j in range(NG):
            s = scores[j]
            e = jnp.exp(s - jnp.max(s, 0, keepdims=True)) * pb[j]
            p = (e * (1.0 / jnp.sum(e, 0, keepdims=True))).astype(bf16)
            ps.append(p)
            outs.append(diag_t(dot(vs[j], p, TN)).T[:TP].astype(bf16))
        for j in range(NG):
            p_o[g, j] = ps[j]
            a_o[rows, cols[j]] = outs[j]
        return carry

    lax.fori_loop(0, G, window, 0, unroll=G)


def attn_fwd(geo, me, tok, pb, bufs, vec=None, G=4):
    B = tok.shape[0]
    R = B * TP
    S = jax.ShapeDtypeStruct
    act = S((R, D), bf16)
    blk = pl.BlockSpec((G * TP, D), lambda i: (i, 0))
    given = [] if vec is None else [vec]
    out_specs = [blk, blk, blk, blk, pl.BlockSpec((G, NG, TP, GH * TL), lambda i: (i, 0, 0, 0)), blk]
    out_shape = [act, act, act, act, S((B, NG, TP, GH * TL), bf16), act]
    if vec is None:
        out_specs += [whole((8, D)), whole((1, FF))]
        out_shape += [S((8, D), f32), S((1, FF), f32)]
    return pl.pallas_call(
        functools.partial(attn_fwd_body, geo, G, vec is not None),
        grid=(B // G,),
        in_specs=[smem(), pl.BlockSpec((G, WT, D), lambda i: (i, 0, 0)), whole(pb.shape)]
        + [anyspace()] * len(bufs)
        + [whole(g.shape) for g in given],
        out_specs=out_specs,
        out_shape=out_shape,
        scratch_shapes=[
            pltpu.VMEM((G * TP, D), f32),
            pltpu.VMEM((3 * NG, D, TL), bf16),
            pltpu.VMEM((geo.nw, geo.nz, EXTRA, TL), bf16),
            pltpu.SemaphoreType.DMA,
            pltpu.SemaphoreType.DMA,
        ],
        compiler_params=params(28),
        cost_estimate=cost(30),
        name="attn_fwd",
    )(me, tok, pb, *bufs, *given)


GC = 0.7978845608028654
GA = 0.044715


def gelu_both(u):
    u2 = u * u
    t = jnp.tanh(u * (GC + (GC * GA) * u2))
    h = 0.5 + 0.5 * t
    act = u * h
    slope = h + (act * (2.0 - 2.0 * h)) * (GC + (3.0 * GC * GA) * u2)
    return act, slope


def scatter_out(geo, me, blocks, outs):
    cores = geo.cores
    for c in range(cores):
        for xy in range(geo.nw // cores):
            w = me[0] ^ (xy * cores + c)
            for e in range(geo.nz):
                z = me[1] ^ e
                at = 0
                for ref, pick in blocks:
                    for part in pick(ref, w, z):
                        outs[c * (geo.nw // cores) + xy][e, at : at + part.shape[0], :] = part.astype(bf16)
                        at += part.shape[0]


def mlp_body(geo, G, FC, *refs):
    nb = geo.nw
    me, live, tok, cot, attn = refs[:5]
    bufs = refs[5 : 5 + nb]
    vec, b1 = refs[5 + nb : 7 + nb]
    refs = refs[7 + nb :]
    out_o, dx1_o, da_o, gv_o, gb1_o = refs[:5]
    outs = refs[5 : 5 + geo.nw]
    xs, dys, gp, g1, g2, gv, gb1, acc, dn2, wp, w1, w2, sem = refs[5 + geo.nw :]
    i = pl.program_id(0)
    n = pl.num_programs(0)

    @pl.when(i == 0)
    def _():
        moves = copies_b(geo, bufs, me, wp, w1, w2, sem)
        for m in moves:
            m.start()
        for ref in (xs, dys, gp, g1, g2, gv, gb1):
            ref[...] = jnp.zeros_like(ref)
        for m in moves:
            m.wait()

    for g in range(G):
        xs[g * TP : g * TP + WT, :] = tok[g].astype(f32)
        mask = (i * G + g < live[0]).astype(f32)
        dys[g * TP : g * TP + WT, :] = cot[g].astype(f32) * mask
    at = attn[...]
    wpv = wide(wp, 0, NG)
    x1 = xs[...] + dot(at, wpv) + vec[4:5, :]
    acc[...] = x1 + vec[7:8, :]
    xhat, r = norm(x1)
    n2 = (xhat * vec[5:6, :] + vec[6:7, :]).astype(bf16)
    n2t = n2.T
    dyf = dys[...]
    dy = dyf.astype(bf16)
    dyt = dy.T
    ns = FC // TL
    n = FF // FC

    def first(c):
        cols = slice(c * FC, (c + 1) * FC)
        w1c = wide(w1, c * ns, ns)
        w2c = jnp.concatenate([w2[z, cols.start // geo.r : cols.stop // geo.r].reshape(FC, TL) for z in range(NG)], 1)
        return w1c, w2c, dot(n2, w1c), dot(dy, w2c, NT)

    def last(c):
        cols = slice(c * FC, (c + 1) * FC)
        w1c, w2c = work[c][:2]
        a, du = mids[c]
        acc[...] += dot(a, w2c)
        t2 = dot(dyt, a)
        t1 = dot(n2t, du)
        for k in range(ns):
            g2[c * ns + k] += t2[:, k * TL : (k + 1) * TL]
            g1[c * ns + k] += t1[:, k * TL : (k + 1) * TL]
        gb1[:, cols] += jnp.sum(du.astype(f32), 0, keepdims=True)
        d = dot(du, w1c, NT)
        if c == 0:
            dn2[...] = d
        else:
            dn2[...] += d

    work = [first(c) for c in range(1)]
    mids = []
    for c in range(n + 1):
        if c + 1 < n:
            work.append(first(c + 1))
        if c < n:
            a, ga = gelu_both(work[c][2] + b1[:, c * FC : (c + 1) * FC])
            mids.append((a.astype(bf16), (work[c][3] * ga).astype(bf16)))
        if c >= 1:
            last(c - 1)
    n = pl.num_programs(0)
    for g in range(G):
        mask = (i * G + g < live[0]).astype(f32)
        out_o[g] = (acc[g * TP : g * TP + WT, :] * mask).astype(bf16)
    dn = dn2[...]
    gv[7:8, :] += jnp.sum(dyf, 0, keepdims=True)
    gv[5:6, :] += jnp.sum(dn * xhat, 0, keepdims=True)
    gv[6:7, :] += jnp.sum(dn, 0, keepdims=True)
    dx1 = dyf + norm_back(dn, xhat, r, vec[5:6, :])
    dx1_o[...] = dx1
    dl = dx1.astype(bf16)
    gv[4:5, :] += jnp.sum(dl.astype(f32), 0, keepdims=True)
    tp = dot(at.T, dl)
    for k in range(NG):
        gp[k] += tp[:, k * TL : (k + 1) * TL]
    da_o[...] = dot(dl, wpv, NT).astype(bf16)

    @pl.when(i == n - 1)
    def _():
        gv_o[...] = gv[...]
        gb1_o[...] = gb1[...]

        def rows(ref, n):
            def pick(ref, w, z):
                at = pl.multiple_of(w * geo.r, geo.r)
                return [ref[z * n + k, pl.ds(at, geo.r), :] for k in range(n)]

            return ref, pick

        def turned(ref, w, z):
            n, r = geo.r2 // TL, D // geo.nz
            at = pl.multiple_of(z * r, r)
            return [ref[w * n + k, pl.ds(at, r), :] for k in range(n)]

        scatter_out(geo, me, [rows(gp, geo.cp), rows(g1, geo.c1), (g2, turned)], outs)


def mlp(geo, me, live, tok, cot, attn, bufs, vec, b1, G=4, FC=512):
    B = tok.shape[0]
    R = B * TP
    M = G * TP
    blk = pl.BlockSpec((M, D), lambda i: (i, 0))
    win = pl.BlockSpec((G, WT, D), lambda i: (i, 0, 0))
    S = jax.ShapeDtypeStruct
    gshape = (geo.nz, geo.blocks * geo.r, TL)
    V = pltpu.VMEM
    return pl.pallas_call(
        functools.partial(mlp_body, geo, G, FC),
        grid=(B // G,),
        in_specs=[smem(), smem(), win, win, blk] + [anyspace()] * len(bufs) + [whole(vec.shape), whole(b1.shape)],
        out_specs=[win, blk, blk, whole((8, D)), whole((1, FF))] + [whole(gshape)] * geo.nw,
        out_shape=[S(tok.shape, bf16), S((R, D), f32), S((R, D), bf16), S((8, D), f32), S((1, FF), f32)]
        + [S(gshape, bf16)] * geo.nw,
        scratch_shapes=[
            V((M, D), f32),
            V((M, D), f32),
            V((NG, D, TL), f32),
            V((FF // TL, D, TL), f32),
            V((FF // TL, D, TL), f32),
            V((8, D), f32),
            V((1, FF), f32),
            V((M, D), f32),
            V((M, D), f32),
            V((NG, D, TL), bf16),
            V((FF // TL, D, TL), bf16),
            V((NG, FF // geo.r, geo.r, TL), bf16),
            pltpu.SemaphoreType.DMA,
        ],
        compiler_params=params(44),
        cost_estimate=cost(44),
        name="mlp",
    )(me, live, tok, cot, attn, *bufs, vec, b1)


def attn_bwd_body(geo, G, *refs):
    nb = geo.nw
    me, q, k, v, p, da, xh, vec, gv2, gb1, place = refs[:11]
    bufs = refs[11 : 11 + nb]
    refs = refs[11 + nb :]
    dc_o, small_o = refs[:2]
    outs = refs[2 : 2 + geo.nw]
    gq, gb, gt, wq, rs, ex, sem = refs[2 + geo.nw :]
    i = pl.program_id(0)
    n = pl.num_programs(0)

    @pl.when(i == 0)
    def _():
        for m in copies_a(geo, bufs, me, wq, sem):
            m.start()
        for ref in (gq, gb, gt):
            ref[...] = jnp.zeros_like(ref)

    def window(g, carry):
        rows = pl.ds(pl.multiple_of(g * TP, 16), TP)
        cols = [slice(j * TL, (j + 1) * TL) for j in range(NG)]
        ks = [k[rows, c] for c in cols]
        vs = [v[rows, c] for c in cols]
        bqs = [spread(q[rows, c]) for c in cols]
        bas = [spread(da[rows, c]) for c in cols]
        dps = [dot(vs[i], bas[i], NT) for i in range(2)]
        dqs, dks, dvs, dss = [], [], [], []
        pts = []
        for j in range(NG + 1):
            if j + 2 < NG:
                dps.append(dot(vs[j + 2], bas[j + 2], NT))
            if j < NG:
                pts.append(p[g, j])
                pf = pts[j].astype(f32)
                t = pf * dps[j]
                dss.append((t - pf * jnp.sum(t, 0, keepdims=True)).astype(bf16))
            if 0 <= j - 0 < NG:
                i = j - 0
                dvs.append(dot(pts[i], bas[i]).astype(bf16))
            if 0 <= j - 1 < NG:
                i = j - 1
                dks.append(dot(dss[i], bqs[i]).astype(bf16))
                dqs.append((diag_t(dot(ks[i], dss[i], TN)).T[:TP] * SCALE).astype(bf16))
        for j in range(NG):
            gt[j] += dss[j].astype(f32)
            dc_o[rows, j * TL : (j + 1) * TL] = dqs[j]
            dc_o[rows, D + j * TL : D + (j + 1) * TL] = dks[j]
            dc_o[rows, 2 * D + j * TL : 2 * D + (j + 1) * TL] = dvs[j]
        return carry

    lax.fori_loop(0, G, window, 0, unroll=G)
    xt = xh[...].T
    for c in range(3):
        cols = slice(c * D, (c + 1) * D)
        dc = dc_o[:, cols]
        t = dot(xt, dc)
        for s in range(NG):
            gq[c * NG + s] += t[:, s * TL : (s + 1) * TL]
        gb[:, cols] += jnp.sum(dc.astype(f32), 0, keepdims=True)

    @pl.when(i == n - 1)
    def _():
        for m in copies_a(geo, bufs, me, wq, sem):
            m.wait()
        sums = gb[...]
        g_col = jnp.broadcast_to(vec[0:1, :], (TL, D)).T
        s_col = jnp.broadcast_to(vec[1:2, :], (TL, D)).T
        gain = jnp.zeros((D, TL), f32)
        shift = jnp.zeros((D, TL), f32)
        for s in range(3 * NG):
            part = gq[s]
            w = wq[s].astype(f32)
            total = sums[:, s * TL : (s + 1) * TL]
            gain = gain + part * w
            shift = shift + w * total
            gq[s] = part * g_col + s_col * total
        gain = jnp.sum(gain.T, 0, keepdims=True)
        shift = jnp.sum(shift.T, 0, keepdims=True)
        small_o[0:1, :] = gain
        small_o[1:2, :] = shift
        small_o[2:3, :] = sums[:, :D]
        small_o[3:4, :] = sums[:, 2 * D :]
        small_o[4:8, :] = gv2[4:8, :]
        small_o[8:24, :TT] = table_sum(gt, place, rs)
        for k in range(FF // TL):
            small_o[8 + k : 9 + k, TT:] = gb1[:, k * TL : (k + 1) * TL]

        if nb > 1:
            for z in range(geo.nz):
                ex[z] = extra_rows(geo, small_o, gb1, z)

        def rows(ref, w, z):
            at = pl.multiple_of(w * geo.r, geo.r)
            parts = [ref[z * geo.cq + s, pl.ds(at, geo.r), :] for s in range(geo.cq)]
            return parts if nb == 1 else parts + [ex[z]]

        scatter_out(geo, me, [(gq, rows)], outs)


def extra_rows(geo, small, gb1, z):
    nh = HEADS // geo.nz
    vec = small[0:8, z * TL : (z + 1) * TL]
    first = z * (FF // geo.nz)
    bias = [gb1[:, first + k * TL : first + (k + 1) * TL] for k in range(FF // geo.nz // TL)]
    table = [small[8 + z * nh : 8 + (z + 1) * nh, k * TL : (k + 1) * TL] for k in range(TT // TL)]
    rows = [vec] + bias + table
    used = sum(r.shape[0] for r in rows)
    return jnp.concatenate(rows + [jnp.zeros((EXTRA - used, TL), f32)], 0)


def attn_bwd(geo, me, q, k, v, p, da, xh, vec, gv2, gb1, place, bufs, G=4):
    R = q.shape[0]
    B = R // TP
    blk = pl.BlockSpec((G * TP, D), lambda i: (i, 0))
    S = jax.ShapeDtypeStruct
    V = pltpu.VMEM
    gshape = (geo.nz, geo.rows_a + (EXTRA if geo.cores == 2 else 0), TL)
    return pl.pallas_call(
        functools.partial(attn_bwd_body, geo, G),
        grid=(B // G,),
        in_specs=[smem(), blk, blk, blk, pl.BlockSpec((G, NG, TP, GH * TL), lambda i: (i, 0, 0, 0)), blk, blk]
        + [whole(x.shape) for x in (vec, gv2, gb1, place)]
        + [anyspace()] * len(bufs),
        out_specs=[pl.BlockSpec((G * TP, 3 * D), lambda i: (i, 0)), whole((24, D))] + [whole(gshape)] * geo.nw,
        out_shape=[S((R, 3 * D), bf16), S((24, D), f32)] + [S(gshape, bf16)] * geo.nw,
        scratch_shapes=[
            V((3 * NG, D, TL), f32),
            V((1, 3 * D), f32),
            V((NG, TP, GH * TL), f32),
            V((3 * NG, D, TL), bf16),
            V((2, HEADS * 16, TL), f32),
            V((geo.nz, EXTRA, TL), f32),
            pltpu.SemaphoreType.DMA,
        ],
        compiler_params=params(32),
        cost_estimate=cost(30),
        name="attn_bwd",
    )(me, q, k, v, p, da, xh, vec, gv2, gb1, place, *bufs)


def input_bwd_body(geo, G, *refs):
    nb = geo.nw
    me, tok, dc, dx1, vec = refs[:5]
    bufs = refs[5 : 5 + nb]
    gt_o, xs, wq, sem = refs[5 + nb :]

    @pl.when(pl.program_id(0) == 0)
    def _():
        moves = copies_a(geo, bufs, me, wq, sem)
        for m in moves:
            m.start()
        xs[...] = jnp.zeros_like(xs)
        for m in moves:
            m.wait()

    for g in range(G):
        xs[g * TP : g * TP + WT, :] = tok[g].astype(f32)
    dn = dot(dc[...], wide(wq, 0, 3 * NG), NT)
    xhat, r = norm(xs[...])
    dx = dx1[...] + norm_back(dn, xhat, r, vec[0:1, :])
    for g in range(G):
        gt_o[g] = dx[g * TP : g * TP + WT].astype(bf16)


def input_bwd(geo, me, tok, dc, dx1, vec, bufs, G=4):
    B = tok.shape[0]
    blk = pl.BlockSpec((G * TP, D), lambda i: (i, 0))
    win = pl.BlockSpec((G, WT, D), lambda i: (i, 0, 0))
    S = jax.ShapeDtypeStruct
    V = pltpu.VMEM
    return pl.pallas_call(
        functools.partial(input_bwd_body, geo, G),
        grid=(B // G,),
        in_specs=[smem(), win, pl.BlockSpec((G * TP, 3 * D), lambda i: (i, 0)), blk, whole(vec.shape)]
        + [anyspace()] * len(bufs),
        out_specs=win,
        out_shape=S(tok.shape, bf16),
        scratch_shapes=[V((G * TP, D), f32), V((3 * NG, D, TL), bf16), pltpu.SemaphoreType.DMA],
        compiler_params=params(24),
        cost_estimate=cost(10),
        name="input_bwd",
    )(me, tok, dc, dx1, vec, *bufs)


def finish_body(geo, nz, *refs):
    me, low_a, low_b = refs[:3]
    got_b = refs[3 : 2 + nz]
    got_a = refs[2 + nz : 1 + 2 * nz]
    gq_o, gp_o, g1_o, g2_o, vec_o, b1_o, tab_o, tab = refs[1 + 2 * nz :]
    r, r2 = geo.r, geo.r2
    rows = geo.rows_a + EXTRA

    def total(low, got, lo, n):
        out = low[0, lo : lo + n, :].astype(f32)
        for x in got:
            out = out + x[lo : lo + n, :].astype(f32)
        return out

    for i in range(geo.cq):
        gq_o[:, i * TL : (i + 1) * TL] = total(low_a, got_a, i * r, r)
    at = 0
    for ref, n in ((gp_o, geo.cp), (g1_o, geo.c1)):
        for i in range(n):
            ref[:, i * TL : (i + 1) * TL] = total(low_b, got_b, at, r)
            at += r
    wide_z = D // nz
    for k in range(r2 // TL):
        g2_o[k * TL : (k + 1) * TL, :] = total(low_b, got_b, at, wide_z).T
        at += wide_z
    nb = FF // nz // TL
    small = total(low_a, got_a, geo.rows_a, 16)
    own, own1 = vec_o.shape[1], b1_o.shape[1]
    vec_o[...] = pltpu.roll(small[:8], (TL - me[0] * own) % TL, 1)[:, :own]
    first = me[0] * own1
    b1 = pltpu.roll(small[8 : 8 + nb], (TL - first % TL) % TL, 1)
    row = lax.broadcasted_iota(jnp.int32, b1.shape, 0) == first // TL
    b1_o[...] = jnp.sum(jnp.where(row, b1, 0.0), 0, keepdims=True)[:, :own1]
    nh = HEADS // nz
    lo = 8 + nb
    for e in range(nz):
        t = low_a[e, geo.rows_a : rows, :].astype(f32)
        for d in range(1, nz):
            t = t + got_a[d - 1][rows + (e ^ d) * EXTRA : rows + ((e ^ d) + 1) * EXTRA, :].astype(f32)
        for k in range(TT // TL):
            tab[me[1] ^ e, :, k * TL : (k + 1) * TL] = t[lo + k * nh : lo + (k + 1) * nh]
    full = jnp.concatenate([tab[z] for z in range(nz)], 0)
    tab_o[...] = full[:, :TABLE]


def finish(geo, nw, nz, me, low_a, low_b, got_b, got_a):
    S = jax.ShapeDtypeStruct
    vmem = pl.BlockSpec(memory_space=pltpu.VMEM)
    return pl.pallas_call(
        functools.partial(finish_body, geo, nz),
        in_specs=[smem()] + [vmem] * (2 * nz),
        out_specs=[vmem] * 7,
        out_shape=[
            S((geo.r, geo.cq * TL), f32),
            S((geo.r, geo.cp * TL), f32),
            S((geo.r, geo.c1 * TL), f32),
            S((geo.r2, geo.cp * TL), f32),
            S((8, D // (nw * nz)), f32),
            S((1, FF // (nw * nz)), f32),
            S((HEADS, TABLE), f32),
        ],
        scratch_shapes=[pltpu.VMEM((nz, HEADS // nz, TT), f32)],
        compiler_params=pltpu.CompilerParams(vmem_limit_bytes=12 * 2**20),
        cost_estimate=cost(3),
        name="finish",
    )(me, low_a, low_b, *got_b, *got_a)


def swap(x, axis, size, d):
    return lax.ppermute(x, axis, [(i, i ^ d) for i in range(size)])


def after(x, *deps):
    return lax.optimization_barrier((x, *deps))[0]


def gather_z(buf, nz):
    return jnp.stack([buf] + [swap(buf, "fsdp", nz, e) for e in range(1, nz)])


def gather_xy(mine, nw):
    return [mine] + [swap(mine, "win", nw, 2 * d) for d in range(1, nw // 2)]


def gather_core(planes, nw):
    return [y for x in planes for y in (x, swap(x, "win", nw, 1))]


def sum_core(parts, nw):
    n = nw // 2
    out = [None] * n
    for d in reversed(range(n)):
        out[d] = (parts[d].astype(f32) + swap(parts[n + d], "win", nw, 1).astype(f32)).astype(bf16)
    return out


def swap_xy(sums, nw):
    return [sums[0]] + [swap(sums[d], "win", nw, 2 * d) for d in range(1, nw // 2)]


def sum_xy(parts):
    return functools.reduce(jnp.add, [x.astype(f32) for x in parts]).astype(bf16)


def swap_z(low, nz):
    return [swap(low[e], "fsdp", nz, e) for e in range(1, nz)]


def unslab(x, n):
    r = x.shape[0] // n
    return jnp.concatenate([x[i * r : (i + 1) * r] for i in range(n)], 1)


def split_b(geo, x):
    a, b = geo.cp * geo.r, (geo.cp + geo.c1) * geo.r
    two = x[b:].reshape(geo.r2 // TL, D // geo.nz, TL).transpose(0, 2, 1).reshape(geo.r2, D // geo.nz)
    return unslab(x[:a], geo.cp), unslab(x[a:b], geo.c1), two


def body(nw, nz, tokens, live, vectors, fc1_bias, w_qkv, w_proj, w_fc1, w_fc2, rel_table, cotangent):
    both = ("fsdp", "win")
    fast = D // nz == TL and FF // nw % TL == 0 and D // nw % 16 == 0 and nw > 1 and nz > 1
    fast = fast and nw & (nw - 1) == 0 and nz & (nz - 1) == 0
    place = offset_place()
    table = jnp.pad(rel_table.T, ((0, 0), (0, TT - TABLE)))
    dev = lax.axis_index(both)
    own, own1 = D // (nw * nz), FF // (nw * nz)
    if fast:
        geo = Geometry(nw, nz)
        me = jnp.stack([lax.axis_index("win"), lax.axis_index("fsdp")]).astype(jnp.int32)
        buf_a = pack((geo.rows_a + EXTRA, TL), w_qkv, vectors, fc1_bias.reshape(1, -1))
        buf_b = pack((geo.blocks, geo.r, TL), w_proj, w_fc1, w_fc2)
        mine_a = gather_z(buf_a, nz)
        pb = bias(table, place)
        planes_a = gather_xy(mine_a, nw)
        mine_b = gather_z(buf_b, nz)
        bufs_a = gather_core(planes_a, nw)
        planes_b = gather_xy(mine_b, nw)
        own_core = swap(planes_b[0], "win", nw, 1)
        xh, q, k, v, p, att, vec, b1 = attn_fwd(geo, me, tokens, pb, bufs_a)
        rest = lax.optimization_barrier((*planes_b[1:], att))[:-1]
        bufs_b = [planes_b[0], own_core] + gather_core(rest, nw)
        out, dx1, da, gv2, gb1, *gw = mlp(geo, me, live, tokens, cotangent, att, bufs_b, vec, b1)
        sums_b = sum_core(gw, nw)
        parts_b = swap_xy(sums_b, nw)
        gv2 = after(gv2, *sums_b)
        dc, _, *gq = attn_bwd(geo, me, q, k, v, p, da, xh, vec, gv2, gb1, place, bufs_a)
        res = lax.optimization_barrier((*parts_b, *gq))
        parts_b, gq = res[: len(parts_b)], res[len(parts_b) :]
        low_b = sum_xy(parts_b)
        sums_a = sum_core(gq, nw)
        parts_a = swap_xy(sums_a, nw)
        held = after(low_b, *sums_a)
        own_b = [swap((low_b if e == nz - 1 else held)[e], "fsdp", nz, e) for e in range(1, nz)]
        grad_tokens = input_bwd(geo, me, tokens, dc, dx1, after(vec, *sums_a), bufs_a)
        parts_a = lax.optimization_barrier((*parts_a, grad_tokens))[:-1]
        low_a = sum_xy(parts_a)
        tail = low_a[:, geo.rows_a :].reshape(nz * EXTRA, TL)
        own_a = [swap(jnp.concatenate([low_a[e], tail], 0), "fsdp", nz, e) for e in range(1, nz)]
        grad_qkv, grad_proj, grad_one, grad_two, grad_vectors, grad_bias, grad_table = finish(
            geo, nw, nz, me, low_a, low_b, own_b, own_a
        )
        grad_bias = grad_bias.reshape(-1)
        grad_table = grad_table.T
    else:
        geo = Geometry(1, 1)
        me = jnp.zeros((2,), jnp.int32)

        def full(w):
            return lax.all_gather(lax.all_gather(w, "fsdp", axis=1, tiled=True), "win", axis=0, tiled=True)

        bufs_a = [slabs(full(w_qkv))[None]]
        bufs_b = [jnp.concatenate([slabs(full(w)) for w in (w_proj, w_fc1, w_fc2)], 0).reshape(1, geo.blocks, D, TL)]
        vec = lax.all_gather(vectors, both, axis=1, tiled=True)
        b1 = lax.all_gather(fc1_bias, both, axis=0, tiled=True).reshape(1, -1)
        pb = bias(table, place)
        xh, q, k, v, p, att = attn_fwd(geo, me, tokens, pb, bufs_a, vec)
        out, dx1, da, gv2, gb1, gw = mlp(geo, me, live, tokens, cotangent, att, bufs_b, vec, b1)
        dc, small, gq = attn_bwd(geo, me, q, k, v, p, da, xh, vec, gv2, gb1, place, bufs_a)
        grad_tokens = input_bwd(geo, me, tokens, dc, dx1, vec, bufs_a)

        def down(g):
            g = lax.psum_scatter(g.astype(bf16), "win", scatter_dimension=0, tiled=True)
            return lax.psum_scatter(g, "fsdp", scatter_dimension=1, tiled=True).astype(f32)

        grad_qkv = down(unslab(gq[0], geo.cq))
        grad_proj, grad_one, grad_two = [down(g) for g in split_b(geo, gw[0])]
        small = lax.psum(small, both)
        grad_vectors = lax.dynamic_slice_in_dim(small[:8], dev * own, own, 1)
        grad_bias = lax.dynamic_slice_in_dim(small[8:, TT:].reshape(FF), dev * own1, own1, 0)
        grad_table = small[8:, :TABLE].T
    return out, grad_tokens, grad_vectors, grad_bias, grad_qkv, grad_proj, grad_one, grad_two, grad_table


def solution(mesh):
    split = P(("fsdp", "win"), None, None)
    vecs = P(None, ("fsdp", "win"))
    flat = P(("fsdp", "win"))
    cut = P("win", "fsdp")
    return jax.shard_map(
        functools.partial(body, mesh.shape["win"], mesh.shape["fsdp"]),
        mesh=mesh,
        in_specs=(split, flat, vecs, flat, cut, cut, cut, cut, P(), split),
        out_specs=(split, split, vecs, flat, cut, cut, cut, cut, P()),
        check_vma=False,
    )
```
